768 devices in a mesh: depth: 24 (over x, z_lo), inslab: 32 (over y, z_hi, core).
Axes of the slice: x: 4, y: 8, z: 12 (z_hi: 2, z_lo: 6; z = z_hi * 6 + z_lo), core: 2. Of those that a mesh axis runs over, the one named last changes fastest.
Arguments:
- pressure: float32 [1536, 32, 1024], P(('depth', 'inslab')), may hold values from -6 to 6
- source: float32 [1536, 32, 1024], P(('depth', 'inslab')), may hold values from -4 to 4
- perm: float32 [1536, 32, 1024], P(('depth', 'inslab')), may hold values from 3e-07 to 3
- brinkman: float32 [1536], P(('depth', 'inslab')), may hold values from 0.5 to 4
- depth_source: int32 [1536, 2], P(('depth', 'inslab')), may hold values from -1 to 1, as said below
- sideways_neighbour_table: int32 [1536, 4], P(('depth', 'inslab')), may hold values from -1 to 65, as said below
- edge_blocks: int32 [768, 2, 2], P(('depth', 'inslab')), may hold values from 0 to 1, as said below
- restrict_take: int32 [1536], P(('depth', 'inslab')), may hold values from 0 to 63, as said below
Outputs:
- smoothed: float32 [1536, 32, 1024], P(('depth', 'inslab'))
- coarse_residual: float32 [1536, 16, 256], P(('depth', 'inslab'))
The draws below stay inside these ranges and needn't reach their ends.
Inputs may be any that keep to these rules, and one draw needn't show every extreme that they name: `sideways_neighbour_table`: neighbour links are mutual: if block a names b in a direction, b names a in the opposite one. Devices of one depth index own disjoint strips of blocks of one slab; edge blocks of a peer are its rows facing the neighbour strip; a remote peer q is always the inslab index one below or one above the device's own. `depth_source`: links across depth are mutual and join blocks of the same inslab index on neighbouring depth indices. `edge_blocks`: each row lists distinct slots of the device. `restrict_take`: over the devices of one depth index, every fine block of the slab is named exactly once.
All inputs are finite; a program needn't handle non-finite values.
Results may differ from the reference program's by a relative error of at most 0.0003.
Values sent between devices are 32-bit elements; how exact they have to be, the bound alone decides.
A program may use at most 32 MiB of HBM per device.

```python
import math
import jax
import jax.numpy as jnp
from jax import lax

EDGE = 32
STRIP_ROWS = 1
STRIP_COLS = 2
BLK_DEV = 2
BLOCKS = 1536
N_DEPTH = 24
N_INSLAB = 32
DEVICES = 768


def random_order(key, extent):
    scores = jax.random.randint(key, extent, 0, 1 << 20) * extent[-1] + jnp.arange(extent[-1], dtype=jnp.int32)
    return jnp.argsort(scores, axis=-1).astype(jnp.int32)


def lattice(key):
    flipped = jax.random.randint(jax.random.fold_in(key, 101), (N_DEPTH, 1), 0, 2)
    member = jnp.arange(N_INSLAB, dtype=jnp.int32)[None, :]
    strips = jnp.where(flipped == 1, N_INSLAB - 1 - member, member).astype(jnp.int32)
    holders = strips
    positions = random_order(jax.random.fold_in(key, 102), (N_DEPTH, N_INSLAB, BLK_DEV))
    slot_of = jnp.argsort(positions, axis=-1).astype(jnp.int32)
    return (strips, holders, positions, slot_of)


def draw_source(key, part):
    key = jax.random.fold_in(key, 7)
    extent = (BLOCKS, EDGE, EDGE * EDGE)
    values = jnp.clip(jax.random.normal(key, extent, jnp.float32), -4.0, 4.0)
    return values


def draw_perm(key, part):
    key = jax.random.fold_in(key, 9)
    extent = (BLOCKS, EDGE, EDGE * EDGE)
    pore_cell = jax.random.randint(jax.random.fold_in(key, 1), extent, 0, 10) < 6
    magnitude = jnp.exp(jax.random.uniform(jax.random.fold_in(key, 2), extent, jnp.float32, -1.2039728, 1.0986123))
    return jnp.where(pore_cell, magnitude, 1e-06 * magnitude)


def draw_depth_source(key, part):
    key = jax.random.fold_in(key, 5)
    pairing = random_order(jax.random.fold_in(key, 1), (N_DEPTH - 1, N_INSLAB, BLK_DEV))
    member = jnp.arange(N_INSLAB, dtype=jnp.int32)[None, :, None]
    kept = (jax.random.randint(jax.random.fold_in(key, 2), pairing.shape, 0, 8) != 0) | (member == 0)
    upward = jnp.where(kept, pairing, -1)
    inverse = jnp.argsort(pairing, axis=-1).astype(jnp.int32)
    downward = jnp.where(jnp.take_along_axis(kept, inverse, axis=-1), inverse, -1)
    edge_rows = -jnp.ones((1, N_INSLAB, BLK_DEV), jnp.int32)
    plus_x = jnp.concatenate([upward, edge_rows], axis=0)
    minus_x = jnp.concatenate([edge_rows, downward], axis=0)
    return jnp.stack([minus_x, plus_x], axis=-1).reshape(BLOCKS, 2).astype(jnp.int32)


def draw_sideways_neighbour_table(key, part):
    strips, holders, positions, slot_of = lattice(key)
    row_pos = positions // STRIP_COLS
    col_pos = positions % STRIP_COLS
    strip_full = strips[:, :, None] + jnp.zeros_like(positions)

    def local(offset):
        return jnp.take_along_axis(slot_of, jnp.clip(positions + offset, 0, BLK_DEV - 1), axis=-1)

    def holder(strip_index):
        flat = jnp.clip(strip_index, 0, N_INSLAB - 1).reshape(N_DEPTH, N_INSLAB * BLK_DEV)
        return jnp.take_along_axis(holders, flat, axis=-1).reshape(N_DEPTH, N_INSLAB, BLK_DEV)
    remote_below = BLK_DEV + holder(strip_full - 1) * STRIP_COLS + col_pos
    remote_above = BLK_DEV + holder(strip_full + 1) * STRIP_COLS + col_pos
    minus_y = jnp.where(row_pos > 0, local(-STRIP_COLS), jnp.where(strip_full > 0, remote_below, -1))
    plus_y = jnp.where(row_pos < STRIP_ROWS - 1, local(STRIP_COLS), jnp.where(strip_full < N_INSLAB - 1, remote_above, -1))
    minus_z = jnp.where(col_pos > 0, local(-1), -1)
    plus_z = jnp.where(col_pos < STRIP_COLS - 1, local(1), -1)
    return jnp.stack([minus_y, plus_y, minus_z, plus_z], axis=-1).reshape(BLOCKS, 4).astype(jnp.int32)


def draw_edge_blocks(key, part):
    strips, holders, positions, slot_of = lattice(key)
    low_edge = slot_of[:, :, :STRIP_COLS]
    high_edge = slot_of[:, :, (STRIP_ROWS - 1) * STRIP_COLS:]
    return jnp.stack([low_edge, high_edge], axis=2).reshape(DEVICES, 2, STRIP_COLS).astype(jnp.int32)


def draw_restrict_take(key, part):
    key = jax.random.fold_in(key, 12)
    owned = random_order(key, (N_DEPTH, N_INSLAB * BLK_DEV))
    return owned.reshape(BLOCKS).astype(jnp.int32)


def shard_levels(stream_key, shape, cuts, least, largest):
    loudness, own = 1.0, jax.random.fold_in(stream_key, 6)
    for dim, blocks in cuts:
        steps = jnp.exp(jax.random.uniform(jax.random.fold_in(own, dim), (blocks,), jnp.float32, least / len(cuts), largest / len(cuts)))
        loudness = loudness * jnp.repeat(steps, shape[dim] // blocks).reshape([-1 if axis == dim else 1 for axis in range(len(shape))])
    return loudness


def noise(rng, dims, scale, reach, cuts=(), held_as=jnp.bfloat16):
    loudness = shard_levels(rng, dims, cuts, -0.22, 0.18) if cuts else 1.0
    values = jax.random.normal(rng, dims, jnp.float32) * scale * loudness
    return jnp.minimum(jnp.maximum(values, -reach), reach).astype(held_as)


def setup_inputs(seed: int = 0) -> dict:
    keys = jax.random.split(jax.random.key(seed), 9)
    return {
        "pressure": noise(keys[0], (BLOCKS, EDGE, EDGE * EDGE), 1.0, 6.0, ((0, 768),), jnp.float32),
        "source": draw_source(jax.random.fold_in(keys[8], 71), 0),
        "perm": draw_perm(jax.random.fold_in(keys[8], 71), 0),
        "brinkman": jnp.clip(jnp.exp(math.log(4.0) - 2.0794415 * jax.random.uniform(keys[3], (BLOCKS,), jnp.float32) ** shard_levels(keys[3], (BLOCKS,), ((0, 768),), -0.2, 0.2)), 0.5, 4.0),
        "depth_source": draw_depth_source(jax.random.fold_in(keys[8], 71), 0),
        "sideways_neighbour_table": draw_sideways_neighbour_table(jax.random.fold_in(keys[8], 71), 0),
        "edge_blocks": draw_edge_blocks(jax.random.fold_in(keys[8], 71), 0),
        "restrict_take": draw_restrict_take(jax.random.fold_in(keys[8], 71), 0),
    }


OMEGA = 0.8
OPPOSITE = (1, 0, 3, 2, 5, 4)


def block_faces(field):
    number, edge_len, plane_len = field.shape
    return [field[:, 0, :], field[:, -1, :],
            field[:, :, :edge_len].reshape(number, plane_len),
            field[:, :, plane_len - edge_len:].reshape(number, plane_len),
            field[:, :, 0::edge_len].reshape(number, plane_len),
            field[:, :, edge_len - 1::edge_len].reshape(number, plane_len)]


def beside(field, ghosts):
    number, edge_len, plane_len = field.shape
    z_position = lax.broadcasted_iota(jnp.int32, (1, 1, plane_len), 2) % edge_len
    zero_cells = jnp.zeros((number, edge_len, 1), field.dtype)
    minus_x = jnp.concatenate([ghosts[0][:, None, :], field[:, :-1, :]], axis=1)
    plus_x = jnp.concatenate([field[:, 1:, :], ghosts[1][:, None, :]], axis=1)
    minus_y = jnp.concatenate([ghosts[2].reshape(number, edge_len, edge_len), field[:, :, :plane_len - edge_len]], axis=2)
    plus_y = jnp.concatenate([field[:, :, edge_len:], ghosts[3].reshape(number, edge_len, edge_len)], axis=2)
    minus_z = jnp.where(z_position == 0, jnp.repeat(ghosts[4].reshape(number, edge_len, edge_len), edge_len, axis=2),
                        jnp.concatenate([zero_cells, field[:, :, :-1]], axis=2))
    plus_z = jnp.where(z_position == edge_len - 1, jnp.repeat(ghosts[5].reshape(number, edge_len, edge_len), edge_len, axis=2),
                       jnp.concatenate([field[:, :, 1:], zero_cells], axis=2))
    return [minus_x, plus_x, minus_y, plus_y, minus_z, plus_z]


def coefficients(perm, kghosts, brinkman):
    face_weights = [2.0 * perm * neighbour / (perm + neighbour) for neighbour in beside(perm, kghosts)]
    diagonal = brinkman[:, None, None] + face_weights[0] + face_weights[1] + face_weights[2] + face_weights[3] + face_weights[4] + face_weights[5]
    return face_weights, diagonal


def operate(field, ghosts, face_weights, diagonal):
    neighbours = beside(field, ghosts)
    flux = face_weights[0] * neighbours[0]
    for direction in range(1, 6):
        flux = flux + face_weights[direction] * neighbours[direction]
    return diagonal * field - flux


def restrict(residual):
    number, edge_len, plane_len = residual.shape
    half_len = edge_len // 2
    paired = residual[:, 0::2, :] + residual[:, 1::2, :]
    row_index = lax.broadcasted_iota(jnp.int32, (plane_len, half_len * half_len), 0)
    column = lax.broadcasted_iota(jnp.int32, (plane_len, half_len * half_len), 1)
    target = (row_index // edge_len // 2) * half_len + (row_index % edge_len) // 2
    pooling = (target == column).astype(jnp.float32)
    return 0.125 * jnp.einsum("bxp,pq->bxq", paired, pooling, precision=lax.Precision.HIGHEST)


def neighbour_ids(depth_source, sideways_neighbour_table, edge_blocks):
    device = jnp.arange(BLOCKS, dtype=jnp.int32) // BLK_DEV
    slab = device // N_INSLAB
    member = device % N_INSLAB
    below = jnp.where(depth_source[:, 0] >= 0, ((slab - 1) * N_INSLAB + member) * BLK_DEV + depth_source[:, 0], -1)
    above = jnp.where(depth_source[:, 1] >= 0, ((slab + 1) * N_INSLAB + member) * BLK_DEV + depth_source[:, 1], -1)

    def lateral(neighbour_value, edge_side):
        remote = jnp.maximum(neighbour_value - BLK_DEV, 0)
        peer_device = slab * N_INSLAB + remote // STRIP_COLS
        foreign_block_slot = edge_blocks[peer_device, edge_side, remote % STRIP_COLS]
        return jnp.where(neighbour_value < 0, -1, jnp.where(neighbour_value < BLK_DEV, device * BLK_DEV + neighbour_value, peer_device * BLK_DEV + foreign_block_slot))

    minus_y = lateral(sideways_neighbour_table[:, 0], 1)
    plus_y = lateral(sideways_neighbour_table[:, 1], 0)
    minus_z = jnp.where(sideways_neighbour_table[:, 2] >= 0, device * BLK_DEV + sideways_neighbour_table[:, 2], -1)
    plus_z = jnp.where(sideways_neighbour_table[:, 3] >= 0, device * BLK_DEV + sideways_neighbour_table[:, 3], -1)
    return [below, above, minus_y, plus_y, minus_z, plus_z]


def gather_ghosts(field, identities):
    all_faces = block_faces(field)
    ghost_list = []
    for direction in range(6):
        requested_blocks = identities[direction]
        rows = jnp.take(all_faces[OPPOSITE[direction]], jnp.maximum(requested_blocks, 0), axis=0)
        ghost_list.append(jnp.where((requested_blocks >= 0)[:, None], rows, 0.0))
    return jnp.stack(ghost_list, axis=1)


def grouped(array):
    return array.reshape((DEVICES, BLK_DEV) + array.shape[1:])


def reference(pressure, source, perm, brinkman, depth_source, sideways_neighbour_table, edge_blocks, restrict_take):
    identities = neighbour_ids(depth_source, sideways_neighbour_table, edge_blocks)
    kghosts = grouped(gather_ghosts(perm, identities))

    def relax(items):
        pressure_now, perm_now, source_now, drag_now, pghost, kghost = items
        face_weights, diagonal = coefficients(perm_now, [kghost[:, i] for i in range(6)], drag_now)
        applied = operate(pressure_now, [pghost[:, i] for i in range(6)], face_weights, diagonal)
        return pressure_now + OMEGA * (source_now - applied) / diagonal

    def residual_pieces(items):
        pressure_now, perm_now, source_now, drag_now, pghost, kghost = items
        face_weights, diagonal = coefficients(perm_now, [kghost[:, i] for i in range(6)], drag_now)
        applied = operate(pressure_now, [pghost[:, i] for i in range(6)], face_weights, diagonal)
        return restrict(source_now - applied)

    pressure_now = pressure
    for iteration in range(2):
        peer_ghost_blocks = grouped(gather_ghosts(pressure_now, identities))
        pressure_now = lax.map(relax, (grouped(pressure_now), grouped(perm), grouped(source), grouped(brinkman), peer_ghost_blocks, kghosts)).reshape(pressure.shape)
    peer_ghost_blocks = grouped(gather_ghosts(pressure_now, identities))
    pieces = lax.map(residual_pieces, (grouped(pressure_now), grouped(perm), grouped(source), grouped(brinkman), peer_ghost_blocks, kghosts))
    taking = restrict_take.reshape(DEVICES, BLK_DEV)
    receiver = jnp.arange(DEVICES, dtype=jnp.int32)[:, None]
    sender = (receiver // N_INSLAB) * N_INSLAB + taking // BLK_DEV
    slot_index = taking % BLK_DEV
    coarse = pieces[sender, slot_index]
    return pressure_now, coarse.reshape((BLOCKS,) + pieces.shape[2:])
```

```python
import jax
import jax.numpy as jnp
from jax import lax
from jax.experimental import pallas as pl
from jax.experimental.pallas import tpu as pltpu
from jax.sharding import PartitionSpec as P

OMEGA = 0.8
MESH = pl.DeviceIdType.MESH
F32 = jnp.float32
CHUNKS, SUB, LANES = 4, 8, 1024


def kernel(
    p_hbm, s_hbm, k_hbm, brink, ds, snt, eb, take,
    out_hbm, coarse_hbm,
    u0, src, perm, u1, u2, g, dg, inv, wxm, wxp, wym, wyp, wzm, wzp,
    wxlo, wxhi, wylo, wyhi, res, pool,
    xs1, xs2, xs3, xr1, xr2, xr3, ys1, ys2, ys3, yr1, yr2, yr3,
    wants, gathered, sib_out, sib_in, zp_out, zp_in, coarse,
    in_sem, out_sem, hs_sem, hr_sem, ws_sem, wr_sem, gs_sem, gr_sem, es_sem, er_sem,
):
    depth = lax.axis_index("depth")
    me = lax.axis_index("inslab")
    n_depth = lax.axis_size("depth")
    n_in = lax.axis_size("inslab")
    n_y = n_in // 4
    my_y = me // 4
    zh = (me // 2) % 2
    core = me % 2

    def at(y, z, c):
        return (depth, (y * 2 + z) * 2 + c)

    d_low = (lax.rem(depth + n_depth - 1, n_depth), me)
    d_high = (lax.rem(depth + 1, n_depth), me)
    i_low = (depth, lax.rem(me + n_in - 1, n_in))
    i_high = (depth, lax.rem(me + 1, n_in))
    sib = at(my_y, zh, 1 - core)
    zpar = at(my_y, 1 - zh, core)
    zdia = at(my_y, 1 - zh, 1 - core)
    y_peers = [at(lax.rem(my_y + o, n_y), zh, core) for o in range(1, n_y)]

    loads = [
        pltpu.make_async_copy(h, v, in_sem.at[i])
        for i, (h, v) in enumerate([(k_hbm, perm), (p_hbm, u0), (s_hbm, src)])
    ]
    for load in loads:
        load.start()

    barrier = pltpu.get_barrier_semaphore()
    partners = [d_low, d_high, i_low, i_high, sib, zpar, zdia] + y_peers
    for partner in partners:
        pl.semaphore_signal(barrier, inc=1, device_id=partner, device_id_type=MESH)

    lane128 = lax.broadcasted_iota(jnp.int32, (CHUNKS, SUB, 128), 2)
    row = lax.broadcasted_iota(jnp.int32, (SUB, LANES), 0)
    lane = lax.broadcasted_iota(jnp.int32, (SUB, LANES), 1)
    zpos = lane % 32

    def remote(a, b, s, r, device):
        copy = pltpu.make_async_remote_copy(
            src_ref=a, dst_ref=b, send_sem=s, recv_sem=r, device_id=device, device_id_type=MESH
        )
        copy.start()
        return copy

    wrow = lax.broadcasted_iota(jnp.int32, (SUB, 128), 0)
    wants[0] = jnp.where(wrow < 4, take[0], take[1])

    def faces_minus(limit_low):
        found = False
        for a in range(2):
            w = snt[a, 0]
            remote_w = w >= 2
            low = w - 2 < 2 * me
            hit = remote_w & (low if limit_low else jnp.logical_not(low))
            found = hit if a == 0 else found | hit
        return found

    low_is_minus = faces_minus(True)
    high_is_minus = faces_minus(False)

    def y_faces(field):
        low = [field[a, :, :, 0:128] for a in range(2)]
        high = [pltpu.roll(field[a, :, :, LANES - 128 : LANES], 32, 2) for a in range(2)]
        return low, high

    def pair_for(faces, minus):
        low, high = faces
        cols = []
        for c in range(2):
            from_low = jnp.where(eb[0, 0, c] == 1, low[1], low[0])
            from_high = jnp.where(eb[0, 1, c] == 1, high[1], high[0])
            cols.append(jnp.where(minus, from_low, from_high))
        return jnp.where(lane128 < 32, cols[0], pltpu.roll(cols[1], 32, 2))

    def fold(pair):
        half = CHUNKS // 2
        return jnp.where(
            lane128[:half] < 64, pair[:half], pltpu.roll(pair[half:], 64, 2)
        )

    def unfold(packed):
        return jnp.concatenate([packed, pltpu.roll(packed, 64, 2)], axis=0)

    def x_faces(field, low):
        if low:
            return [field[a, 0, 0:1, :] for a in range(2)]
        return [field[a, CHUNKS - 1, SUB - 1 : SUB, :] for a in range(2)]

    def send_round(number, xs, ys, xr, yr):
        base = 4 * number
        return [
            remote(ys.at[0], yr.at[1], hs_sem.at[base], hr_sem.at[base], i_low),
            remote(ys.at[1], yr.at[0], hs_sem.at[base + 1], hr_sem.at[base + 1], i_high),
            remote(xs.at[0], xr.at[1], hs_sem.at[base + 2], hr_sem.at[base + 2], d_low),
            remote(xs.at[1], xr.at[0], hs_sem.at[base + 3], hr_sem.at[base + 3], d_high),
        ]

    def fill_x(xs, first, field):
        for side in range(2):
            for a, face in enumerate(x_faces(field, side == 0)):
                xs[side, first + a : first + a + 1, :] = face

    loads[0].wait()
    loads[1].wait()
    fill_x(xs1, 0, u0)
    fill_x(xs1, 2, perm)
    for side, minus in enumerate((low_is_minus, high_is_minus)):
        pp = pair_for(y_faces(u0), minus)
        kk = pair_for(y_faces(perm), minus)
        ys1[side] = jnp.where(lane128 < 64, pp, pltpu.roll(kk, 64, 2))
    pl.semaphore_wait(barrier, len(partners))
    sent = send_round(0, xs1, ys1, xr1, yr1)
    want_copies = [
        remote(wants.at[0], wants.at[1 + j], ws_sem.at[j], wr_sem.at[j], device)
        for j, device in enumerate((sib, zpar, zdia))
    ]

    def zslot(a, direction):
        return jnp.maximum(snt[a, 2 + direction], 0)

    def beside(field, a, k):
        u = field[a, k]
        before = field[a, jnp.maximum(k - 1, 0), SUB - 1 : SUB, :]
        after = field[a, jnp.minimum(k + 1, CHUNKS - 1), 0:1, :]
        um = jnp.where(row == 0, before, pltpu.roll(u, 1, 0))
        up = jnp.where(row == SUB - 1, after, pltpu.roll(u, SUB - 1, 0))
        ym = pltpu.roll(u, 32, 1)
        yp = pltpu.roll(u, LANES - 32, 1)
        nm = field[zslot(a, 0), k]
        np_ = field[zslot(a, 1), k]
        zm = jnp.where(zpos == 0, pltpu.roll(nm, LANES - 31, 1), pltpu.roll(u, 1, 1))
        zp = jnp.where(zpos == 31, pltpu.roll(np_, 31, 1), pltpu.roll(u, LANES - 1, 1))
        return u, (um, up, ym, yp, zm, zp)

    def weights(k, _):
        for a in range(2):
            kk, nbs = beside(perm, a, k)
            has_zm = snt[a, 2] >= 0
            has_zp = snt[a, 3] >= 0
            keep = (
                jnp.logical_not((row == 0) & (k == 0)),
                jnp.logical_not((row == SUB - 1) & (k == CHUNKS - 1)),
                lane >= 32,
                lane < LANES - 32,
                jnp.logical_or(zpos != 0, has_zm),
                jnp.logical_or(zpos != 31, has_zp),
            )
            total = jnp.full((SUB, LANES), brink[a], F32)
            for store, nb, mask in zip((wxm, wxp, wym, wyp, wzm, wzp), nbs, keep):
                w = jnp.where(mask, 2.0 * kk * nb / (kk + nb), 0.0)
                store[a, k] = w
                total = total + w
            dg[a, k] = total
        return 0

    lax.fori_loop(0, CHUNKS, weights, 0)
    loads[2].wait()

    def neighbour_sum(field):
        def step(k, _):
            for a in range(2):
                _, nbs = beside(field, a, k)
                total = src[a, k]
                for store, nb in zip((wxm, wxp, wym, wyp, wzm, wzp), nbs):
                    total = total + store[a, k] * nb
                g[a, k] = total
            return 0

        lax.fori_loop(0, CHUNKS, step, 0)

    neighbour_sum(u0)

    prow = lax.broadcasted_iota(jnp.int32, (512, 128), 0)
    pcol = lax.broadcasted_iota(jnp.int32, (512, 128), 1)
    pool[...] = ((prow // 64) * 16 + (prow % 32) // 2 == pcol).astype(F32)

    def x_ghost(message, a, direction, first):
        slot = ds[a, direction]
        zero = jnp.zeros((1, LANES), F32)
        return jnp.where(
            slot == 0,
            message[first : first + 1, :],
            jnp.where(slot == 1, message[first + 1 : first + 2, :], zero),
        )

    def y_ghost(faces, pairs, a, direction):
        w = snt[a, direction]
        c1 = w % 2 == 1
        from_low = w - 2 < 2 * me
        low_pair, high_pair = pairs
        pair = jnp.where(from_low, low_pair, high_pair)
        far = jnp.where(c1, pltpu.roll(pair, 96, 2), pair)
        near = jnp.where(w == 1, faces[1], faces[0])
        found = jnp.where(w >= 2, far, near)
        return jnp.where((lane128 < 32) & (w >= 0), found, 0.0)

    def harmonic(a, b):
        return 2.0 * a * b / (a + b)

    for copy in sent:
        copy.wait_recv()

    k_low, k_high = y_faces(perm)
    u_low, u_high = y_faces(u0)
    k_pairs = [pltpu.roll(yr1[i], 64, 2) for i in range(2)]
    u_pairs = [yr1[i] for i in range(2)]
    for a in range(2):
        for direction, chunk, r, keep in ((0, 0, 0, wxlo), (1, CHUNKS - 1, SUB - 1, wxhi)):
            kg = x_ghost(xr1[direction], a, direction, 2)
            ug = x_ghost(xr1[direction], a, direction, 0)
            w = harmonic(perm[a, chunk, r : r + 1, :], kg)
            keep[a : a + 1, :] = w
            dg[a, chunk, r : r + 1, :] += w
            g[a, chunk, r : r + 1, :] += w * ug
        kg = y_ghost(k_high, k_pairs, a, 0)
        ug = y_ghost(u_high, u_pairs, a, 0)
        w = jnp.where(lane128 < 32, harmonic(k_low[a], kg), 0.0)
        wylo[a] = w
        dg[a, :, :, 0:128] += w
        g[a, :, :, 0:128] += w * ug
        kg = y_ghost(k_low, k_pairs, a, 1)
        ug = y_ghost(u_low, u_pairs, a, 1)
        w = jnp.where(lane128 < 32, harmonic(k_high[a], kg), 0.0)
        wyhi[a] = w
        dg[a, :, :, LANES - 128 : LANES] += pltpu.roll(w, 96, 2)
        g[a, :, :, LANES - 128 : LANES] += pltpu.roll(w * ug, 96, 2)

    def first_update(k, _):
        for a in range(2):
            i = OMEGA / dg[a, k]
            inv[a, k] = i
            u1[a, k] = (1.0 - OMEGA) * u0[a, k] + i * g[a, k]
        return 0

    lax.fori_loop(0, CHUNKS, first_update, 0)

    def exchange(number, field, xs, ys, xr, yr):
        fill_x(xs, 0, field)
        faces = y_faces(field)
        for side, minus in enumerate((low_is_minus, high_is_minus)):
            ys[side] = fold(pair_for(faces, minus))
        return send_round(number, xs, ys, xr, yr)

    def correct(field, copies, xr, yr):
        for copy in copies:
            copy.wait_recv()
        low, high = y_faces(field)
        pairs = [unfold(yr[i]) for i in range(2)]
        for a in range(2):
            g[a, 0, 0:1, :] += wxlo[a : a + 1, :] * x_ghost(xr[0], a, 0, 0)
            g[a, CHUNKS - 1, SUB - 1 : SUB, :] += wxhi[a : a + 1, :] * x_ghost(xr[1], a, 1, 0)
            g[a, :, :, 0:128] += wylo[a] * y_ghost(high, pairs, a, 0)
            g[a, :, :, LANES - 128 : LANES] += pltpu.roll(
                wyhi[a] * y_ghost(low, pairs, a, 1), 96, 2
            )

    sent2 = exchange(1, u1, xs2, ys2, xr2, yr2)
    neighbour_sum(u1)
    correct(u1, sent2, xr2, yr2)

    def second_update(k, _):
        for a in range(2):
            u2[a, k] = (1.0 - OMEGA) * u1[a, k] + inv[a, k] * g[a, k]
        return 0

    lax.fori_loop(0, CHUNKS, second_update, 0)
    sent3 = exchange(2, u2, xs3, ys3, xr3, yr3)
    store = pltpu.make_async_copy(u2, out_hbm, out_sem.at[0])
    store.start()
    neighbour_sum(u2)
    correct(u2, sent3, xr3, yr3)

    def residual(k, _):
        for a in range(2):
            at_row = pl.multiple_of(a * 32 + k * SUB, SUB)
            r = g[a, k] - dg[a, k] * u2[a, k]
            for t in range(8):
                res[t, pl.ds(at_row, SUB), :] = r[:, 128 * t : 128 * t + 128]
        return 0

    lax.fori_loop(0, CHUNKS, residual, 0)
    paired = [
        0.125 * (res[t, pl.ds(0, 32, stride=2), :] + res[t, pl.ds(1, 32, stride=2), :])
        for t in range(8)
    ]
    stacked = jnp.concatenate(
        [jnp.concatenate(paired[4 * h : 4 * h + 4], axis=1) for h in range(2)], axis=0
    )
    pooled = jnp.dot(
        stacked, pool[...], preferred_element_type=F32, precision=lax.Precision.HIGHEST
    )
    for a in range(2):
        for t in range(2):
            gathered[my_y, a, :, 128 * t : 128 * t + 128] = pooled[
                32 * t + 16 * a : 32 * t + 16 * a + 16, :
            ]

    spread = [
        remote(
            gathered.at[my_y], gathered.at[my_y], gs_sem.at[o], gr_sem.at[o], device
        )
        for o, device in enumerate(y_peers)
    ]
    for copy in want_copies:
        copy.wait_recv()
    for copy in spread:
        copy.wait_recv()

    shape = (n_y, 2, 16, 256)
    piece_id = (
        (lax.broadcasted_iota(jnp.int32, shape, 0) * 4 + zh * 2 + core) * 2
        + lax.broadcasted_iota(jnp.int32, shape, 1)
    )

    def own(holder, j):
        w = wants[holder, 4 * j : 4 * j + 1, :]
        w = jnp.concatenate([w, w], axis=1).reshape(1, 1, 1, 256)
        return jnp.sum(jnp.where(piece_id == w, gathered[...], 0.0), axis=(0, 1))

    for slot, holder in enumerate((1, 3)):
        for j in range(2):
            sib_out[2 * slot + j] = own(holder, j)
    to_sib = remote(sib_out, sib_in, es_sem.at[0], er_sem.at[0], sib)
    for j in range(2):
        zp_out[j] = own(2, j)
        coarse[j] = own(0, j)
    to_sib.wait_recv()
    for j in range(2):
        zp_out[j] += sib_in[2 + j]
    to_zpar = remote(zp_out, zp_in, es_sem.at[1], er_sem.at[1], zpar)
    for j in range(2):
        coarse[j] += sib_in[j]
    to_zpar.wait_recv()
    for j in range(2):
        coarse[j] += zp_in[j]
    last = pltpu.make_async_copy(coarse, coarse_hbm, out_sem.at[1])
    last.start()
    for copy in sent + want_copies + sent2 + sent3 + spread + [to_sib, to_zpar]:
        copy.wait_send()
    store.wait()
    last.wait()


def body(pressure, source, perm, brinkman, depth_source, sideways, edge_blocks, restrict_take):
    big = (2, CHUNKS, SUB, LANES)
    n_y = lax.axis_size("inslab") // 4
    vm = lambda *shape: pltpu.VMEM(shape, F32)
    dma = lambda n: pltpu.SemaphoreType.DMA((n,))
    anywhere = pl.BlockSpec(memory_space=pltpu.HBM)
    scalars = pl.BlockSpec(memory_space=pltpu.SMEM)
    smoothed, coarse = pl.pallas_call(
        kernel,
        out_shape=(
            jax.ShapeDtypeStruct(big, F32),
            jax.ShapeDtypeStruct((2, 16, 256), F32),
        ),
        in_specs=[anywhere] * 3 + [scalars] * 5,
        out_specs=(anywhere, anywhere),
        scratch_shapes=[vm(*big) for _ in range(14)]
        + [
            vm(2, LANES), vm(2, LANES),
            vm(2, CHUNKS, SUB, 128), vm(2, CHUNKS, SUB, 128),
            vm(8, 64, 128), vm(512, 128),
            vm(2, 4, LANES), vm(2, 2, LANES), vm(2, 2, LANES),
            vm(2, 4, LANES), vm(2, 2, LANES), vm(2, 2, LANES),
            vm(2, 4, SUB, 128), vm(2, 2, SUB, 128), vm(2, 2, SUB, 128),
            vm(2, 4, SUB, 128), vm(2, 2, SUB, 128), vm(2, 2, SUB, 128),
            pltpu.VMEM((4, SUB, 128), jnp.int32),
            vm(n_y, 2, 16, 256),
            vm(4, 16, 256), vm(4, 16, 256), vm(2, 16, 256), vm(2, 16, 256), vm(2, 16, 256),
            dma(3), dma(2), dma(12), dma(12), dma(3), dma(3), dma(n_y - 1), dma(n_y - 1),
            dma(2), dma(2),
        ],
        compiler_params=pltpu.CompilerParams(
            collective_id=0, has_side_effects=True, vmem_limit_bytes=62 * 1024 * 1024
        ),
    )(
        pressure.reshape(big), source.reshape(big), perm.reshape(big), brinkman,
        depth_source, sideways, edge_blocks, restrict_take,
    )
    return smoothed.reshape(pressure.shape), coarse


def solution(mesh):
    group = ("depth", "inslab")
    return jax.shard_map(
        body,
        mesh=mesh,
        in_specs=(
            P(group, None, None),
            P(group, None, None),
            P(group, None, None),
            P(group),
            P(group, None),
            P(group, None),
            P(group, None, None),
            P(group),
        ),
        out_specs=(P(group, None, None), P(group, None, None)),
        check_vma=False,
    )
```

```python
import jax
import jax.numpy as jnp
from jax import lax
from jax.experimental import pallas as pl
from jax.experimental.pallas import tpu as pltpu
from jax.sharding import PartitionSpec as P

OMEGA = 0.8
MESH = pl.DeviceIdType.MESH
F32 = jnp.float32
I32 = jnp.int32
CHUNKS, SUB, LANES = 4, 8, 1024
LAST = LANES - 128


def harmonic(a, b):
    return 2.0 * a * b / (a + b)


def kernel(
    p_hbm, s_hbm, k_hbm, brink_hbm, ds_hbm, snt_hbm, eb_hbm, take_hbm,
    out_hbm, coarse_hbm,
    brink, ds, snt, eb, take,
    u0, src, perm, u1, u2, g, dg, inv, wxm, wxp, wym, wyp, wzm, wzp,
    wxe, wye, res, pool, pool_face,
    xs, xr, ys, yr, edge_out, edge_in,
    tables, face_sum, gathered, x_out, x_in, sib_out, sib_in, zp_out, zp_in, coarse,
    in_sem, out_sem, hs_sem, hr_sem, ts_sem, tr_sem, gs_sem, gr_sem, xs_sem, xr_sem, es_sem, er_sem,
):
    depth = lax.axis_index("depth")
    me = lax.axis_index("inslab")
    n_depth = lax.axis_size("depth")
    n_in = lax.axis_size("inslab")
    n_y = n_in // 4
    my_y = me // 4
    zh = (me // 2) % 2
    core = me % 2

    def at(d, y, z, c):
        return (d, (y * 2 + z) * 2 + c)

    deeper = [lax.rem(depth + n_depth - 1, n_depth), lax.rem(depth + 1, n_depth)]
    beside_me = [lax.rem(me + n_in - 1, n_in), lax.rem(me + 1, n_in)]
    row_peers = [
        at(depth, my_y, zh, 1 - core), at(depth, my_y, 1 - zh, core), at(depth, my_y, 1 - zh, 1 - core)
    ]
    y_peers = [at(depth, lax.rem(my_y + o, n_y), zh, core) for o in range(1, n_y)]
    x_peers = [
        [at(deeper[side], lax.rem(my_y + o, n_y), zh, core) for o in range(n_y)] for side in range(2)
    ]
    i_peers = [(depth, m) for m in beside_me]
    d_peers = [(d, me) for d in deeper]
    corners = [[(d, m) for m in beside_me] for d in deeper]

    has = [depth > 0, depth < n_depth - 1]

    barrier = pltpu.get_barrier_semaphore()

    def greet(partner):
        pl.semaphore_signal(barrier, inc=1, device_id=partner, device_id_type=MESH)

    always = i_peers + row_peers + y_peers
    for partner in always:
        greet(partner)
    for side in range(2):
        pl.when(has[side])(lambda side=side: [greet(p) for p in [d_peers[side]] + corners[side]] and None)
    greeted = len(always) + sum(jnp.where(has[side], 1 + len(corners[side]), 0) for side in range(2))

    small = [(snt_hbm, snt), (ds_hbm, ds), (eb_hbm, eb), (take_hbm, take), (brink_hbm, brink)]
    loads = [
        pltpu.make_async_copy(h, v, in_sem.at[i])
        for i, (h, v) in enumerate([(k_hbm, perm), (p_hbm, u0), (s_hbm, src)] + small)
    ]
    for load in loads:
        load.start()
    for load in loads[3:]:
        load.wait()

    lane3 = lax.broadcasted_iota(I32, (CHUNKS, SUB, 128), 2)
    lane1 = lax.broadcasted_iota(I32, (1, 128), 1)
    row = lax.broadcasted_iota(I32, (SUB, LANES), 0)
    lane = lax.broadcasted_iota(I32, (SUB, LANES), 1)
    zpos = lane % 32
    quarter3 = lane3 // 32
    quarter1 = lane1 // 32

    def remote(a, b, s, r, device):
        copy = pltpu.make_async_remote_copy(
            src_ref=a, dst_ref=b, send_sem=s, recv_sem=r, device_id=device, device_id_type=MESH
        )
        copy.start()
        return copy

    class Link:
        def __init__(self, a, b, s, r, device, side):
            self.args, self.side = (a, b, s, r, device), side
            pl.when(has[side])(lambda: self.make().start())

        def make(self):
            a, b, s, r, device = self.args
            return pltpu.make_async_remote_copy(
                src_ref=a, dst_ref=b, send_sem=s, recv_sem=r, device_id=device, device_id_type=MESH
            )

        def wait_recv(self):
            pl.when(has[1 - self.side])(lambda: self.make().wait_recv())

        def wait_send(self):
            pl.when(has[self.side])(lambda: self.make().wait_send())

    def lies_minus(low):
        found = []
        for a in range(2):
            w = snt[a, 0]
            below = w - 2 < 2 * me
            found.append((w >= 2) & (below if low else jnp.logical_not(below)))
        return found[0] | found[1]

    minus = [lies_minus(True), lies_minus(False)]

    def quarter_of(a, direction):
        w = snt[a, direction]
        column = w & 1
        q = jnp.where(w - 2 < 2 * me, column, 2 + column)
        return jnp.where(w >= 2, q, -1)

    codes = [[quarter_of(a, direction) for direction in range(2)] for a in range(2)]

    trow = lax.broadcasted_iota(I32, (SUB, 128), 0)

    def as_rows(entries):
        tile = jnp.zeros((SUB, 128), I32)
        for i, value in enumerate(entries):
            tile = jnp.where(trow == i, value, tile)
        return tile

    tables[0] = as_rows([take[0], take[1]] + [codes[a][s] for a in range(2) for s in range(2)])
    links = as_rows(
        [ds[a, s] for a in range(2) for s in range(2)]
        + [eb[0, s, c] for s in range(2) for c in range(2)]
    ).astype(F32)

    def y_faces(field):
        low = [field[a, :, :, 0:128] for a in range(2)]
        high = [pltpu.roll(field[a, :, :, LAST:LANES], 32, 2) for a in range(2)]
        return low, high

    def pair_for(faces, is_minus):
        low, high = faces
        cols = []
        for c in range(2):
            from_low = jnp.where(eb[0, 0, c] == 1, low[1], low[0])
            from_high = jnp.where(eb[0, 1, c] == 1, high[1], high[0])
            cols.append(jnp.where(is_minus, from_low, from_high))
        return jnp.where(lane3 < 32, cols[0], pltpu.roll(cols[1], 32, 2))

    def x_face(field, side, a):
        if side == 0:
            return field[a, 0, 0:1, :]
        return field[a, CHUNKS - 1, SUB - 1 : SUB, :]

    def fill(first, second, block):
        for side in range(2):
            for a in range(2):
                n = 4 * block + a
                xs[side, n : n + 1, :] = x_face(first, side, a)
                xs[side, n + 2 : n + 3, :] = x_face(second, side, a)
        one, two = y_faces(first), y_faces(second)
        for peer in range(2):
            ys[peer, CHUNKS * block : CHUNKS * block + CHUNKS] = jnp.where(
                lane3 < 64, pair_for(one, minus[peer]), pltpu.roll(pair_for(two, minus[peer]), 64, 2)
            )

    loads[0].wait()
    loads[1].wait()
    fill(u0, perm, 0)
    for peer in range(2):
        ys[peer, 2 * CHUNKS] = links
    for side in range(2):
        for f, field in enumerate((u0, perm)):
            lines = []
            for a in range(2):
                face = x_face(field, side, a)
                lines.append([face[:, 0:128], pltpu.roll(face[:, LAST:LANES], 32, 1)])
            by_column = [
                jnp.where(eb[0, s, c] == 1, lines[1][s], lines[0][s]) for s in range(2) for c in range(2)
            ]
            by_slot = [lines[a][s] for a in range(2) for s in range(2)]
            for n, listed in enumerate((by_column, by_slot)):
                packed = listed[0]
                for q in range(1, 4):
                    packed = jnp.where(quarter1 == q, pltpu.roll(listed[q], 32 * q, 1), packed)
                edge_out[side, 2 * n + f : 2 * n + f + 1, :] = packed
    def zslot(a, direction):
        return jnp.maximum(snt[a, 2 + direction], 0)

    def beside(field, a, k):
        u = field[a, k]
        before = field[a, jnp.maximum(k - 1, 0), SUB - 1 : SUB, :]
        after = field[a, jnp.minimum(k + 1, CHUNKS - 1), 0:1, :]
        um = jnp.where(row == 0, before, pltpu.roll(u, 1, 0))
        up = jnp.where(row == SUB - 1, after, pltpu.roll(u, SUB - 1, 0))
        ym = pltpu.roll(u, 32, 1)
        yp = pltpu.roll(u, LANES - 32, 1)
        nm = field[zslot(a, 0), k]
        np_ = field[zslot(a, 1), k]
        zm = jnp.where(zpos == 0, pltpu.roll(nm, LANES - 31, 1), pltpu.roll(u, 1, 1))
        zp = jnp.where(zpos == 31, pltpu.roll(np_, 31, 1), pltpu.roll(u, LANES - 1, 1))
        return u, (um, up, ym, yp, zm, zp)

    def weights(k, _):
        for a in range(2):
            kk, nbs = beside(perm, a, k)
            has_zm = snt[a, 2] >= 0
            has_zp = snt[a, 3] >= 0
            keep = (
                jnp.logical_not((row == 0) & (k == 0)),
                jnp.logical_not((row == SUB - 1) & (k == CHUNKS - 1)),
                lane >= 32,
                lane < LANES - 32,
                jnp.logical_or(zpos != 0, has_zm),
                jnp.logical_or(zpos != 31, has_zp),
            )
            total = jnp.full((SUB, LANES), brink[a], F32)
            for store, nb, mask in zip((wxm, wxp, wym, wyp, wzm, wzp), nbs, keep):
                w = jnp.where(mask, harmonic(kk, nb), 0.0)
                store[a, k] = w
                total = total + w
            dg[a, k] = total
        return 0

    lax.fori_loop(0, CHUNKS, weights, 0)
    loads[2].wait()

    def neighbour_sum(field):
        def step(k, _):
            for a in range(2):
                _, nbs = beside(field, a, k)
                total = src[a, k]
                for store, nb in zip((wxm, wxp, wym, wyp, wzm, wzp), nbs):
                    total = total + store[a, k] * nb
                g[a, k] = total
            return 0

        lax.fori_loop(0, CHUNKS, step, 0)

    neighbour_sum(u0)
    fill(g, dg, 1)

    pl.semaphore_wait(barrier, greeted)
    sent = []
    for peer in range(2):
        sent.append(remote(ys.at[peer], yr.at[1 - peer], hs_sem.at[peer], hr_sem.at[peer], i_peers[peer]))
    for side in range(2):
        for peer in range(2):
            n = 4 + 2 * side + peer
            sent.append(
                Link(
                    edge_out.at[side], edge_in.at[1 - side, 1 - peer],
                    hs_sem.at[n], hr_sem.at[n], corners[side][peer], side,
                )
            )
    for side in range(2):
        n = 2 + side
        sent.append(
            Link(xs.at[side], xr.at[1 - side], hs_sem.at[n], hr_sem.at[n], d_peers[side], side)
        )
        sent.append(
            Link(
                tables.at[0], tables.at[2 - side], ts_sem.at[side], tr_sem.at[side], d_peers[side], side
            )
        )
    wants = [
        remote(tables.at[0], tables.at[3 + j], ts_sem.at[2 + j], tr_sem.at[2 + j], device)
        for j, device in enumerate(row_peers)
    ]

    prow = lax.broadcasted_iota(I32, (512, 128), 0)
    pcol = lax.broadcasted_iota(I32, (512, 128), 1)
    pool[...] = 0.125 * ((prow // 64) * 16 + (prow % 32) // 2 == pcol).astype(F32)
    frow = lax.broadcasted_iota(I32, (256, 128), 0)
    fcol = lax.broadcasted_iota(I32, (256, 128), 1)
    spot = (frow % 128) // 32 * 32 + (1 - frow // 128) * 16 + (frow % 32) // 2
    pool_face[...] = 0.125 * (spot == fcol).astype(F32)

    def pick(choice, options):
        found = jnp.zeros_like(options[0])
        for i, option in enumerate(options):
            found = jnp.where(choice == i, option, found)
        return found

    for side in range(2):

        @pl.when(jnp.logical_not(has[side]))
        def _():
            xr[side] = jnp.ones((8, LANES), F32)
            x_in[side] = jnp.zeros((n_y, 2, 2, 128), F32)
            tables[1 + side] = jnp.full((SUB, 128), -1, I32)
            for peer in range(2):
                edge_in[side, peer] = jnp.zeros((4, 128), F32)

    for copy in sent:
        copy.wait_recv()

    px, kx, gx, dx = (
        [[xr[s, n + j : n + j + 1, :] for j in range(2)] for s in range(2)] for n in (0, 2, 4, 6)
    )

    def both(block):
        low, high = [yr[peer, CHUNKS * block : CHUNKS * block + CHUNKS] for peer in range(2)]
        return (
            jnp.where(lane3 < 64, low, pltpu.roll(high, 64, 2)),
            jnp.where(lane3 < 64, pltpu.roll(low, 64, 2), high),
        )

    py, ky = both(0)
    gy, dy = both(1)

    def rotated(quarters):
        return [quarters] + [pltpu.roll(quarters, 128 - 32 * q, 2) for q in range(1, 4)]

    def own_faces(field):
        low, high = y_faces(field)
        return [[low[a], high[a]] for a in range(2)]

    def into_quarters(faces, keys):
        total = jnp.zeros((CHUNKS, SUB, 128), F32)
        for a in range(2):
            for direction in range(2):
                face = jnp.where(lane3 < 32, faces[a][direction], 0.0)
                face = face + pltpu.roll(face, 32, 2)
                face = face + pltpu.roll(face, 64, 2)
                total = total + jnp.where(quarter3 == keys[a][direction], face, 0.0)
        return total

    k_faces, u_faces = own_faces(perm), own_faces(u0)
    k_turned, u_turned = rotated(ky), rotated(py)

    def add_y(ref, a, direction, value):
        if direction == 0:
            ref[a, :, :, 0:128] += value
        else:
            ref[a, :, :, LAST:LANES] += pltpu.roll(value, 96, 2)

    def add_x(ref, a, side, value):
        if side == 0:
            ref[a, 0, 0:1, :] += value
        else:
            ref[a, CHUNKS - 1, SUB - 1 : SUB, :] += value

    for a in range(2):
        for side in range(2):
            w = harmonic(x_face(perm, side, a), pick(ds[a, side], kx[side]))
            wxe[side, a : a + 1, :] = w
            add_x(dg, a, side, w)
            add_x(g, a, side, w * pick(ds[a, side], px[side]))
        for direction in range(2):
            kg = pick(codes[a][direction], k_turned)
            w = jnp.where(lane3 < 32, harmonic(k_faces[a][direction], kg), 0.0)
            wye[a, direction] = w
            add_y(dg, a, direction, w)
            add_y(g, a, direction, w * pick(codes[a][direction], u_turned))

    def line(packed, start, target):
        return pltpu.roll(packed, (target - start) % 4 * 32, 1) if start != target else packed

    px1 = []
    for side in range(2):
        found = []
        for j in range(2):
            gsum, dsum = gx[side][j], dx[side][j]
            mine_p = jnp.zeros((1, LANES), F32)
            mine_k = jnp.zeros((1, LANES), F32)
            for a in range(2):
                linked = ds[a, side] == j
                mine_p = jnp.where(linked, x_face(u0, side, a), mine_p)
                mine_k = jnp.where(linked, x_face(perm, side, a), mine_k)
            w = harmonic(kx[side][j], mine_k)
            gsum = gsum + w * mine_p
            dsum = dsum + w
            ends = []
            for direction in range(2):
                code = tables[1 + side, 2 + 2 * j + direction : 3 + 2 * j + direction, :]
                start = 2 if direction == 0 else 0
                target = 0 if direction == 0 else 3
                values = []
                for f in range(2):
                    options = [
                        line(edge_in[side, peer, f : f + 1, :], start + c, target)
                        for peer in range(2)
                        for c in range(2)
                    ]
                    values.append(pick(code, options))
                kk = kx[side][j][:, 0:128] if direction == 0 else kx[side][j][:, LAST:LANES]
                w = jnp.where(quarter1 == target, harmonic(kk, values[1]), 0.0)
                ends.append((w, w * values[0]))
            gap = jnp.zeros((1, LANES - 256), F32)
            dsum = dsum + jnp.concatenate([ends[0][0], gap, ends[1][0]], axis=1)
            gsum = gsum + jnp.concatenate([ends[0][1], gap, ends[1][1]], axis=1)
            found.append((1.0 - OMEGA) * px[side][j] + OMEGA * gsum / dsum)
        px1.append(found)

    mine_k = into_quarters(k_faces, codes)
    w = harmonic(ky, mine_k)
    gy = gy + w * into_quarters(u_faces, codes)
    dy = dy + w
    slots = []
    for peer in range(2):
        held = yr[peer, 2 * CHUNKS]
        for c in range(2):
            slots.append(jnp.where(minus[peer], held[6 + c : 7 + c, :], held[4 + c : 5 + c, :]))
    rows3 = lax.broadcasted_iota(I32, (CHUNKS, SUB, 128), 0) * SUB + lax.broadcasted_iota(
        I32, (CHUNKS, SUB, 128), 1
    )
    for side in range(2):
        values = []
        for f in range(2):
            total = jnp.zeros((1, 128), F32)
            for q in range(4):
                peer = q // 2
                held = yr[peer, 2 * CHUNKS]
                link = jnp.where(
                    slots[q] == 1, held[2 + side : 3 + side, :], held[side : side + 1, :]
                )
                edge = edge_in[side, peer, 2 + f : 3 + f, :]
                options = [
                    jnp.where(minus[peer], line(edge, 2 * s + 1, q), line(edge, 2 * s, q))
                    for s in range(2)
                ]
                total = jnp.where(quarter1 == q, pick(link, options), total)
            values.append(total)
        r = 0 if side == 0 else CHUNKS * SUB - 1
        here = ky[0, 0:1, :] if side == 0 else ky[CHUNKS - 1, SUB - 1 : SUB, :]
        w = harmonic(here, values[1])
        dy = dy + jnp.where(rows3 == r, w.reshape(1, 1, 128), 0.0)
        gy = gy + jnp.where(rows3 == r, (w * values[0]).reshape(1, 1, 128), 0.0)
    py1 = (1.0 - OMEGA) * py + OMEGA * gy / dy

    def first_update(k, _):
        for a in range(2):
            i = OMEGA / dg[a, k]
            inv[a, k] = i
            u1[a, k] = (1.0 - OMEGA) * u0[a, k] + i * g[a, k]
        return 0

    lax.fori_loop(0, CHUNKS, first_update, 0)
    neighbour_sum(u1)
    u_turned = rotated(py1)
    for a in range(2):
        for side in range(2):
            add_x(g, a, side, wxe[side, a : a + 1, :] * pick(ds[a, side], px1[side]))
        for direction in range(2):
            add_y(g, a, direction, wye[a, direction] * pick(codes[a][direction], u_turned))

    def second_update(k, _):
        for a in range(2):
            u2[a, k] = (1.0 - OMEGA) * u1[a, k] + inv[a, k] * g[a, k]
        return 0

    lax.fori_loop(0, CHUNKS, second_update, 0)
    store = pltpu.make_async_copy(u2, out_hbm, out_sem.at[0])
    store.start()
    neighbour_sum(u2)

    def residual(k, _):
        for a in range(2):
            at_row = pl.multiple_of(a * 32 + k * SUB, SUB)
            r = g[a, k] - dg[a, k] * u2[a, k]
            for t in range(8):
                res[t, pl.ds(at_row, SUB), :] = r[:, 128 * t : 128 * t + 128]
        return 0

    lax.fori_loop(0, CHUNKS, residual, 0)
    paired = [
        res[t, pl.ds(0, 32, stride=2), :] + res[t, pl.ds(1, 32, stride=2), :] for t in range(8)
    ]
    stacked = [jnp.concatenate(paired[4 * h : 4 * h + 4], axis=1) for h in range(2)]

    across = []
    for side in range(2):
        flows = [wxe[side, a : a + 1, :] * x_face(u2, side, a) for a in range(2)]
        for s in range(2):
            total = jnp.zeros((1, LANES), F32)
            for a in range(2):
                total = total + jnp.where(ds[a, side] == s, flows[a], 0.0)
            across.append(total)
    across = jnp.concatenate(across, axis=0)
    stacked += [across[:, 0:512], across[:, 512:1024]]
    pooled = jnp.dot(
        jnp.concatenate(stacked, axis=0), pool[...],
        preferred_element_type=F32, precision=lax.Precision.HIGHEST,
    )
    for a in range(2):
        for t in range(2):
            gathered[my_y, 2 * a + t] = pooled[32 * t + 16 * a : 32 * t + 16 * a + 16, :]
    for side in range(2):
        for t in range(2):
            x_out[side, t] = pooled[64 + 4 * t + 2 * side : 66 + 4 * t + 2 * side, :]

    u_faces = own_faces(u2)
    for direction in range(2):
        total = jnp.zeros((CHUNKS, SUB, 128), F32)
        for a in range(2):
            face = wye[a, direction] * u_faces[a][direction]
            face = face + pltpu.roll(face, 32, 2)
            face = face + pltpu.roll(face, 64, 2)
            code = codes[a][direction]
            slot = pick(code, slots)
            key = jnp.where(code >= 2, 2.0, 0.0) + slot
            hit = (quarter1.astype(F32) == key) & (code >= 0)
            total = total + jnp.where(hit.reshape(1, 1, 128), face, 0.0)
        face_sum[direction] = total.reshape(CHUNKS * SUB, 128)
    halves = []
    for direction in range(2):
        even = face_sum[direction, pl.ds(0, 16, stride=2), :]
        halves.append(even + face_sum[direction, pl.ds(1, 16, stride=2), :])
    gathered[my_y, 4] = jnp.dot(
        jnp.concatenate(halves, axis=1), pool_face[...],
        preferred_element_type=F32, precision=lax.Precision.HIGHEST,
    )

    spread = [
        remote(gathered.at[my_y], gathered.at[my_y], gs_sem.at[o], gr_sem.at[o], device)
        for o, device in enumerate(y_peers)
    ]
    for side in range(2):
        for o, device in enumerate(x_peers[side]):
            n = side * n_y + o
            spread.append(
                Link(x_out.at[side], x_in.at[1 - side, my_y], xs_sem.at[n], xr_sem.at[n], device, side)
            )
    for copy in wants:
        copy.wait_recv()
    for copy in spread:
        copy.wait_recv()

    def device_at(y):
        return (y * 2 + zh) * 2 + core

    piece = (n_y, 2, 16, 128)
    piece_id = device_at(lax.broadcasted_iota(I32, piece, 0)) * 2 + lax.broadcasted_iota(I32, piece, 1)
    x_shape = (n_y, 2, 128)
    x_id = device_at(lax.broadcasted_iota(I32, x_shape, 0)) * 2 + lax.broadcasted_iota(I32, x_shape, 1)
    y_shape = (n_y, 16, 128)
    y_lane = lax.broadcasted_iota(I32, y_shape, 2)
    y_id = (device_at(lax.broadcasted_iota(I32, y_shape, 0)) + 2 * (y_lane // 64) - 1) * 2 + (
        y_lane % 64
    ) // 32
    lane2 = lax.broadcasted_iota(I32, (16, 128), 1)
    row2 = lax.broadcasted_iota(I32, (16, 128), 0)

    def own(holder, j, out, at_slot):
        w = tables[holder, j : j + 1, :]
        w3, w4 = w.reshape(1, 1, 128), w.reshape(1, 1, 1, 128)
        y_part = jnp.sum(jnp.where(y_id == w3, gathered[:, 4], 0.0), axis=0)
        y_part = y_part + pltpu.roll(y_part, 64, 1)
        y_part = y_part + pltpu.roll(y_part, 32, 1)
        for t in range(2):
            held = jnp.stack([gathered[:, t], gathered[:, 2 + t]], axis=1)
            found = jnp.sum(jnp.where(piece_id == w4, held, 0.0), axis=(0, 1))
            found = found + jnp.where(lane2 < 16 if t == 0 else lane2 >= 112, y_part, 0.0)
            for side in range(2):
                x_part = jnp.sum(
                    jnp.where(x_id == w3, x_in[side, :, t], 0.0), axis=(0, 1)
                ).reshape(1, 128)
                found = found + jnp.where(row2 == (0 if side == 0 else 15), x_part, 0.0)
            out[at_slot, :, 128 * t : 128 * t + 128] = found

    for slot, holder in enumerate((3, 5)):
        for j in range(2):
            own(holder, j, sib_out, 2 * slot + j)
    to_sib = remote(sib_out, sib_in, es_sem.at[0], er_sem.at[0], row_peers[0])
    for j in range(2):
        own(4, j, zp_out, j)
        own(0, j, coarse, j)
    to_sib.wait_recv()
    for j in range(2):
        zp_out[j] += sib_in[2 + j]
    to_zpar = remote(zp_out, zp_in, es_sem.at[1], er_sem.at[1], row_peers[1])
    for j in range(2):
        coarse[j] += sib_in[j]
    to_zpar.wait_recv()
    for j in range(2):
        coarse[j] += zp_in[j]
    last = pltpu.make_async_copy(coarse, coarse_hbm, out_sem.at[1])
    last.start()
    for copy in sent + wants + spread + [to_sib, to_zpar]:
        copy.wait_send()
    store.wait()
    last.wait()


def body(pressure, source, perm, brinkman, depth_source, sideways, edge_blocks, restrict_take):
    big = (2, CHUNKS, SUB, LANES)
    n_y = lax.axis_size("inslab") // 4
    vm = lambda *shape: pltpu.VMEM(shape, F32)
    dma = lambda n: pltpu.SemaphoreType.DMA((n,))
    anywhere = pl.BlockSpec(memory_space=pltpu.HBM)
    arrays = [x.reshape(big) for x in (pressure, source, perm)]
    arrays += [brinkman, depth_source, sideways, edge_blocks, restrict_take]
    smoothed, coarse = pl.pallas_call(
        kernel,
        out_shape=(
            jax.ShapeDtypeStruct(big, F32),
            jax.ShapeDtypeStruct((2, 16, 256), F32),
        ),
        in_specs=[anywhere] * 8,
        out_specs=(anywhere, anywhere),
        scratch_shapes=[
            pltpu.SMEM((2,), F32), pltpu.SMEM((2, 2), I32), pltpu.SMEM((2, 4), I32),
            pltpu.SMEM((1, 2, 2), I32), pltpu.SMEM((2,), I32),
        ]
        + [vm(*big) for _ in range(14)]
        + [
            vm(2, 2, LANES), vm(2, 2, CHUNKS, SUB, 128), vm(8, 64, 128), vm(512, 128), vm(256, 128),
            vm(2, 8, LANES), vm(2, 8, LANES),
            vm(2, 2 * CHUNKS + 1, SUB, 128), vm(2, 2 * CHUNKS + 1, SUB, 128),
            vm(2, 4, 128), vm(2, 2, 4, 128),
            pltpu.VMEM((6, SUB, 128), I32),
            vm(2, CHUNKS * SUB, 128),
            vm(n_y, 5, 16, 128), vm(2, 2, 2, 128), vm(2, n_y, 2, 2, 128),
            vm(4, 16, 256), vm(4, 16, 256), vm(2, 16, 256), vm(2, 16, 256), vm(2, 16, 256),
            dma(8), dma(2), dma(8), dma(8), dma(5), dma(5), dma(n_y - 1), dma(n_y - 1),
            dma(2 * n_y), dma(2 * n_y), dma(2), dma(2),
        ],
        compiler_params=pltpu.CompilerParams(
            collective_id=0, has_side_effects=True, vmem_limit_bytes=32 * 1024 * 1024
        ),
    )(*[pltpu.with_memory_space_constraint(x, pltpu.HBM) for x in arrays])
    return smoothed.reshape(pressure.shape), coarse


def solution(mesh):
    group = ("depth", "inslab")
    return jax.shard_map(
        body,
        mesh=mesh,
        in_specs=(
            P(group, None, None),
            P(group, None, None),
            P(group, None, None),
            P(group),
            P(group, None),
            P(group, None),
            P(group, None, None),
            P(group),
        ),
        out_specs=(P(group, None, None), P(group, None, None)),
        check_vma=False,
    )
```

```python
import jax
import jax.numpy as jnp
from jax import lax
from jax.experimental import pallas as pl
from jax.experimental.pallas import tpu as pltpu
from jax.sharding import PartitionSpec as P

OMEGA = 0.8
MESH = pl.DeviceIdType.MESH
F32 = jnp.float32
I32 = jnp.int32
CHUNKS, SUB, LANES = 4, 8, 1024
LAST = LANES - 128


def harmonic(a, b):
    return 2.0 * a * b / (a + b)


def kernel(
    p_hbm, s_hbm, k_hbm, brink_hbm, ds_hbm, snt_hbm, eb_hbm, take_hbm,
    out_hbm, coarse_hbm,
    brink, ds, snt, eb, take,
    u0, src, perm, u1, u2, g, ga, dg, inv, wxm, wxp, wym, wyp, wzm, wzp,
    wxe, wye, res, pool, pool_face,
    xs, xr, ys, yr, edge_out, edge_in,
    tables, face_sum, bulk, late, x_out, x_in, bulk_out, bulk_in, shell_out, shell_in, coarse,
    in_sem, out_sem, hs_sem, hr_sem, ts_sem, tr_sem, bs_sem, br_sem, gs_sem, gr_sem, xs_sem, xr_sem, es_sem, er_sem,
):
    depth = lax.axis_index("depth")
    me = lax.axis_index("inslab")
    n_depth = lax.axis_size("depth")
    n_in = lax.axis_size("inslab")
    n_y = n_in // 4
    my_y = me // 4
    zh = (me // 2) % 2
    core = me % 2

    def at(d, y, z, c):
        return (d, (y * 2 + z) * 2 + c)

    deeper = [lax.rem(depth + n_depth - 1, n_depth), lax.rem(depth + 1, n_depth)]
    beside_me = [lax.rem(me + n_in - 1, n_in), lax.rem(me + 1, n_in)]
    row_peers = [
        at(depth, my_y, zh, 1 - core), at(depth, my_y, 1 - zh, core), at(depth, my_y, 1 - zh, 1 - core)
    ]
    y_peers = [at(depth, lax.rem(my_y + o, n_y), zh, core) for o in range(1, n_y)]
    x_peers = [
        [at(deeper[side], lax.rem(my_y + o, n_y), zh, core) for o in range(n_y)] for side in range(2)
    ]
    i_peers = [(depth, m) for m in beside_me]
    d_peers = [(d, me) for d in deeper]
    corners = [[(d, m) for m in beside_me] for d in deeper]

    has = [depth > 0, depth < n_depth - 1]

    barrier = pltpu.get_barrier_semaphore()

    def greet(partner):
        pl.semaphore_signal(barrier, inc=1, device_id=partner, device_id_type=MESH)

    always = i_peers + row_peers + y_peers
    for partner in always:
        greet(partner)
    for side in range(2):
        pl.when(has[side])(lambda side=side: [greet(p) for p in [d_peers[side]] + corners[side]] and None)
    greeted = len(always) + sum(jnp.where(has[side], 1 + len(corners[side]), 0) for side in range(2))

    small = [(snt_hbm, snt), (ds_hbm, ds), (eb_hbm, eb), (take_hbm, take), (brink_hbm, brink)]
    loads = [
        pltpu.make_async_copy(h, v, in_sem.at[i])
        for i, (h, v) in enumerate([(k_hbm, perm), (p_hbm, u0), (s_hbm, src)] + small)
    ]
    for load in loads:
        load.start()
    for load in loads[3:]:
        load.wait()

    lane3 = lax.broadcasted_iota(I32, (CHUNKS, SUB, 128), 2)
    lane1 = lax.broadcasted_iota(I32, (1, 128), 1)
    row = lax.broadcasted_iota(I32, (SUB, LANES), 0)
    lane = lax.broadcasted_iota(I32, (SUB, LANES), 1)
    zpos = lane % 32
    quarter3 = lane3 // 32
    quarter1 = lane1 // 32

    def remote(a, b, s, r, device):
        copy = pltpu.make_async_remote_copy(
            src_ref=a, dst_ref=b, send_sem=s, recv_sem=r, device_id=device, device_id_type=MESH
        )
        copy.start()
        return copy

    class Link:
        def __init__(self, a, b, s, r, device, side):
            self.args, self.side = (a, b, s, r, device), side
            pl.when(has[side])(lambda: self.make().start())

        def make(self):
            a, b, s, r, device = self.args
            return pltpu.make_async_remote_copy(
                src_ref=a, dst_ref=b, send_sem=s, recv_sem=r, device_id=device, device_id_type=MESH
            )

        def wait_recv(self):
            pl.when(has[1 - self.side])(lambda: self.make().wait_recv())

        def wait_send(self):
            pl.when(has[self.side])(lambda: self.make().wait_send())

    def lies_minus(low):
        found = []
        for a in range(2):
            w = snt[a, 0]
            below = w - 2 < 2 * me
            found.append((w >= 2) & (below if low else jnp.logical_not(below)))
        return found[0] | found[1]

    minus = [lies_minus(True), lies_minus(False)]

    def quarter_of(a, direction):
        w = snt[a, direction]
        column = w & 1
        q = jnp.where(w - 2 < 2 * me, column, 2 + column)
        return jnp.where(w >= 2, q, -1)

    codes = [[quarter_of(a, direction) for direction in range(2)] for a in range(2)]

    trow = lax.broadcasted_iota(I32, (SUB, 128), 0)

    def as_rows(entries):
        tile = jnp.zeros((SUB, 128), I32)
        for i, value in enumerate(entries):
            tile = jnp.where(trow == i, value, tile)
        return tile

    tables[0] = as_rows([take[0], take[1]] + [codes[a][s] for a in range(2) for s in range(2)])
    links = as_rows(
        [ds[a, s] for a in range(2) for s in range(2)]
        + [eb[0, s, c] for s in range(2) for c in range(2)]
    ).astype(F32)

    def y_faces(field):
        low = [field[a, :, :, 0:128] for a in range(2)]
        high = [pltpu.roll(field[a, :, :, LAST:LANES], 32, 2) for a in range(2)]
        return low, high

    def pair_for(faces, is_minus):
        low, high = faces
        cols = []
        for c in range(2):
            from_low = jnp.where(eb[0, 0, c] == 1, low[1], low[0])
            from_high = jnp.where(eb[0, 1, c] == 1, high[1], high[0])
            cols.append(jnp.where(is_minus, from_low, from_high))
        return jnp.where(lane3 < 32, cols[0], pltpu.roll(cols[1], 32, 2))

    def x_face(field, side, a):
        if side == 0:
            return field[a, 0, 0:1, :]
        return field[a, CHUNKS - 1, SUB - 1 : SUB, :]

    def fill(first, second, block):
        for side in range(2):
            for a in range(2):
                n = 4 * block + a
                xs[side, n : n + 1, :] = x_face(first, side, a)
                xs[side, n + 2 : n + 3, :] = x_face(second, side, a)
        one, two = y_faces(first), y_faces(second)
        for peer in range(2):
            ys[peer, CHUNKS * block : CHUNKS * block + CHUNKS] = jnp.where(
                lane3 < 64, pair_for(one, minus[peer]), pltpu.roll(pair_for(two, minus[peer]), 64, 2)
            )

    loads[0].wait()
    loads[1].wait()
    fill(u0, perm, 0)
    for peer in range(2):
        ys[peer, 2 * CHUNKS] = links
    for side in range(2):
        for f, field in enumerate((u0, perm)):
            lines = []
            for a in range(2):
                face = x_face(field, side, a)
                lines.append([face[:, 0:128], pltpu.roll(face[:, LAST:LANES], 32, 1)])
            by_column = [
                jnp.where(eb[0, s, c] == 1, lines[1][s], lines[0][s]) for s in range(2) for c in range(2)
            ]
            by_slot = [lines[a][s] for a in range(2) for s in range(2)]
            for n, listed in enumerate((by_column, by_slot)):
                packed = listed[0]
                for q in range(1, 4):
                    packed = jnp.where(quarter1 == q, pltpu.roll(listed[q], 32 * q, 1), packed)
                edge_out[side, 2 * n + f : 2 * n + f + 1, :] = packed
    def zslot(a, direction):
        return jnp.maximum(snt[a, 2 + direction], 0)

    def beside(field, a, k):
        u = field[a, k]
        before = field[a, jnp.maximum(k - 1, 0), SUB - 1 : SUB, :]
        after = field[a, jnp.minimum(k + 1, CHUNKS - 1), 0:1, :]
        um = jnp.where(row == 0, before, pltpu.roll(u, 1, 0))
        up = jnp.where(row == SUB - 1, after, pltpu.roll(u, SUB - 1, 0))
        ym = pltpu.roll(u, 32, 1)
        yp = pltpu.roll(u, LANES - 32, 1)
        nm = field[zslot(a, 0), k]
        np_ = field[zslot(a, 1), k]
        zm = jnp.where(zpos == 0, pltpu.roll(nm, LANES - 31, 1), pltpu.roll(u, 1, 1))
        zp = jnp.where(zpos == 31, pltpu.roll(np_, 31, 1), pltpu.roll(u, LANES - 1, 1))
        return u, (um, up, ym, yp, zm, zp)

    def weights(k, _):
        for a in range(2):
            kk, nbs = beside(perm, a, k)
            has_zm = snt[a, 2] >= 0
            has_zp = snt[a, 3] >= 0
            keep = (
                jnp.logical_not((row == 0) & (k == 0)),
                jnp.logical_not((row == SUB - 1) & (k == CHUNKS - 1)),
                lane >= 32,
                lane < LANES - 32,
                jnp.logical_or(zpos != 0, has_zm),
                jnp.logical_or(zpos != 31, has_zp),
            )
            total = jnp.full((SUB, LANES), brink[a], F32)
            for store, nb, mask in zip((wxm, wxp, wym, wyp, wzm, wzp), nbs, keep):
                w = jnp.where(mask, harmonic(kk, nb), 0.0)
                store[a, k] = w
                total = total + w
            dg[a, k] = total
        return 0

    lax.fori_loop(0, CHUNKS, weights, 0)
    loads[2].wait()

    def neighbour_sum(field, into):
        def step(k, _):
            for a in range(2):
                _, nbs = beside(field, a, k)
                total = src[a, k]
                for store, nb in zip((wxm, wxp, wym, wyp, wzm, wzp), nbs):
                    total = total + store[a, k] * nb
                into[a, k] = total
            return 0

        lax.fori_loop(0, CHUNKS, step, 0)

    neighbour_sum(u0, g)
    fill(g, dg, 1)

    prow = lax.broadcasted_iota(I32, (512, 128), 0)
    pcol = lax.broadcasted_iota(I32, (512, 128), 1)
    pool[...] = 0.125 * ((prow // 64) * 16 + (prow % 32) // 2 == pcol).astype(F32)
    frow = lax.broadcasted_iota(I32, (128, 128), 0)
    fcol = lax.broadcasted_iota(I32, (128, 128), 1)
    pool_face[...] = 0.125 * (frow // 32 * 16 + (frow % 32) // 2 == fcol).astype(F32)

    def pooled_residual(field, sums, more):
        def step(k, _):
            for a in range(2):
                at_row = pl.multiple_of(a * 32 + k * SUB, SUB)
                r = sums[a, k] - dg[a, k] * field[a, k]
                for t in range(8):
                    res[t, pl.ds(at_row, SUB), :] = r[:, 128 * t : 128 * t + 128]
            return 0

        lax.fori_loop(0, CHUNKS, step, 0)
        paired = [
            res[t, pl.ds(0, 32, stride=2), :] + res[t, pl.ds(1, 32, stride=2), :] for t in range(8)
        ]
        stacked = [jnp.concatenate(paired[4 * h : 4 * h + 4], axis=1) for h in range(2)]
        return jnp.dot(
            jnp.concatenate(stacked + more, axis=0), pool[...],
            preferred_element_type=F32, precision=lax.Precision.HIGHEST,
        )

    def piece_of(pooled, a, t):
        return pooled[32 * t + 16 * a : 32 * t + 16 * a + 16, :]

    def inner_first(k, _):
        for a in range(2):
            i = OMEGA / dg[a, k]
            inv[a, k] = i
            u1[a, k] = (1.0 - OMEGA) * u0[a, k] + i * g[a, k]
        return 0

    def inner_second(k, _):
        for a in range(2):
            u2[a, k] = (1.0 - OMEGA) * u1[a, k] + inv[a, k] * ga[a, k]
        return 0

    def inner_pieces():
        lax.fori_loop(0, CHUNKS, inner_first, 0)
        neighbour_sum(u1, ga)
        lax.fori_loop(0, CHUNKS, inner_second, 0)
        neighbour_sum(u2, ga)
        pooled = pooled_residual(u2, ga, [])
        for a in range(2):
            for t in range(2):
                n = 4 * a + 2 * t
                bulk[my_y, n : n + 2] = piece_of(pooled, a, t).reshape(2, SUB, 128)
        sides = jnp.where(quarter1 % 2 == 0, minus[0].astype(F32), minus[1].astype(F32))
        bulk[my_y, 8] = jnp.broadcast_to(sides, (SUB, 128))

    inner_pieces()
    pl.semaphore_wait(barrier, greeted)
    sent = []
    for peer in range(2):
        sent.append(remote(ys.at[peer], yr.at[1 - peer], hs_sem.at[peer], hr_sem.at[peer], i_peers[peer]))
    for side in range(2):
        for peer in range(2):
            n = 4 + 2 * side + peer
            sent.append(
                Link(
                    edge_out.at[side], edge_in.at[1 - side, 1 - peer],
                    hs_sem.at[n], hr_sem.at[n], corners[side][peer], side,
                )
            )
    for side in range(2):
        n = 2 + side
        sent.append(
            Link(xs.at[side], xr.at[1 - side], hs_sem.at[n], hr_sem.at[n], d_peers[side], side)
        )
        sent.append(
            Link(
                tables.at[0], tables.at[2 - side], ts_sem.at[side], tr_sem.at[side], d_peers[side], side
            )
        )
    wants = [
        remote(tables.at[0], tables.at[3 + j], ts_sem.at[2 + j], tr_sem.at[2 + j], device)
        for j, device in enumerate(row_peers)
    ]
    early = [
        remote(bulk.at[my_y], bulk.at[my_y], bs_sem.at[o], br_sem.at[o], device)
        for o, device in enumerate(y_peers)
    ]

    def pick(choice, options):
        found = jnp.zeros_like(options[0])
        for i, option in enumerate(options):
            found = jnp.where(choice == i, option, found)
        return found

    for side in range(2):

        @pl.when(jnp.logical_not(has[side]))
        def _():
            xr[side] = jnp.ones((8, LANES), F32)
            x_in[side] = jnp.zeros((n_y, 2, 2, 128), F32)
            tables[1 + side] = jnp.full((SUB, 128), -1, I32)
            for peer in range(2):
                edge_in[side, peer] = jnp.zeros((4, 128), F32)

    for copy in sent:
        copy.wait_recv()

    px, kx, gx, dx = (
        [[xr[s, n + j : n + j + 1, :] for j in range(2)] for s in range(2)] for n in (0, 2, 4, 6)
    )

    def both(block):
        low, high = [yr[peer, CHUNKS * block : CHUNKS * block + CHUNKS] for peer in range(2)]
        return (
            jnp.where(lane3 < 64, low, pltpu.roll(high, 64, 2)),
            jnp.where(lane3 < 64, pltpu.roll(low, 64, 2), high),
        )

    py, ky = both(0)
    gy, dy = both(1)

    def rotated(quarters):
        return [quarters] + [pltpu.roll(quarters, 128 - 32 * q, 2) for q in range(1, 4)]

    def own_faces(field):
        low, high = y_faces(field)
        return [[low[a], high[a]] for a in range(2)]

    def into_quarters(faces, keys):
        total = jnp.zeros((CHUNKS, SUB, 128), F32)
        for a in range(2):
            for direction in range(2):
                face = jnp.where(lane3 < 32, faces[a][direction], 0.0)
                face = face + pltpu.roll(face, 32, 2)
                face = face + pltpu.roll(face, 64, 2)
                total = total + jnp.where(quarter3 == keys[a][direction], face, 0.0)
        return total

    k_faces, u_faces = own_faces(perm), own_faces(u0)
    k_turned, u_turned = rotated(ky), rotated(py)

    def add_y(ref, a, direction, value):
        if direction == 0:
            ref[a, :, :, 0:128] += value
        else:
            ref[a, :, :, LAST:LANES] += pltpu.roll(value, 96, 2)

    def add_x(ref, a, side, value):
        if side == 0:
            ref[a, 0, 0:1, :] += value
        else:
            ref[a, CHUNKS - 1, SUB - 1 : SUB, :] += value

    for a in range(2):
        for side in range(2):
            w = harmonic(x_face(perm, side, a), pick(ds[a, side], kx[side]))
            wxe[side, a : a + 1, :] = w
            add_x(dg, a, side, w)
            add_x(g, a, side, w * pick(ds[a, side], px[side]))
        for direction in range(2):
            kg = pick(codes[a][direction], k_turned)
            w = jnp.where(lane3 < 32, harmonic(k_faces[a][direction], kg), 0.0)
            wye[a, direction] = w
            add_y(dg, a, direction, w)
            add_y(g, a, direction, w * pick(codes[a][direction], u_turned))

    def line(packed, start, target):
        return pltpu.roll(packed, (target - start) % 4 * 32, 1) if start != target else packed

    px1 = []
    for side in range(2):
        found = []
        for j in range(2):
            gsum, dsum = gx[side][j], dx[side][j]
            mine_p = jnp.zeros((1, LANES), F32)
            mine_k = jnp.zeros((1, LANES), F32)
            for a in range(2):
                linked = ds[a, side] == j
                mine_p = jnp.where(linked, x_face(u0, side, a), mine_p)
                mine_k = jnp.where(linked, x_face(perm, side, a), mine_k)
            w = harmonic(kx[side][j], mine_k)
            gsum = gsum + w * mine_p
            dsum = dsum + w
            ends = []
            for direction in range(2):
                code = tables[1 + side, 2 + 2 * j + direction : 3 + 2 * j + direction, :]
                start = 2 if direction == 0 else 0
                target = 0 if direction == 0 else 3
                values = []
                for f in range(2):
                    options = [
                        line(edge_in[side, peer, f : f + 1, :], start + c, target)
                        for peer in range(2)
                        for c in range(2)
                    ]
                    values.append(pick(code, options))
                kk = kx[side][j][:, 0:128] if direction == 0 else kx[side][j][:, LAST:LANES]
                w = jnp.where(quarter1 == target, harmonic(kk, values[1]), 0.0)
                ends.append((w, w * values[0]))
            gap = jnp.zeros((1, LANES - 256), F32)
            dsum = dsum + jnp.concatenate([ends[0][0], gap, ends[1][0]], axis=1)
            gsum = gsum + jnp.concatenate([ends[0][1], gap, ends[1][1]], axis=1)
            found.append((1.0 - OMEGA) * px[side][j] + OMEGA * gsum / dsum)
        px1.append(found)

    mine_k = into_quarters(k_faces, codes)
    w = harmonic(ky, mine_k)
    gy = gy + w * into_quarters(u_faces, codes)
    dy = dy + w
    slots = []
    for peer in range(2):
        held = yr[peer, 2 * CHUNKS]
        for c in range(2):
            slots.append(jnp.where(minus[peer], held[6 + c : 7 + c, :], held[4 + c : 5 + c, :]))
    rows3 = lax.broadcasted_iota(I32, (CHUNKS, SUB, 128), 0) * SUB + lax.broadcasted_iota(
        I32, (CHUNKS, SUB, 128), 1
    )
    for side in range(2):
        values = []
        for f in range(2):
            total = jnp.zeros((1, 128), F32)
            for q in range(4):
                peer = q // 2
                held = yr[peer, 2 * CHUNKS]
                link = jnp.where(
                    slots[q] == 1, held[2 + side : 3 + side, :], held[side : side + 1, :]
                )
                edge = edge_in[side, peer, 2 + f : 3 + f, :]
                options = [
                    jnp.where(minus[peer], line(edge, 2 * s + 1, q), line(edge, 2 * s, q))
                    for s in range(2)
                ]
                total = jnp.where(quarter1 == q, pick(link, options), total)
            values.append(total)
        r = 0 if side == 0 else CHUNKS * SUB - 1
        here = ky[0, 0:1, :] if side == 0 else ky[CHUNKS - 1, SUB - 1 : SUB, :]
        w = harmonic(here, values[1])
        dy = dy + jnp.where(rows3 == r, w.reshape(1, 1, 128), 0.0)
        gy = gy + jnp.where(rows3 == r, (w * values[0]).reshape(1, 1, 128), 0.0)
    py1 = (1.0 - OMEGA) * py + OMEGA * gy / dy

    def first_update(k, _):
        for a in range(2):
            i = OMEGA / dg[a, k]
            inv[a, k] = i
            u1[a, k] = (1.0 - OMEGA) * u0[a, k] + i * g[a, k]
        return 0

    lax.fori_loop(0, CHUNKS, first_update, 0)
    neighbour_sum(u1, g)
    u_turned = rotated(py1)
    for a in range(2):
        for side in range(2):
            add_x(g, a, side, wxe[side, a : a + 1, :] * pick(ds[a, side], px1[side]))
        for direction in range(2):
            add_y(g, a, direction, wye[a, direction] * pick(codes[a][direction], u_turned))

    def second_update(k, _):
        for a in range(2):
            u2[a, k] = (1.0 - OMEGA) * u1[a, k] + inv[a, k] * g[a, k]
        return 0

    lax.fori_loop(0, CHUNKS, second_update, 0)
    store = pltpu.make_async_copy(u2, out_hbm, out_sem.at[0])
    store.start()
    neighbour_sum(u2, g)

    across = []
    for side in range(2):
        flows = [wxe[side, a : a + 1, :] * x_face(u2, side, a) for a in range(2)]
        for s in range(2):
            total = jnp.zeros((1, LANES), F32)
            for a in range(2):
                total = total + jnp.where(ds[a, side] == s, flows[a], 0.0)
            across.append(total)
    across = jnp.concatenate(across, axis=0)
    pooled = pooled_residual(u2, g, [across[:, 0:512], across[:, 512:1024]])
    lane2 = lax.broadcasted_iota(I32, (16, 128), 1)
    edges = jnp.zeros((16, 128), F32)
    for a in range(2):
        for t in range(2):
            part = piece_of(pooled, a, t)
            late[my_y, a, 4 * t : 4 * t + 2, :] = part[0:2, :]
            late[my_y, a, 4 * t + 2 : 4 * t + 4, :] = part[14:16, :]
            part = part if a == t else pltpu.roll(part, 64, 1)
            edges = jnp.where(lane2 // 32 == 2 * a + t, part, edges)
    late[my_y, 2:4] = edges.reshape(2, SUB, 128)
    for side in range(2):
        for t in range(2):
            x_out[side, t] = pooled[64 + 4 * t + 2 * side : 66 + 4 * t + 2 * side, :]

    u_faces = own_faces(u2)
    for direction in range(2):
        total = jnp.zeros((CHUNKS, SUB, 128), F32)
        for a in range(2):
            face = wye[a, direction] * u_faces[a][direction]
            face = face + pltpu.roll(face, 32, 2)
            face = face + pltpu.roll(face, 64, 2)
            code = codes[a][direction]
            slot = pick(code, slots)
            key = jnp.where(code >= 2, 2.0, 0.0) + slot
            hit = (quarter1.astype(F32) == key) & (code >= 0)
            total = total + jnp.where(hit.reshape(1, 1, 128), face, 0.0)
        face_sum[direction] = total.reshape(CHUNKS * SUB, 128)
    halves = [
        face_sum[direction, pl.ds(first, 16, stride=2), :] for direction in range(2) for first in range(2)
    ]
    faces = jnp.dot(
        halves[0] + halves[1] + halves[2] + halves[3], pool_face[...],
        preferred_element_type=F32, precision=lax.Precision.HIGHEST,
    )
    late[my_y, 4] = jnp.where(lane2[0:8] < 64, faces[0:8], pltpu.roll(faces[8:16], 64, 1))

    spread = [
        remote(late.at[my_y], late.at[my_y], gs_sem.at[o], gr_sem.at[o], device)
        for o, device in enumerate(y_peers)
    ]
    for side in range(2):
        for o, device in enumerate(x_peers[side]):
            n = side * n_y + o
            spread.append(
                Link(x_out.at[side], x_in.at[1 - side, my_y], xs_sem.at[n], xr_sem.at[n], device, side)
            )
    for copy in wants + early:
        copy.wait_recv()

    def device_at(y):
        return (y * 2 + zh) * 2 + core

    def iota(shape, dim):
        return lax.broadcasted_iota(I32, shape, dim)

    bulk_shape = (n_y, 2, 4, SUB, 128)
    bulk_id = device_at(iota(bulk_shape, 0)) * 2 + iota(bulk_shape, 1)

    def want(holder, j):
        return tables[holder, j : j + 1, :]

    holders = (0, 3, 4, 5)
    for h in (2, 3, 1, 0):
        held = bulk[:, 0:8].reshape(bulk_shape)
        for j in range(2):
            w = want(holders[h], j).reshape(1, 1, 1, 1, 128)
            bulk_out[h, 4 * j : 4 * j + 4] = jnp.sum(jnp.where(bulk_id == w, held, 0.0), axis=(0, 1))
    rows_of_bulk = [
        remote(bulk_out.at[1 + j], bulk_in.at[j], es_sem.at[j], er_sem.at[j], row_peers[j])
        for j in (1, 2, 0)
    ]

    for copy in spread:
        copy.wait_recv()

    a_shape = (n_y, 2, SUB, 128)
    a_id = device_at(iota(a_shape, 0)) * 2 + iota(a_shape, 1)
    b_id = device_at(iota(a_shape, 0)) * 2 + iota(a_shape, 3) // 64
    x_shape = (n_y, 2, 128)
    x_id = device_at(iota(x_shape, 0)) * 2 + iota(x_shape, 1)
    y_shape = (n_y, SUB, 128)
    y_lane = iota(y_shape, 2)
    y_id = (device_at(iota(y_shape, 0)) + 2 * (y_lane // 32 % 2) - 1) * 2 + y_lane // 16 % 2
    row8 = iota((SUB, 128), 0)
    lane8 = iota((SUB, 128), 1)

    def shell(holder, j):
        w2 = want(holder, j)
        w3, w4 = w2.reshape(1, 1, 128), w2.reshape(1, 1, 1, 128)
        rows = jnp.sum(jnp.where(a_id == w4, late[:, 0:2], 0.0), axis=(0, 1))
        edges = jnp.sum(jnp.where(b_id == w4, late[:, 2:4], 0.0), axis=0)
        halves = [edges[n] + pltpu.roll(edges[n], 64, 1) for n in range(2)]
        for side in range(2):
            line = [
                jnp.sum(jnp.where(x_id == w3, x_in[side, :, t], 0.0), axis=(0, 1)).reshape(1, 128)
                for t in range(2)
            ]
            for t in range(2):
                rows = rows + jnp.where(row8 == 4 * t + 3 * side, line[t], 0.0)
            both_ends = jnp.where(lane8 < 32, line[0], pltpu.roll(line[1], 64, 1))
            halves[side] = halves[side] + jnp.where(row8 == 7 * side, both_ends, 0.0)
        found = jnp.where(y_id == w3, late[:, 4], 0.0)
        for f in range(2):
            part = jnp.sum(jnp.where(bulk[:, 8] == f, found, 0.0), axis=0)
            part = part + pltpu.roll(part, 112, 1)
            part = part + pltpu.roll(part, 96, 1)
            spot = lane8 // 16 == 3 * f
            for n in range(2):
                turn = (48 * f + 64 * n) % 128
                moved = pltpu.roll(part, turn, 1) if turn else part
                halves[n] = halves[n] + jnp.where(spot, moved, 0.0)
        return rows, halves

    rows_of_shells = []
    for h in (3, 2, 1, 0):
        one, two = shell(holders[h], 0), shell(holders[h], 1)
        shell_out[h, 0] = one[0]
        shell_out[h, 1] = two[0]
        for n in range(2):
            shell_out[h, 2 + n] = jnp.where(lane8 < 64, one[1][n], pltpu.roll(two[1][n], 64, 1))
        if h:
            rows_of_shells.append(
                remote(
                    shell_out.at[h], shell_in.at[h - 1], es_sem.at[2 + h], er_sem.at[2 + h],
                    row_peers[h - 1],
                )
            )
    for copy in rows_of_bulk:
        copy.wait_recv()
    inner = bulk_out[0] + bulk_in[0] + bulk_in[1] + bulk_in[2]
    for copy in rows_of_shells:
        copy.wait_recv()
    outer = shell_out[0] + shell_in[0] + shell_in[1] + shell_in[2]
    for j in range(2):
        rows = outer[j]
        turned = pltpu.roll(rows, 4, 0)
        for n in range(2):
            edges = outer[2 + n] if j == 0 else pltpu.roll(outer[2 + n], 64, 1)
            for t in range(2):
                line = rows if t == n else turned
                found = jnp.where(row8 < 2 if n == 0 else row8 >= 6, line, inner[4 * j + 2 * t + n])
                if t == 0:
                    found = jnp.where(lane8 < 32, edges, found)
                else:
                    found = jnp.where(lane8 >= 96, pltpu.roll(edges, 64, 1), found)
                coarse[j, SUB * n : SUB * n + SUB, 128 * t : 128 * t + 128] = found
    last = pltpu.make_async_copy(coarse, coarse_hbm, out_sem.at[1])
    last.start()
    for copy in sent + wants + early + spread + rows_of_bulk + rows_of_shells:
        copy.wait_send()
    store.wait()
    last.wait()


def body(pressure, source, perm, brinkman, depth_source, sideways, edge_blocks, restrict_take):
    big = (2, CHUNKS, SUB, LANES)
    n_y = lax.axis_size("inslab") // 4
    vm = lambda *shape: pltpu.VMEM(shape, F32)
    dma = lambda n: pltpu.SemaphoreType.DMA((n,))
    anywhere = pl.BlockSpec(memory_space=pltpu.HBM)
    arrays = [x.reshape(big) for x in (pressure, source, perm)]
    arrays += [brinkman, depth_source, sideways, edge_blocks, restrict_take]
    smoothed, coarse = pl.pallas_call(
        kernel,
        out_shape=(
            jax.ShapeDtypeStruct(big, F32),
            jax.ShapeDtypeStruct((2, 16, 256), F32),
        ),
        in_specs=[anywhere] * 8,
        out_specs=(anywhere, anywhere),
        scratch_shapes=[
            pltpu.SMEM((2,), F32), pltpu.SMEM((2, 2), I32), pltpu.SMEM((2, 4), I32),
            pltpu.SMEM((1, 2, 2), I32), pltpu.SMEM((2,), I32),
        ]
        + [vm(*big) for _ in range(15)]
        + [
            vm(2, 2, LANES), vm(2, 2, CHUNKS, SUB, 128), vm(8, 64, 128), vm(512, 128), vm(128, 128),
            vm(2, 8, LANES), vm(2, 8, LANES),
            vm(2, 2 * CHUNKS + 1, SUB, 128), vm(2, 2 * CHUNKS + 1, SUB, 128),
            vm(2, 4, 128), vm(2, 2, 4, 128),
            pltpu.VMEM((6, SUB, 128), I32),
            vm(2, CHUNKS * SUB, 128),
            vm(n_y, 9, SUB, 128), vm(n_y, 5, SUB, 128), vm(2, 2, 2, 128), vm(2, n_y, 2, 2, 128),
            vm(4, 8, SUB, 128), vm(3, 8, SUB, 128), vm(4, 4, SUB, 128), vm(3, 4, SUB, 128), vm(2, 16, 256),
            dma(8), dma(2), dma(8), dma(8), dma(5), dma(5), dma(n_y - 1), dma(n_y - 1),
            dma(n_y - 1), dma(n_y - 1), dma(2 * n_y), dma(2 * n_y), dma(6), dma(6),
        ],
        compiler_params=pltpu.CompilerParams(
            collective_id=0, has_side_effects=True, vmem_limit_bytes=32 * 1024 * 1024
        ),
    )(*[pltpu.with_memory_space_constraint(x, pltpu.HBM) for x in arrays])
    return smoothed.reshape(pressure.shape), coarse


def solution(mesh):
    group = ("depth", "inslab")
    return jax.shard_map(
        body,
        mesh=mesh,
        in_specs=(
            P(group, None, None),
            P(group, None, None),
            P(group, None, None),
            P(group),
            P(group, None),
            P(group, None),
            P(group, None, None),
            P(group),
        ),
        out_specs=(P(group, None, None), P(group, None, None)),
        check_vma=False,
    )
```

```python
import jax
import jax.numpy as jnp
from jax import lax
from jax.experimental import pallas as pl
from jax.experimental.pallas import tpu as pltpu
from jax.sharding import PartitionSpec as P

OMEGA = 0.8
MESH = pl.DeviceIdType.MESH
F32 = jnp.float32
I32 = jnp.int32
CHUNKS, SUB, LANES = 4, 8, 1024
LAST = LANES - 128


def harmonic(a, b):
    return 2.0 * a * b / (a + b)


def kernel(
    p_hbm, s_hbm, k_hbm, brink_hbm, ds_hbm, snt_hbm, eb_hbm, take_hbm,
    out_hbm, coarse_hbm,
    brink, ds, snt, eb, take,
    u0, src, perm, u1, u2, g, ga, dg, inv, wxm, wxp, wym, wyp, wzm, wzp,
    wxe, wye, res, pool, pool_face,
    xs, xr, ys, yr, edge_out, edge_in,
    tables, face_sum, bulk, late, x_out, x_in, bulk_out, bulk_in, shell_out, shell_in, coarse,
    in_sem, out_sem, hs_sem, hr_sem, ts_sem, tr_sem, bs_sem, br_sem, gs_sem, gr_sem, xs_sem, xr_sem, es_sem, er_sem,
):
    depth = lax.axis_index("depth")
    me = lax.axis_index("inslab")
    n_depth = lax.axis_size("depth")
    n_in = lax.axis_size("inslab")
    n_y = n_in // 4
    my_y = me // 4
    zh = (me // 2) % 2
    core = me % 2

    def at(d, y, z, c):
        return (d, (y * 2 + z) * 2 + c)

    deeper = [lax.rem(depth + n_depth - 1, n_depth), lax.rem(depth + 1, n_depth)]
    beside_me = [lax.rem(me + n_in - 1, n_in), lax.rem(me + 1, n_in)]
    row_peers = [
        at(depth, my_y, zh, 1 - core), at(depth, my_y, 1 - zh, core), at(depth, my_y, 1 - zh, 1 - core)
    ]
    y_peers = [at(depth, lax.rem(my_y + o, n_y), zh, core) for o in range(1, n_y)]
    x_peers = [
        [at(deeper[side], lax.rem(my_y + o, n_y), zh, core) for o in range(n_y)] for side in range(2)
    ]
    i_peers = [(depth, m) for m in beside_me]
    d_peers = [(d, me) for d in deeper]
    corners = [[(d, m) for m in beside_me] for d in deeper]

    has = [depth > 0, depth < n_depth - 1]

    barrier = pltpu.get_barrier_semaphore()

    def greet(partner):
        pl.semaphore_signal(barrier, inc=1, device_id=partner, device_id_type=MESH)

    always = i_peers + row_peers + y_peers
    for partner in always:
        greet(partner)
    for side in range(2):
        pl.when(has[side])(lambda side=side: [greet(p) for p in [d_peers[side]] + corners[side]] and None)
    greeted = len(always) + sum(jnp.where(has[side], 1 + len(corners[side]), 0) for side in range(2))

    small = [(snt_hbm, snt), (ds_hbm, ds), (eb_hbm, eb), (take_hbm, take), (brink_hbm, brink)]
    loads = [
        pltpu.make_async_copy(h, v, in_sem.at[i])
        for i, (h, v) in enumerate([(k_hbm, perm), (p_hbm, u0), (s_hbm, src)] + small)
    ]
    for load in loads:
        load.start()
    for load in loads[3:]:
        load.wait()

    lane3 = lax.broadcasted_iota(I32, (CHUNKS, SUB, 128), 2)
    lane1 = lax.broadcasted_iota(I32, (1, 128), 1)
    row = lax.broadcasted_iota(I32, (SUB, LANES), 0)
    lane = lax.broadcasted_iota(I32, (SUB, LANES), 1)
    zpos = lane % 32
    quarter3 = lane3 // 32
    quarter1 = lane1 // 32

    def remote(a, b, s, r, device):
        copy = pltpu.make_async_remote_copy(
            src_ref=a, dst_ref=b, send_sem=s, recv_sem=r, device_id=device, device_id_type=MESH
        )
        copy.start()
        return copy

    class Link:
        def __init__(self, a, b, s, r, device, side):
            self.args, self.side = (a, b, s, r, device), side
            pl.when(has[side])(lambda: self.make().start())

        def make(self):
            a, b, s, r, device = self.args
            return pltpu.make_async_remote_copy(
                src_ref=a, dst_ref=b, send_sem=s, recv_sem=r, device_id=device, device_id_type=MESH
            )

        def wait_recv(self):
            pl.when(has[1 - self.side])(lambda: self.make().wait_recv())

        def wait_send(self):
            pl.when(has[self.side])(lambda: self.make().wait_send())

    def lies_minus(low):
        found = []
        for a in range(2):
            w = snt[a, 0]
            below = w - 2 < 2 * me
            found.append((w >= 2) & (below if low else jnp.logical_not(below)))
        return found[0] | found[1]

    minus = [lies_minus(True), lies_minus(False)]

    def quarter_of(a, direction):
        w = snt[a, direction]
        column = w & 1
        q = jnp.where(w - 2 < 2 * me, column, 2 + column)
        return jnp.where(w >= 2, q, -1)

    codes = [[quarter_of(a, direction) for direction in range(2)] for a in range(2)]

    trow = lax.broadcasted_iota(I32, (SUB, 128), 0)

    def as_rows(entries):
        tile = jnp.zeros((SUB, 128), I32)
        for i, value in enumerate(entries):
            tile = jnp.where(trow == i, value, tile)
        return tile

    tables[0] = as_rows([take[0], take[1]] + [codes[a][s] for a in range(2) for s in range(2)])
    links = as_rows(
        [ds[a, s] for a in range(2) for s in range(2)]
        + [eb[0, s, c] for s in range(2) for c in range(2)]
    ).astype(F32)

    def y_faces(field):
        low = [field[a, :, :, 0:128] for a in range(2)]
        high = [pltpu.roll(field[a, :, :, LAST:LANES], 32, 2) for a in range(2)]
        return low, high

    def pair_for(faces, is_minus):
        low, high = faces
        cols = []
        for c in range(2):
            from_low = jnp.where(eb[0, 0, c] == 1, low[1], low[0])
            from_high = jnp.where(eb[0, 1, c] == 1, high[1], high[0])
            cols.append(jnp.where(is_minus, from_low, from_high))
        return jnp.where(lane3 < 32, cols[0], pltpu.roll(cols[1], 32, 2))

    def x_face(field, side, a):
        if side == 0:
            return field[a, 0, 0:1, :]
        return field[a, CHUNKS - 1, SUB - 1 : SUB, :]

    def fill(first, second, block):
        for side in range(2):
            for a in range(2):
                n = 4 * block + a
                xs[side, n : n + 1, :] = x_face(first, side, a)
                xs[side, n + 2 : n + 3, :] = x_face(second, side, a)
        one, two = y_faces(first), y_faces(second)
        for peer in range(2):
            ys[peer, CHUNKS * block : CHUNKS * block + CHUNKS] = jnp.where(
                lane3 < 64, pair_for(one, minus[peer]), pltpu.roll(pair_for(two, minus[peer]), 64, 2)
            )

    loads[0].wait()
    loads[1].wait()
    fill(u0, perm, 0)
    for peer in range(2):
        ys[peer, 2 * CHUNKS] = links
    for side in range(2):
        for f, field in enumerate((u0, perm)):
            lines = []
            for a in range(2):
                face = x_face(field, side, a)
                lines.append([face[:, 0:128], pltpu.roll(face[:, LAST:LANES], 32, 1)])
            by_column = [
                jnp.where(eb[0, s, c] == 1, lines[1][s], lines[0][s]) for s in range(2) for c in range(2)
            ]
            by_slot = [lines[a][s] for a in range(2) for s in range(2)]
            for n, listed in enumerate((by_column, by_slot)):
                packed = listed[0]
                for q in range(1, 4):
                    packed = jnp.where(quarter1 == q, pltpu.roll(listed[q], 32 * q, 1), packed)
                edge_out[side, 2 * n + f : 2 * n + f + 1, :] = packed
    def zslot(a, direction):
        return jnp.maximum(snt[a, 2 + direction], 0)

    def beside(field, a, k):
        u = field[a, k]
        before = field[a, jnp.maximum(k - 1, 0), SUB - 1 : SUB, :]
        after = field[a, jnp.minimum(k + 1, CHUNKS - 1), 0:1, :]
        um = jnp.where(row == 0, before, pltpu.roll(u, 1, 0))
        up = jnp.where(row == SUB - 1, after, pltpu.roll(u, SUB - 1, 0))
        ym = pltpu.roll(u, 32, 1)
        yp = pltpu.roll(u, LANES - 32, 1)
        nm = field[zslot(a, 0), k]
        np_ = field[zslot(a, 1), k]
        zm = jnp.where(zpos == 0, pltpu.roll(nm, LANES - 31, 1), pltpu.roll(u, 1, 1))
        zp = jnp.where(zpos == 31, pltpu.roll(np_, 31, 1), pltpu.roll(u, LANES - 1, 1))
        return u, (um, up, ym, yp, zm, zp)

    def weights(k, _):
        for a in range(2):
            kk, nbs = beside(perm, a, k)
            has_zm = snt[a, 2] >= 0
            has_zp = snt[a, 3] >= 0
            keep = (
                jnp.logical_not((row == 0) & (k == 0)),
                jnp.logical_not((row == SUB - 1) & (k == CHUNKS - 1)),
                lane >= 32,
                lane < LANES - 32,
                jnp.logical_or(zpos != 0, has_zm),
                jnp.logical_or(zpos != 31, has_zp),
            )
            total = jnp.full((SUB, LANES), brink[a], F32)
            for store, nb, mask in zip((wxm, wxp, wym, wyp, wzm, wzp), nbs, keep):
                w = jnp.where(mask, harmonic(kk, nb), 0.0)
                store[a, k] = w
                total = total + w
            dg[a, k] = total
        return 0

    lax.fori_loop(0, CHUNKS, weights, 0)
    loads[2].wait()

    def neighbour_sum(field, into, first=0, stride=1, count=CHUNKS):
        def step(n, _):
            k = first + stride * n
            for a in range(2):
                _, nbs = beside(field, a, k)
                total = src[a, k]
                for store, nb in zip((wxm, wxp, wym, wyp, wzm, wzp), nbs):
                    total = total + store[a, k] * nb
                into[a, k] = total
            return 0

        lax.fori_loop(0, count, step, 0)

    neighbour_sum(u0, g)
    fill(g, dg, 1)

    prow = lax.broadcasted_iota(I32, (512, 128), 0)
    pcol = lax.broadcasted_iota(I32, (512, 128), 1)
    pool[...] = 0.125 * ((prow // 64) * 16 + (prow % 32) // 2 == pcol).astype(F32)
    frow = lax.broadcasted_iota(I32, (128, 128), 0)
    fcol = lax.broadcasted_iota(I32, (128, 128), 1)
    pool_face[...] = 0.125 * (frow // 32 * 16 + (frow % 32) // 2 == fcol).astype(F32)

    def pooled_residual(field, sums):
        def step(k, _):
            for a in range(2):
                at_row = pl.multiple_of(a * 32 + k * SUB, SUB)
                r = sums[a, k] - dg[a, k] * field[a, k]
                for t in range(8):
                    res[t, pl.ds(at_row, SUB), :] = r[:, 128 * t : 128 * t + 128]
            return 0

        lax.fori_loop(0, CHUNKS, step, 0)
        paired = [
            res[t, pl.ds(0, 32, stride=2), :] + res[t, pl.ds(1, 32, stride=2), :] for t in range(8)
        ]
        stacked = [jnp.concatenate(paired[4 * h : 4 * h + 4], axis=1) for h in range(2)]
        return jnp.dot(
            jnp.concatenate(stacked, axis=0), pool[...],
            preferred_element_type=F32, precision=lax.Precision.HIGHEST,
        )

    def piece_of(pooled, a, t):
        return pooled[32 * t + 16 * a : 32 * t + 16 * a + 16, :]

    def inner_first(k, _):
        for a in range(2):
            i = OMEGA / dg[a, k]
            inv[a, k] = i
            u1[a, k] = (1.0 - OMEGA) * u0[a, k] + i * g[a, k]
        return 0

    def inner_second(k, _):
        for a in range(2):
            u2[a, k] = (1.0 - OMEGA) * u1[a, k] + inv[a, k] * ga[a, k]
        return 0

    def inner_pieces():
        lax.fori_loop(0, CHUNKS, inner_first, 0)
        neighbour_sum(u1, ga)
        lax.fori_loop(0, CHUNKS, inner_second, 0)
        neighbour_sum(u2, ga)
        pooled = pooled_residual(u2, ga)
        for a in range(2):
            for t in range(2):
                n = 4 * a + 2 * t
                bulk[my_y, n : n + 2] = piece_of(pooled, a, t).reshape(2, SUB, 128)
        sides = jnp.where(quarter1 % 2 == 0, minus[0].astype(F32), minus[1].astype(F32))
        bulk[my_y, 8] = jnp.broadcast_to(sides, (SUB, 128))

    pl.when(zh == 0)(inner_pieces)
    pl.semaphore_wait(barrier, greeted)
    sent = []
    for peer in range(2):
        sent.append(remote(ys.at[peer], yr.at[1 - peer], hs_sem.at[peer], hr_sem.at[peer], i_peers[peer]))
    for side in range(2):
        for peer in range(2):
            n = 4 + 2 * side + peer
            sent.append(
                Link(
                    edge_out.at[side], edge_in.at[1 - side, 1 - peer],
                    hs_sem.at[n], hr_sem.at[n], corners[side][peer], side,
                )
            )
    for side in range(2):
        n = 2 + side
        sent.append(
            Link(xs.at[side], xr.at[1 - side], hs_sem.at[n], hr_sem.at[n], d_peers[side], side)
        )
        sent.append(
            Link(
                tables.at[0], tables.at[2 - side], ts_sem.at[side], tr_sem.at[side], d_peers[side], side
            )
        )
    wants = [
        remote(tables.at[0], tables.at[3 + j], ts_sem.at[2 + j], tr_sem.at[2 + j], device)
        for j, device in enumerate(row_peers)
    ]
    pl.when(zh == 1)(inner_pieces)
    early = [
        remote(bulk.at[my_y], bulk.at[my_y], bs_sem.at[o], br_sem.at[o], device)
        for o, device in enumerate(y_peers)
    ]

    def pick(choice, options):
        found = jnp.zeros_like(options[0])
        for i, option in enumerate(options):
            found = jnp.where(choice == i, option, found)
        return found

    for side in range(2):

        @pl.when(jnp.logical_not(has[side]))
        def _():
            xr[side] = jnp.ones((8, LANES), F32)
            x_in[side] = jnp.zeros((n_y, 2, 2, 128), F32)
            tables[1 + side] = jnp.full((SUB, 128), -1, I32)
            for peer in range(2):
                edge_in[side, peer] = jnp.zeros((4, 128), F32)

    for copy in sent:
        copy.wait_recv()

    px, kx, gx, dx = (
        [[xr[s, n + j : n + j + 1, :] for j in range(2)] for s in range(2)] for n in (0, 2, 4, 6)
    )

    def both(block):
        low, high = [yr[peer, CHUNKS * block : CHUNKS * block + CHUNKS] for peer in range(2)]
        return (
            jnp.where(lane3 < 64, low, pltpu.roll(high, 64, 2)),
            jnp.where(lane3 < 64, pltpu.roll(low, 64, 2), high),
        )

    py, ky = both(0)
    gy, dy = both(1)

    def rotated(quarters):
        return [quarters] + [pltpu.roll(quarters, 128 - 32 * q, 2) for q in range(1, 4)]

    def own_faces(field):
        low, high = y_faces(field)
        return [[low[a], high[a]] for a in range(2)]

    def into_quarters(faces, keys):
        total = jnp.zeros((CHUNKS, SUB, 128), F32)
        for a in range(2):
            for direction in range(2):
                face = jnp.where(lane3 < 32, faces[a][direction], 0.0)
                face = face + pltpu.roll(face, 32, 2)
                face = face + pltpu.roll(face, 64, 2)
                total = total + jnp.where(quarter3 == keys[a][direction], face, 0.0)
        return total

    k_faces, u_faces = own_faces(perm), own_faces(u0)
    k_turned, u_turned = rotated(ky), rotated(py)

    def add_y(ref, a, direction, value):
        if direction == 0:
            ref[a, :, :, 0:128] += value
        else:
            ref[a, :, :, LAST:LANES] += pltpu.roll(value, 96, 2)

    def add_x(ref, a, side, value):
        if side == 0:
            ref[a, 0, 0:1, :] += value
        else:
            ref[a, CHUNKS - 1, SUB - 1 : SUB, :] += value

    for a in range(2):
        for side in range(2):
            w = harmonic(x_face(perm, side, a), pick(ds[a, side], kx[side]))
            wxe[side, a : a + 1, :] = w
            add_x(dg, a, side, w)
            add_x(g, a, side, w * pick(ds[a, side], px[side]))
        for direction in range(2):
            kg = pick(codes[a][direction], k_turned)
            w = jnp.where(lane3 < 32, harmonic(k_faces[a][direction], kg), 0.0)
            wye[a, direction] = w
            add_y(dg, a, direction, w)
            add_y(g, a, direction, w * pick(codes[a][direction], u_turned))

    def line(packed, start, target):
        return pltpu.roll(packed, (target - start) % 4 * 32, 1) if start != target else packed

    px1 = []
    for side in range(2):
        found = []
        for j in range(2):
            gsum, dsum = gx[side][j], dx[side][j]
            mine_p = jnp.zeros((1, LANES), F32)
            mine_k = jnp.zeros((1, LANES), F32)
            for a in range(2):
                linked = ds[a, side] == j
                mine_p = jnp.where(linked, x_face(u0, side, a), mine_p)
                mine_k = jnp.where(linked, x_face(perm, side, a), mine_k)
            w = harmonic(kx[side][j], mine_k)
            gsum = gsum + w * mine_p
            dsum = dsum + w
            ends = []
            for direction in range(2):
                code = tables[1 + side, 2 + 2 * j + direction : 3 + 2 * j + direction, :]
                start = 2 if direction == 0 else 0
                target = 0 if direction == 0 else 3
                values = []
                for f in range(2):
                    options = [
                        line(edge_in[side, peer, f : f + 1, :], start + c, target)
                        for peer in range(2)
                        for c in range(2)
                    ]
                    values.append(pick(code, options))
                kk = kx[side][j][:, 0:128] if direction == 0 else kx[side][j][:, LAST:LANES]
                w = jnp.where(quarter1 == target, harmonic(kk, values[1]), 0.0)
                ends.append((w, w * values[0]))
            gap = jnp.zeros((1, LANES - 256), F32)
            dsum = dsum + jnp.concatenate([ends[0][0], gap, ends[1][0]], axis=1)
            gsum = gsum + jnp.concatenate([ends[0][1], gap, ends[1][1]], axis=1)
            found.append((1.0 - OMEGA) * px[side][j] + OMEGA * gsum / dsum)
        px1.append(found)

    mine_k = into_quarters(k_faces, codes)
    w = harmonic(ky, mine_k)
    gy = gy + w * into_quarters(u_faces, codes)
    dy = dy + w
    slots = []
    for peer in range(2):
        held = yr[peer, 2 * CHUNKS]
        for c in range(2):
            slots.append(jnp.where(minus[peer], held[6 + c : 7 + c, :], held[4 + c : 5 + c, :]))
    rows3 = lax.broadcasted_iota(I32, (CHUNKS, SUB, 128), 0) * SUB + lax.broadcasted_iota(
        I32, (CHUNKS, SUB, 128), 1
    )
    for side in range(2):
        values = []
        for f in range(2):
            total = jnp.zeros((1, 128), F32)
            for q in range(4):
                peer = q // 2
                held = yr[peer, 2 * CHUNKS]
                link = jnp.where(
                    slots[q] == 1, held[2 + side : 3 + side, :], held[side : side + 1, :]
                )
                edge = edge_in[side, peer, 2 + f : 3 + f, :]
                options = [
                    jnp.where(minus[peer], line(edge, 2 * s + 1, q), line(edge, 2 * s, q))
                    for s in range(2)
                ]
                total = jnp.where(quarter1 == q, pick(link, options), total)
            values.append(total)
        r = 0 if side == 0 else CHUNKS * SUB - 1
        here = ky[0, 0:1, :] if side == 0 else ky[CHUNKS - 1, SUB - 1 : SUB, :]
        w = harmonic(here, values[1])
        dy = dy + jnp.where(rows3 == r, w.reshape(1, 1, 128), 0.0)
        gy = gy + jnp.where(rows3 == r, (w * values[0]).reshape(1, 1, 128), 0.0)
    py1 = (1.0 - OMEGA) * py + OMEGA * gy / dy

    def first_update(k, _):
        for a in range(2):
            i = OMEGA / dg[a, k]
            inv[a, k] = i
            u1[a, k] = (1.0 - OMEGA) * u0[a, k] + i * g[a, k]
        return 0

    lax.fori_loop(0, CHUNKS, first_update, 0)
    u_turned = rotated(py1)
    y_flow = [
        [wye[a, direction] * pick(codes[a][direction], u_turned) for direction in range(2)]
        for a in range(2)
    ]
    x_flow = [[wxe[side, a : a + 1, :] * pick(ds[a, side], px1[side]) for side in range(2)] for a in range(2)]

    def second_update(chunks):
        for k in chunks:
            for a in range(2):
                g[a, k, :, 0:128] += y_flow[a][0][k]
                g[a, k, :, LAST:LANES] += pltpu.roll(y_flow[a][1][k], 96, 1)
                u2[a, k] = (1.0 - OMEGA) * u1[a, k] + inv[a, k] * g[a, k]

    neighbour_sum(u1, g, 0, CHUNKS - 1, 2)
    for a in range(2):
        for side in range(2):
            add_x(g, a, side, x_flow[a][side])
    second_update((0, CHUNKS - 1))
    across = []
    for side in range(2):
        flows = [wxe[side, a : a + 1, :] * x_face(u2, side, a) for a in range(2)]
        for s in range(2):
            total = jnp.zeros((1, LANES), F32)
            for a in range(2):
                total = total + jnp.where(ds[a, side] == s, flows[a], 0.0)
            across.append(total)
    across = jnp.concatenate(across, axis=0)
    crossing = jnp.dot(
        jnp.concatenate([across[:, 0:512], across[:, 512:1024]], axis=0), pool[...],
        preferred_element_type=F32, precision=lax.Precision.HIGHEST,
    )
    for side in range(2):
        for t in range(2):
            x_out[side, t] = crossing[4 * t + 2 * side : 4 * t + 2 * side + 2, :]
    spread = []
    for side in range(2):
        for o, device in enumerate(x_peers[side]):
            n = side * n_y + o
            spread.append(
                Link(x_out.at[side], x_in.at[1 - side, my_y], xs_sem.at[n], xr_sem.at[n], device, side)
            )
    neighbour_sum(u1, g, 1, 1, CHUNKS - 2)
    second_update(range(1, CHUNKS - 1))
    store = pltpu.make_async_copy(u2, out_hbm, out_sem.at[0])
    store.start()
    neighbour_sum(u2, g)

    pooled = pooled_residual(u2, g)
    lane2 = lax.broadcasted_iota(I32, (16, 128), 1)
    edges = jnp.zeros((16, 128), F32)
    for a in range(2):
        for t in range(2):
            part = piece_of(pooled, a, t)
            late[my_y, a, 4 * t : 4 * t + 2, :] = part[0:2, :]
            late[my_y, a, 4 * t + 2 : 4 * t + 4, :] = part[14:16, :]
            part = part if a == t else pltpu.roll(part, 64, 1)
            edges = jnp.where(lane2 // 32 == 2 * a + t, part, edges)
    late[my_y, 2:4] = edges.reshape(2, SUB, 128)
    u_faces = own_faces(u2)
    for direction in range(2):
        total = jnp.zeros((CHUNKS, SUB, 128), F32)
        for a in range(2):
            face = wye[a, direction] * u_faces[a][direction]
            face = face + pltpu.roll(face, 32, 2)
            face = face + pltpu.roll(face, 64, 2)
            code = codes[a][direction]
            slot = pick(code, slots)
            key = jnp.where(code >= 2, 2.0, 0.0) + slot
            hit = (quarter1.astype(F32) == key) & (code >= 0)
            total = total + jnp.where(hit.reshape(1, 1, 128), face, 0.0)
        face_sum[direction] = total.reshape(CHUNKS * SUB, 128)
    halves = [
        face_sum[direction, pl.ds(first, 16, stride=2), :] for direction in range(2) for first in range(2)
    ]
    faces = jnp.dot(
        halves[0] + halves[1] + halves[2] + halves[3], pool_face[...],
        preferred_element_type=F32, precision=lax.Precision.HIGHEST,
    )
    late[my_y, 4] = jnp.where(lane2[0:8] < 64, faces[0:8], pltpu.roll(faces[8:16], 64, 1))

    spread += [
        remote(late.at[my_y], late.at[my_y], gs_sem.at[o], gr_sem.at[o], device)
        for o, device in enumerate(y_peers)
    ]
    for copy in wants + early:
        copy.wait_recv()

    def device_at(y):
        return (y * 2 + zh) * 2 + core

    def iota(shape, dim):
        return lax.broadcasted_iota(I32, shape, dim)

    bulk_shape = (n_y, 2, 4, SUB, 128)
    bulk_id = device_at(iota(bulk_shape, 0)) * 2 + iota(bulk_shape, 1)

    def want(holder, j):
        return tables[holder, j : j + 1, :]

    holders = (0, 3, 4, 5)
    for h, holder in ((2, 3), (3, 5), (1, 4), (0, 0)):
        held = bulk[:, 0:8].reshape(bulk_shape)
        for j in range(2):
            w = want(holder, j).reshape(1, 1, 1, 1, 128)
            bulk_out[h, 4 * j : 4 * j + 4] = jnp.sum(jnp.where(bulk_id == w, held, 0.0), axis=(0, 1))
        if h == 3:
            to_core = remote(
                bulk_out.at[pl.ds(2, 2)], bulk_in.at[pl.ds(0, 2)], es_sem.at[0], er_sem.at[0], row_peers[0]
            )
    to_core.wait_recv()
    bulk_out[1] += bulk_in[1]
    rows_of_bulk = [
        to_core, remote(bulk_out.at[1], bulk_in.at[2], es_sem.at[1], er_sem.at[1], row_peers[1])
    ]

    for copy in spread:
        copy.wait_recv()

    a_shape = (n_y, 2, SUB, 128)
    a_id = device_at(iota(a_shape, 0)) * 2 + iota(a_shape, 1)
    b_id = device_at(iota(a_shape, 0)) * 2 + iota(a_shape, 3) // 64
    x_shape = (n_y, 2, 128)
    x_id = device_at(iota(x_shape, 0)) * 2 + iota(x_shape, 1)
    y_shape = (n_y, SUB, 128)
    y_lane = iota(y_shape, 2)
    y_id = (device_at(iota(y_shape, 0)) + 2 * (y_lane // 32 % 2) - 1) * 2 + y_lane // 16 % 2
    row8 = iota((SUB, 128), 0)
    lane8 = iota((SUB, 128), 1)

    def shell(holder, j):
        w2 = want(holder, j)
        w3, w4 = w2.reshape(1, 1, 128), w2.reshape(1, 1, 1, 128)
        rows = jnp.sum(jnp.where(a_id == w4, late[:, 0:2], 0.0), axis=(0, 1))
        edges = jnp.sum(jnp.where(b_id == w4, late[:, 2:4], 0.0), axis=0)
        halves = [edges[n] + pltpu.roll(edges[n], 64, 1) for n in range(2)]
        for side in range(2):
            line = [
                jnp.sum(jnp.where(x_id == w3, x_in[side, :, t], 0.0), axis=(0, 1)).reshape(1, 128)
                for t in range(2)
            ]
            for t in range(2):
                rows = rows + jnp.where(row8 == 4 * t + 3 * side, line[t], 0.0)
            both_ends = jnp.where(lane8 < 32, line[0], pltpu.roll(line[1], 64, 1))
            halves[side] = halves[side] + jnp.where(row8 == 7 * side, both_ends, 0.0)
        found = jnp.where(y_id == w3, late[:, 4], 0.0)
        for f in range(2):
            part = jnp.sum(jnp.where(bulk[:, 8] == f, found, 0.0), axis=0)
            part = part + pltpu.roll(part, 112, 1)
            part = part + pltpu.roll(part, 96, 1)
            spot = lane8 // 16 == 3 * f
            for n in range(2):
                turn = (48 * f + 64 * n) % 128
                moved = pltpu.roll(part, turn, 1) if turn else part
                halves[n] = halves[n] + jnp.where(spot, moved, 0.0)
        return rows, halves

    rows_of_shells = []
    for h in (3, 2, 1, 0):
        one, two = shell(holders[h], 0), shell(holders[h], 1)
        shell_out[h, 0] = one[0]
        shell_out[h, 1] = two[0]
        for n in range(2):
            shell_out[h, 2 + n] = jnp.where(lane8 < 64, one[1][n], pltpu.roll(two[1][n], 64, 1))
        if h:
            rows_of_shells.append(
                remote(
                    shell_out.at[h], shell_in.at[h - 1], es_sem.at[2 + h], er_sem.at[2 + h],
                    row_peers[h - 1],
                )
            )
    rows_of_bulk[1].wait_recv()
    inner = bulk_out[0] + bulk_in[0] + bulk_in[2]
    for copy in rows_of_shells:
        copy.wait_recv()
    outer = shell_out[0] + shell_in[0] + shell_in[1] + shell_in[2]
    for j in range(2):
        rows = outer[j]
        turned = pltpu.roll(rows, 4, 0)
        for n in range(2):
            edges = outer[2 + n] if j == 0 else pltpu.roll(outer[2 + n], 64, 1)
            for t in range(2):
                line = rows if t == n else turned
                found = jnp.where(row8 < 2 if n == 0 else row8 >= 6, line, inner[4 * j + 2 * t + n])
                if t == 0:
                    found = jnp.where(lane8 < 32, edges, found)
                else:
                    found = jnp.where(lane8 >= 96, pltpu.roll(edges, 64, 1), found)
                coarse[j, SUB * n : SUB * n + SUB, 128 * t : 128 * t + 128] = found
    last = pltpu.make_async_copy(coarse, coarse_hbm, out_sem.at[1])
    last.start()
    for copy in sent + wants + early + spread + rows_of_bulk + rows_of_shells:
        copy.wait_send()
    store.wait()
    last.wait()


def body(pressure, source, perm, brinkman, depth_source, sideways, edge_blocks, restrict_take):
    big = (2, CHUNKS, SUB, LANES)
    n_y = lax.axis_size("inslab") // 4
    vm = lambda *shape: pltpu.VMEM(shape, F32)
    dma = lambda n: pltpu.SemaphoreType.DMA((n,))
    anywhere = pl.BlockSpec(memory_space=pltpu.HBM)
    arrays = [x.reshape(big) for x in (pressure, source, perm)]
    arrays += [brinkman, depth_source, sideways, edge_blocks, restrict_take]
    smoothed, coarse = pl.pallas_call(
        kernel,
        out_shape=(
            jax.ShapeDtypeStruct(big, F32),
            jax.ShapeDtypeStruct((2, 16, 256), F32),
        ),
        in_specs=[anywhere] * 8,
        out_specs=(anywhere, anywhere),
        scratch_shapes=[
            pltpu.SMEM((2,), F32), pltpu.SMEM((2, 2), I32), pltpu.SMEM((2, 4), I32),
            pltpu.SMEM((1, 2, 2), I32), pltpu.SMEM((2,), I32),
        ]
        + [vm(*big) for _ in range(15)]
        + [
            vm(2, 2, LANES), vm(2, 2, CHUNKS, SUB, 128), vm(8, 64, 128), vm(512, 128), vm(128, 128),
            vm(2, 8, LANES), vm(2, 8, LANES),
            vm(2, 2 * CHUNKS + 1, SUB, 128), vm(2, 2 * CHUNKS + 1, SUB, 128),
            vm(2, 4, 128), vm(2, 2, 4, 128),
            pltpu.VMEM((6, SUB, 128), I32),
            vm(2, CHUNKS * SUB, 128),
            vm(n_y, 9, SUB, 128), vm(n_y, 5, SUB, 128), vm(2, 2, 2, 128), vm(2, n_y, 2, 2, 128),
            vm(4, 8, SUB, 128), vm(3, 8, SUB, 128), vm(4, 4, SUB, 128), vm(3, 4, SUB, 128), vm(2, 16, 256),
            dma(8), dma(2), dma(8), dma(8), dma(5), dma(5), dma(n_y - 1), dma(n_y - 1),
            dma(n_y - 1), dma(n_y - 1), dma(2 * n_y), dma(2 * n_y), dma(6), dma(6),
        ],
        compiler_params=pltpu.CompilerParams(
            collective_id=0, has_side_effects=True, vmem_limit_bytes=32 * 1024 * 1024
        ),
    )(*[pltpu.with_memory_space_constraint(x, pltpu.HBM) for x in arrays])
    return smoothed.reshape(pressure.shape), coarse


def solution(mesh):
    group = ("depth", "inslab")
    return jax.shard_map(
        body,
        mesh=mesh,
        in_specs=(
            P(group, None, None),
            P(group, None, None),
            P(group, None, None),
            P(group),
            P(group, None),
            P(group, None),
            P(group, None, None),
            P(group),
        ),
        out_specs=(P(group, None, None), P(group, None, None)),
        check_vma=False,
    )
```

```python
import jax
import jax.numpy as jnp
from jax import lax
from jax.experimental import pallas as pl
from jax.experimental.pallas import tpu as pltpu
from jax.sharding import PartitionSpec as P

OMEGA = 0.8
MESH = pl.DeviceIdType.MESH
F32 = jnp.float32
I32 = jnp.int32
CHUNKS, SUB, LANES = 4, 8, 1024
LAST = LANES - 128


def harmonic(a, b):
    return 2.0 * a * b / (a + b)


def kernel(
    p_hbm, s_hbm, k_hbm, brink_hbm, ds_hbm, snt_hbm, eb_hbm, take_hbm,
    out_hbm, coarse_hbm,
    brink, ds, snt, eb, take,
    u0, src, perm, u1, u2, g, ga, dg, inv, wxm, wxp, wym, wyp, wzm, wzp,
    wxe, wye, res, pool, pool_face,
    xs, xr, ys, yr, edge_out, edge_in,
    tables, face_sum, bulk, late, x_out, x_in, bulk_out, bulk_in, shell_out, shell_in, coarse,
    in_sem, out_sem, hs_sem, hr_sem, ts_sem, tr_sem, bs_sem, br_sem, gs_sem, gr_sem, xs_sem, xr_sem, es_sem, er_sem,
):
    depth = lax.axis_index("depth")
    me = lax.axis_index("inslab")
    n_depth = lax.axis_size("depth")
    n_in = lax.axis_size("inslab")
    n_y = n_in // 4
    my_y = me // 4
    zh = (me // 2) % 2
    core = me % 2

    def at(d, y, z, c):
        return (d, (y * 2 + z) * 2 + c)

    deeper = [lax.rem(depth + n_depth - 1, n_depth), lax.rem(depth + 1, n_depth)]
    beside_me = [lax.rem(me + n_in - 1, n_in), lax.rem(me + 1, n_in)]
    row_peers = [
        at(depth, my_y, zh, 1 - core), at(depth, my_y, 1 - zh, core), at(depth, my_y, 1 - zh, 1 - core)
    ]
    y_peers = [at(depth, lax.rem(my_y + o, n_y), zh, core) for o in range(1, n_y)]
    x_peers = [
        [at(deeper[side], lax.rem(my_y + o, n_y), zh, core) for o in range(n_y)] for side in range(2)
    ]
    i_peers = [(depth, m) for m in beside_me]
    d_peers = [(d, me) for d in deeper]
    corners = [[(d, m) for m in beside_me] for d in deeper]

    has = [depth > 0, depth < n_depth - 1]

    barrier = pltpu.get_barrier_semaphore()

    def greet(partner):
        pl.semaphore_signal(barrier, inc=1, device_id=partner, device_id_type=MESH)

    always = i_peers + row_peers + y_peers
    for partner in always:
        greet(partner)
    for side in range(2):
        pl.when(has[side])(lambda side=side: [greet(p) for p in [d_peers[side]] + corners[side]] and None)
    greeted = len(always) + sum(jnp.where(has[side], 1 + len(corners[side]), 0) for side in range(2))

    small = [(snt_hbm, snt), (ds_hbm, ds), (eb_hbm, eb), (take_hbm, take), (brink_hbm, brink)]
    loads = [
        pltpu.make_async_copy(h, v, in_sem.at[i])
        for i, (h, v) in enumerate([(k_hbm, perm), (p_hbm, u0), (s_hbm, src)] + small)
    ]
    for load in loads:
        load.start()
    for load in loads[3:]:
        load.wait()

    lane3 = lax.broadcasted_iota(I32, (CHUNKS, SUB, 128), 2)
    lane1 = lax.broadcasted_iota(I32, (1, 128), 1)
    row = lax.broadcasted_iota(I32, (SUB, LANES), 0)
    lane = lax.broadcasted_iota(I32, (SUB, LANES), 1)
    zpos = lane % 32
    quarter3 = lane3 // 32
    quarter1 = lane1 // 32

    def remote(a, b, s, r, device):
        copy = pltpu.make_async_remote_copy(
            src_ref=a, dst_ref=b, send_sem=s, recv_sem=r, device_id=device, device_id_type=MESH
        )
        copy.start()
        return copy

    class Link:
        def __init__(self, a, b, s, r, device, side):
            self.args, self.side = (a, b, s, r, device), side
            pl.when(has[side])(lambda: self.make().start())

        def make(self):
            a, b, s, r, device = self.args
            return pltpu.make_async_remote_copy(
                src_ref=a, dst_ref=b, send_sem=s, recv_sem=r, device_id=device, device_id_type=MESH
            )

        def wait_recv(self):
            pl.when(has[1 - self.side])(lambda: self.make().wait_recv())

        def wait_send(self):
            pl.when(has[self.side])(lambda: self.make().wait_send())

    def lies_minus(low):
        found = []
        for a in range(2):
            w = snt[a, 0]
            below = w - 2 < 2 * me
            found.append((w >= 2) & (below if low else jnp.logical_not(below)))
        return found[0] | found[1]

    minus = [lies_minus(True), lies_minus(False)]

    def quarter_of(a, direction):
        w = snt[a, direction]
        column = w & 1
        q = jnp.where(w - 2 < 2 * me, column, 2 + column)
        return jnp.where(w >= 2, q, -1)

    codes = [[quarter_of(a, direction) for direction in range(2)] for a in range(2)]

    trow = lax.broadcasted_iota(I32, (SUB, 128), 0)

    def as_rows(entries):
        tile = jnp.zeros((SUB, 128), I32)
        for i, value in enumerate(entries):
            tile = jnp.where(trow == i, value, tile)
        return tile

    tables[0] = as_rows([take[0], take[1]] + [codes[a][s] for a in range(2) for s in range(2)])
    links = as_rows(
        [ds[a, s] for a in range(2) for s in range(2)]
        + [eb[0, s, c] for s in range(2) for c in range(2)]
    ).astype(F32)

    def y_faces(field):
        low = [field[a, :, :, 0:128] for a in range(2)]
        high = [pltpu.roll(field[a, :, :, LAST:LANES], 32, 2) for a in range(2)]
        return low, high

    def pair_for(faces, is_minus):
        low, high = faces
        cols = []
        for c in range(2):
            from_low = jnp.where(eb[0, 0, c] == 1, low[1], low[0])
            from_high = jnp.where(eb[0, 1, c] == 1, high[1], high[0])
            cols.append(jnp.where(is_minus, from_low, from_high))
        return jnp.where(lane3 < 32, cols[0], pltpu.roll(cols[1], 32, 2))

    def x_face(field, side, a):
        if side == 0:
            return field[a, 0, 0:1, :]
        return field[a, CHUNKS - 1, SUB - 1 : SUB, :]

    def fill(first, second, block):
        for side in range(2):
            for a in range(2):
                n = 4 * block + a
                xs[side, n : n + 1, :] = x_face(first, side, a)
                xs[side, n + 2 : n + 3, :] = x_face(second, side, a)
        one, two = y_faces(first), y_faces(second)
        for peer in range(2):
            ys[peer, CHUNKS * block : CHUNKS * block + CHUNKS] = jnp.where(
                lane3 < 64, pair_for(one, minus[peer]), pltpu.roll(pair_for(two, minus[peer]), 64, 2)
            )

    loads[0].wait()
    loads[1].wait()
    fill(u0, perm, 0)
    for peer in range(2):
        ys[peer, 2 * CHUNKS] = links
    for side in range(2):
        for f, field in enumerate((u0, perm)):
            lines = []
            for a in range(2):
                face = x_face(field, side, a)
                lines.append([face[:, 0:128], pltpu.roll(face[:, LAST:LANES], 32, 1)])
            by_column = [
                jnp.where(eb[0, s, c] == 1, lines[1][s], lines[0][s]) for s in range(2) for c in range(2)
            ]
            by_slot = [lines[a][s] for a in range(2) for s in range(2)]
            for n, listed in enumerate((by_column, by_slot)):
                packed = listed[0]
                for q in range(1, 4):
                    packed = jnp.where(quarter1 == q, pltpu.roll(listed[q], 32 * q, 1), packed)
                edge_out[side, 2 * n + f : 2 * n + f + 1, :] = packed
    def zslot(a, direction):
        return jnp.maximum(snt[a, 2 + direction], 0)

    def beside(field, a, k):
        u = field[a, k]
        before = field[a, jnp.maximum(k - 1, 0), SUB - 1 : SUB, :]
        after = field[a, jnp.minimum(k + 1, CHUNKS - 1), 0:1, :]
        um = jnp.where(row == 0, before, pltpu.roll(u, 1, 0))
        up = jnp.where(row == SUB - 1, after, pltpu.roll(u, SUB - 1, 0))
        ym = pltpu.roll(u, 32, 1)
        yp = pltpu.roll(u, LANES - 32, 1)
        nm = field[zslot(a, 0), k]
        np_ = field[zslot(a, 1), k]
        zm = jnp.where(zpos == 0, pltpu.roll(nm, LANES - 31, 1), pltpu.roll(u, 1, 1))
        zp = jnp.where(zpos == 31, pltpu.roll(np_, 31, 1), pltpu.roll(u, LANES - 1, 1))
        return u, (um, up, ym, yp, zm, zp)

    def weights(k, _):
        for a in range(2):
            kk, nbs = beside(perm, a, k)
            has_zm = snt[a, 2] >= 0
            has_zp = snt[a, 3] >= 0
            keep = (
                jnp.logical_not((row == 0) & (k == 0)),
                jnp.logical_not((row == SUB - 1) & (k == CHUNKS - 1)),
                lane >= 32,
                lane < LANES - 32,
                jnp.logical_or(zpos != 0, has_zm),
                jnp.logical_or(zpos != 31, has_zp),
            )
            total = jnp.full((SUB, LANES), brink[a], F32)
            for store, nb, mask in zip((wxm, wxp, wym, wyp, wzm, wzp), nbs, keep):
                w = jnp.where(mask, harmonic(kk, nb), 0.0)
                store[a, k] = w
                total = total + w
            dg[a, k] = total
        return 0

    lax.fori_loop(0, CHUNKS, weights, 0)
    loads[2].wait()

    def neighbour_sum(field, into, first=0, stride=1, count=CHUNKS):
        def step(n, _):
            k = first + stride * n
            for a in range(2):
                _, nbs = beside(field, a, k)
                total = src[a, k]
                for store, nb in zip((wxm, wxp, wym, wyp, wzm, wzp), nbs):
                    total = total + store[a, k] * nb
                into[a, k] = total
            return 0

        lax.fori_loop(0, count, step, 0)

    outer_tiles = ((0, 0), (LANES - 256, 128))

    def edge_sum(field, into):
        def step(n, _):
            k = 1 + n
            for a in range(2):
                for start, kept in outer_tiles:
                    part = slice(start, start + 256)
                    u = field[a, k, :, part]
                    nm = field[zslot(a, 0), k, :, part]
                    np_ = field[zslot(a, 1), k, :, part]
                    before = field[a, k - 1, SUB - 1 : SUB, part]
                    after = field[a, k + 1, 0:1, part]
                    nbs = (
                        jnp.where(row[:, 0:256] == 0, before, pltpu.roll(u, 1, 0)),
                        jnp.where(row[:, 0:256] == SUB - 1, after, pltpu.roll(u, SUB - 1, 0)),
                        pltpu.roll(u, 32, 1),
                        pltpu.roll(u, 224, 1),
                        jnp.where(zpos[:, 0:256] == 0, pltpu.roll(nm, 225, 1), pltpu.roll(u, 1, 1)),
                        jnp.where(zpos[:, 0:256] == 31, pltpu.roll(np_, 31, 1), pltpu.roll(u, 255, 1)),
                    )
                    total = src[a, k, :, part]
                    for store, nb in zip((wxm, wxp, wym, wyp, wzm, wzp), nbs):
                        total = total + store[a, k, :, part] * nb
                    into[a, k, :, start + kept : start + kept + 128] = total[:, kept : kept + 128]
            return 0

        lax.fori_loop(0, CHUNKS - 2, step, 0)

    neighbour_sum(u0, g)
    fill(g, dg, 1)

    prow = lax.broadcasted_iota(I32, (512, 128), 0)
    pcol = lax.broadcasted_iota(I32, (512, 128), 1)
    pool[...] = 0.125 * ((prow // 64) * 16 + (prow % 32) // 2 == pcol).astype(F32)
    frow = lax.broadcasted_iota(I32, (128, 128), 0)
    fcol = lax.broadcasted_iota(I32, (128, 128), 1)
    pool_face[...] = 0.125 * (frow // 32 * 16 + (frow % 32) // 2 == fcol).astype(F32)

    def pooled_residual(field, sums):
        def step(k, _):
            for a in range(2):
                at_row = pl.multiple_of(a * 32 + k * SUB, SUB)
                r = sums[a, k] - dg[a, k] * field[a, k]
                for t in range(8):
                    res[t, pl.ds(at_row, SUB), :] = r[:, 128 * t : 128 * t + 128]
            return 0

        lax.fori_loop(0, CHUNKS, step, 0)
        paired = [
            res[t, pl.ds(0, 32, stride=2), :] + res[t, pl.ds(1, 32, stride=2), :] for t in range(8)
        ]
        stacked = [jnp.concatenate(paired[4 * h : 4 * h + 4], axis=1) for h in range(2)]
        return jnp.dot(
            jnp.concatenate(stacked, axis=0), pool[...],
            preferred_element_type=F32, precision=lax.Precision.HIGHEST,
        )

    def piece_of(pooled, a, t):
        return pooled[32 * t + 16 * a : 32 * t + 16 * a + 16, :]

    def inner_first(k, _):
        for a in range(2):
            i = OMEGA / dg[a, k]
            inv[a, k] = i
            u1[a, k] = (1.0 - OMEGA) * u0[a, k] + i * g[a, k]
        return 0

    def inner_second(k, _):
        for a in range(2):
            u2[a, k] = (1.0 - OMEGA) * u1[a, k] + inv[a, k] * ga[a, k]
        return 0

    def inner_pieces():
        lax.fori_loop(0, CHUNKS, inner_first, 0)
        neighbour_sum(u1, ga)
        lax.fori_loop(0, CHUNKS, inner_second, 0)
        neighbour_sum(u2, ga)
        pooled = pooled_residual(u2, ga)
        for a in range(2):
            for t in range(2):
                n = 4 * a + 2 * t
                bulk[my_y, n : n + 2] = piece_of(pooled, a, t).reshape(2, SUB, 128)
        sides = jnp.where(quarter1 % 2 == 0, minus[0].astype(F32), minus[1].astype(F32))
        bulk[my_y, 8] = jnp.broadcast_to(sides, (SUB, 128))

    pl.when(zh == 0)(inner_pieces)
    pl.semaphore_wait(barrier, greeted)
    sent = []
    for peer in range(2):
        sent.append(remote(ys.at[peer], yr.at[1 - peer], hs_sem.at[peer], hr_sem.at[peer], i_peers[peer]))
    for side in range(2):
        for peer in range(2):
            n = 4 + 2 * side + peer
            sent.append(
                Link(
                    edge_out.at[side], edge_in.at[1 - side, 1 - peer],
                    hs_sem.at[n], hr_sem.at[n], corners[side][peer], side,
                )
            )
    for side in range(2):
        n = 2 + side
        sent.append(
            Link(xs.at[side], xr.at[1 - side], hs_sem.at[n], hr_sem.at[n], d_peers[side], side)
        )
        sent.append(
            Link(
                tables.at[0], tables.at[2 - side], ts_sem.at[side], tr_sem.at[side], d_peers[side], side
            )
        )
    wants = [
        remote(tables.at[0], tables.at[3 + j], ts_sem.at[2 + j], tr_sem.at[2 + j], device)
        for j, device in enumerate(row_peers)
    ]
    pl.when(zh == 1)(inner_pieces)
    early = [
        remote(bulk.at[my_y], bulk.at[my_y], bs_sem.at[o], br_sem.at[o], device)
        for o, device in enumerate(y_peers)
    ]

    def pick(choice, options):
        found = jnp.zeros_like(options[0])
        for i, option in enumerate(options):
            found = jnp.where(choice == i, option, found)
        return found

    for side in range(2):

        @pl.when(jnp.logical_not(has[side]))
        def _():
            xr[side] = jnp.ones((8, LANES), F32)
            x_in[side] = jnp.zeros((n_y, 2, 2, 128), F32)
            tables[1 + side] = jnp.full((SUB, 128), -1, I32)
            for peer in range(2):
                edge_in[side, peer] = jnp.zeros((4, 128), F32)

    for copy in sent:
        copy.wait_recv()

    px, kx, gx, dx = (
        [[xr[s, n + j : n + j + 1, :] for j in range(2)] for s in range(2)] for n in (0, 2, 4, 6)
    )

    def both(block):
        low, high = [yr[peer, CHUNKS * block : CHUNKS * block + CHUNKS] for peer in range(2)]
        return (
            jnp.where(lane3 < 64, low, pltpu.roll(high, 64, 2)),
            jnp.where(lane3 < 64, pltpu.roll(low, 64, 2), high),
        )

    py, ky = both(0)
    gy, dy = both(1)

    def rotated(quarters):
        return [quarters] + [pltpu.roll(quarters, 128 - 32 * q, 2) for q in range(1, 4)]

    def own_faces(field):
        low, high = y_faces(field)
        return [[low[a], high[a]] for a in range(2)]

    def into_quarters(faces, keys):
        total = jnp.zeros((CHUNKS, SUB, 128), F32)
        for a in range(2):
            for direction in range(2):
                face = jnp.where(lane3 < 32, faces[a][direction], 0.0)
                face = face + pltpu.roll(face, 32, 2)
                face = face + pltpu.roll(face, 64, 2)
                total = total + jnp.where(quarter3 == keys[a][direction], face, 0.0)
        return total

    k_faces, u_faces = own_faces(perm), own_faces(u0)
    k_turned, u_turned = rotated(ky), rotated(py)

    def add_y(ref, a, direction, value):
        if direction == 0:
            ref[a, :, :, 0:128] += value
        else:
            ref[a, :, :, LAST:LANES] += pltpu.roll(value, 96, 2)

    def add_x(ref, a, side, value):
        if side == 0:
            ref[a, 0, 0:1, :] += value
        else:
            ref[a, CHUNKS - 1, SUB - 1 : SUB, :] += value

    for a in range(2):
        for side in range(2):
            w = harmonic(x_face(perm, side, a), pick(ds[a, side], kx[side]))
            wxe[side, a : a + 1, :] = w
            add_x(dg, a, side, w)
            add_x(g, a, side, w * pick(ds[a, side], px[side]))
        for direction in range(2):
            kg = pick(codes[a][direction], k_turned)
            w = jnp.where(lane3 < 32, harmonic(k_faces[a][direction], kg), 0.0)
            wye[a, direction] = w
            add_y(dg, a, direction, w)
            add_y(g, a, direction, w * pick(codes[a][direction], u_turned))

    def line(packed, start, target):
        return pltpu.roll(packed, (target - start) % 4 * 32, 1) if start != target else packed

    px1 = []
    for side in range(2):
        found = []
        for j in range(2):
            gsum, dsum = gx[side][j], dx[side][j]
            mine_p = jnp.zeros((1, LANES), F32)
            mine_k = jnp.zeros((1, LANES), F32)
            for a in range(2):
                linked = ds[a, side] == j
                mine_p = jnp.where(linked, x_face(u0, side, a), mine_p)
                mine_k = jnp.where(linked, x_face(perm, side, a), mine_k)
            w = harmonic(kx[side][j], mine_k)
            gsum = gsum + w * mine_p
            dsum = dsum + w
            ends = []
            for direction in range(2):
                code = tables[1 + side, 2 + 2 * j + direction : 3 + 2 * j + direction, :]
                start = 2 if direction == 0 else 0
                target = 0 if direction == 0 else 3
                values = []
                for f in range(2):
                    options = [
                        line(edge_in[side, peer, f : f + 1, :], start + c, target)
                        for peer in range(2)
                        for c in range(2)
                    ]
                    values.append(pick(code, options))
                kk = kx[side][j][:, 0:128] if direction == 0 else kx[side][j][:, LAST:LANES]
                w = jnp.where(quarter1 == target, harmonic(kk, values[1]), 0.0)
                ends.append((w, w * values[0]))
            gap = jnp.zeros((1, LANES - 256), F32)
            dsum = dsum + jnp.concatenate([ends[0][0], gap, ends[1][0]], axis=1)
            gsum = gsum + jnp.concatenate([ends[0][1], gap, ends[1][1]], axis=1)
            found.append((1.0 - OMEGA) * px[side][j] + OMEGA * gsum / dsum)
        px1.append(found)

    mine_k = into_quarters(k_faces, codes)
    w = harmonic(ky, mine_k)
    gy = gy + w * into_quarters(u_faces, codes)
    dy = dy + w
    slots = []
    for peer in range(2):
        held = yr[peer, 2 * CHUNKS]
        for c in range(2):
            slots.append(jnp.where(minus[peer], held[6 + c : 7 + c, :], held[4 + c : 5 + c, :]))
    rows3 = lax.broadcasted_iota(I32, (CHUNKS, SUB, 128), 0) * SUB + lax.broadcasted_iota(
        I32, (CHUNKS, SUB, 128), 1
    )
    for side in range(2):
        values = []
        for f in range(2):
            total = jnp.zeros((1, 128), F32)
            for q in range(4):
                peer = q // 2
                held = yr[peer, 2 * CHUNKS]
                link = jnp.where(
                    slots[q] == 1, held[2 + side : 3 + side, :], held[side : side + 1, :]
                )
                edge = edge_in[side, peer, 2 + f : 3 + f, :]
                options = [
                    jnp.where(minus[peer], line(edge, 2 * s + 1, q), line(edge, 2 * s, q))
                    for s in range(2)
                ]
                total = jnp.where(quarter1 == q, pick(link, options), total)
            values.append(total)
        r = 0 if side == 0 else CHUNKS * SUB - 1
        here = ky[0, 0:1, :] if side == 0 else ky[CHUNKS - 1, SUB - 1 : SUB, :]
        w = harmonic(here, values[1])
        dy = dy + jnp.where(rows3 == r, w.reshape(1, 1, 128), 0.0)
        gy = gy + jnp.where(rows3 == r, (w * values[0]).reshape(1, 1, 128), 0.0)
    py1 = (1.0 - OMEGA) * py + OMEGA * gy / dy

    whole = slice(0, LANES)
    parts = [(k, whole) for k in (0, CHUNKS - 1)]
    parts += [(k, part) for k in range(1, CHUNKS - 1) for part in (slice(0, 128), slice(LAST, LANES))]
    for k, part in parts:
        for a in range(2):
            i = OMEGA / dg[a, k, :, part]
            inv[a, k, :, part] = i
            u1[a, k, :, part] = (1.0 - OMEGA) * u0[a, k, :, part] + i * g[a, k, :, part]

    u_turned = rotated(py1)
    y_flow = [
        [wye[a, direction] * pick(codes[a][direction], u_turned) for direction in range(2)]
        for a in range(2)
    ]
    x_flow = [[wxe[side, a : a + 1, :] * pick(ds[a, side], px1[side]) for side in range(2)] for a in range(2)]

    def second_update(chosen):
        for k, part in chosen:
            for a in range(2):
                if part.start == 0:
                    g[a, k, :, 0:128] += y_flow[a][0][k]
                if part.stop == LANES:
                    g[a, k, :, LAST:LANES] += pltpu.roll(y_flow[a][1][k], 96, 1)
                u2[a, k, :, part] = (1.0 - OMEGA) * u1[a, k, :, part] + inv[a, k, :, part] * g[a, k, :, part]

    neighbour_sum(u1, g, 0, CHUNKS - 1, 2)
    for a in range(2):
        for side in range(2):
            add_x(g, a, side, x_flow[a][side])
    second_update(parts[0:2])
    across = []
    for side in range(2):
        flows = [wxe[side, a : a + 1, :] * x_face(u2, side, a) for a in range(2)]
        for s in range(2):
            total = jnp.zeros((1, LANES), F32)
            for a in range(2):
                total = total + jnp.where(ds[a, side] == s, flows[a], 0.0)
            across.append(total)
    across = jnp.concatenate(across, axis=0)
    crossing = jnp.dot(
        jnp.concatenate([across[:, 0:512], across[:, 512:1024]], axis=0), pool[...],
        preferred_element_type=F32, precision=lax.Precision.HIGHEST,
    )
    for side in range(2):
        for t in range(2):
            x_out[side, t] = crossing[4 * t + 2 * side : 4 * t + 2 * side + 2, :]
    spread = []
    for side in range(2):
        for o, device in enumerate(x_peers[side]):
            n = side * n_y + o
            spread.append(
                Link(x_out.at[side], x_in.at[1 - side, my_y], xs_sem.at[n], xr_sem.at[n], device, side)
            )
    edge_sum(u1, g)
    second_update(parts[2:])
    store = pltpu.make_async_copy(u2, out_hbm, out_sem.at[0])
    store.start()
    neighbour_sum(u2, g, 0, CHUNKS - 1, 2)
    edge_sum(u2, g)

    pooled = pooled_residual(u2, g)
    lane2 = lax.broadcasted_iota(I32, (16, 128), 1)
    edges = jnp.zeros((16, 128), F32)
    for a in range(2):
        for t in range(2):
            part = piece_of(pooled, a, t)
            late[my_y, a, 4 * t : 4 * t + 2, :] = part[0:2, :]
            late[my_y, a, 4 * t + 2 : 4 * t + 4, :] = part[14:16, :]
            part = part if a == t else pltpu.roll(part, 64, 1)
            edges = jnp.where(lane2 // 32 == 2 * a + t, part, edges)
    late[my_y, 2:4] = edges.reshape(2, SUB, 128)
    u_faces = own_faces(u2)
    for direction in range(2):
        total = jnp.zeros((CHUNKS, SUB, 128), F32)
        for a in range(2):
            face = wye[a, direction] * u_faces[a][direction]
            face = face + pltpu.roll(face, 32, 2)
            face = face + pltpu.roll(face, 64, 2)
            code = codes[a][direction]
            slot = pick(code, slots)
            key = jnp.where(code >= 2, 2.0, 0.0) + slot
            hit = (quarter1.astype(F32) == key) & (code >= 0)
            total = total + jnp.where(hit.reshape(1, 1, 128), face, 0.0)
        face_sum[direction] = total.reshape(CHUNKS * SUB, 128)
    halves = [
        face_sum[direction, pl.ds(first, 16, stride=2), :] for direction in range(2) for first in range(2)
    ]
    faces = jnp.dot(
        halves[0] + halves[1] + halves[2] + halves[3], pool_face[...],
        preferred_element_type=F32, precision=lax.Precision.HIGHEST,
    )
    late[my_y, 4] = jnp.where(lane2[0:8] < 64, faces[0:8], pltpu.roll(faces[8:16], 64, 1))

    spread += [
        remote(late.at[my_y], late.at[my_y], gs_sem.at[o], gr_sem.at[o], device)
        for o, device in enumerate(y_peers)
    ]
    for copy in wants + early:
        copy.wait_recv()

    def device_at(y):
        return (y * 2 + zh) * 2 + core

    def iota(shape, dim):
        return lax.broadcasted_iota(I32, shape, dim)

    bulk_shape = (n_y, 2, 4, SUB, 128)
    bulk_id = device_at(iota(bulk_shape, 0)) * 2 + iota(bulk_shape, 1)

    def want(holder, j):
        return tables[holder, j : j + 1, :]

    holders = (0, 3, 4, 5)
    for h, holder in ((2, 3), (3, 5), (1, 4), (0, 0)):
        held = bulk[:, 0:8].reshape(bulk_shape)
        for j in range(2):
            w = want(holder, j).reshape(1, 1, 1, 1, 128)
            bulk_out[h, 4 * j : 4 * j + 4] = jnp.sum(jnp.where(bulk_id == w, held, 0.0), axis=(0, 1))
        if h == 3:
            to_core = remote(
                bulk_out.at[pl.ds(2, 2)], bulk_in.at[pl.ds(0, 2)], es_sem.at[0], er_sem.at[0], row_peers[0]
            )
    to_core.wait_recv()
    bulk_out[1] += bulk_in[1]
    rows_of_bulk = [
        to_core, remote(bulk_out.at[1], bulk_in.at[2], es_sem.at[1], er_sem.at[1], row_peers[1])
    ]

    for copy in spread:
        copy.wait_recv()

    a_shape = (n_y, 2, SUB, 128)
    a_id = device_at(iota(a_shape, 0)) * 2 + iota(a_shape, 1)
    b_id = device_at(iota(a_shape, 0)) * 2 + iota(a_shape, 3) // 64
    x_shape = (n_y, 2, 128)
    x_id = device_at(iota(x_shape, 0)) * 2 + iota(x_shape, 1)
    y_shape = (n_y, SUB, 128)
    y_lane = iota(y_shape, 2)
    y_id = (device_at(iota(y_shape, 0)) + 2 * (y_lane // 32 % 2) - 1) * 2 + y_lane // 16 % 2
    row8 = iota((SUB, 128), 0)
    lane8 = iota((SUB, 128), 1)

    def shell(holder, j):
        w2 = want(holder, j)
        w3, w4 = w2.reshape(1, 1, 128), w2.reshape(1, 1, 1, 128)
        rows = jnp.sum(jnp.where(a_id == w4, late[:, 0:2], 0.0), axis=(0, 1))
        edges = jnp.sum(jnp.where(b_id == w4, late[:, 2:4], 0.0), axis=0)
        halves = [edges[n] + pltpu.roll(edges[n], 64, 1) for n in range(2)]
        for side in range(2):
            line = [
                jnp.sum(jnp.where(x_id == w3, x_in[side, :, t], 0.0), axis=(0, 1)).reshape(1, 128)
                for t in range(2)
            ]
            for t in range(2):
                rows = rows + jnp.where(row8 == 4 * t + 3 * side, line[t], 0.0)
            both_ends = jnp.where(lane8 < 32, line[0], pltpu.roll(line[1], 64, 1))
            halves[side] = halves[side] + jnp.where(row8 == 7 * side, both_ends, 0.0)
        found = jnp.where(y_id == w3, late[:, 4], 0.0)
        for f in range(2):
            part = jnp.sum(jnp.where(bulk[:, 8] == f, found, 0.0), axis=0)
            part = part + pltpu.roll(part, 112, 1)
            part = part + pltpu.roll(part, 96, 1)
            spot = lane8 // 16 == 3 * f
            for n in range(2):
                turn = (48 * f + 64 * n) % 128
                moved = pltpu.roll(part, turn, 1) if turn else part
                halves[n] = halves[n] + jnp.where(spot, moved, 0.0)
        return rows, halves

    rows_of_shells = []
    for h in (3, 2, 1, 0):
        one, two = shell(holders[h], 0), shell(holders[h], 1)
        shell_out[h, 0] = one[0]
        shell_out[h, 1] = two[0]
        for n in range(2):
            shell_out[h, 2 + n] = jnp.where(lane8 < 64, one[1][n], pltpu.roll(two[1][n], 64, 1))
        if h:
            rows_of_shells.append(
                remote(
                    shell_out.at[h], shell_in.at[h - 1], es_sem.at[2 + h], er_sem.at[2 + h],
                    row_peers[h - 1],
                )
            )
    rows_of_bulk[1].wait_recv()
    inner = bulk_out[0] + bulk_in[0] + bulk_in[2]
    for copy in rows_of_shells:
        copy.wait_recv()
    outer = shell_out[0] + shell_in[0] + shell_in[1] + shell_in[2]
    for j in range(2):
        rows = outer[j]
        turned = pltpu.roll(rows, 4, 0)
        for n in range(2):
            edges = outer[2 + n] if j == 0 else pltpu.roll(outer[2 + n], 64, 1)
            for t in range(2):
                line = rows if t == n else turned
                found = jnp.where(row8 < 2 if n == 0 else row8 >= 6, line, inner[4 * j + 2 * t + n])
                if t == 0:
                    found = jnp.where(lane8 < 32, edges, found)
                else:
                    found = jnp.where(lane8 >= 96, pltpu.roll(edges, 64, 1), found)
                coarse[j, SUB * n : SUB * n + SUB, 128 * t : 128 * t + 128] = found
    last = pltpu.make_async_copy(coarse, coarse_hbm, out_sem.at[1])
    last.start()
    for copy in sent + wants + early + spread + rows_of_bulk + rows_of_shells:
        copy.wait_send()
    store.wait()
    last.wait()


def body(pressure, source, perm, brinkman, depth_source, sideways, edge_blocks, restrict_take):
    big = (2, CHUNKS, SUB, LANES)
    n_y = lax.axis_size("inslab") // 4
    vm = lambda *shape: pltpu.VMEM(shape, F32)
    dma = lambda n: pltpu.SemaphoreType.DMA((n,))
    anywhere = pl.BlockSpec(memory_space=pltpu.HBM)
    arrays = [x.reshape(big) for x in (pressure, source, perm)]
    arrays += [brinkman, depth_source, sideways, edge_blocks, restrict_take]
    smoothed, coarse = pl.pallas_call(
        kernel,
        out_shape=(
            jax.ShapeDtypeStruct(big, F32),
            jax.ShapeDtypeStruct((2, 16, 256), F32),
        ),
        in_specs=[anywhere] * 8,
        out_specs=(anywhere, anywhere),
        scratch_shapes=[
            pltpu.SMEM((2,), F32), pltpu.SMEM((2, 2), I32), pltpu.SMEM((2, 4), I32),
            pltpu.SMEM((1, 2, 2), I32), pltpu.SMEM((2,), I32),
        ]
        + [vm(*big) for _ in range(15)]
        + [
            vm(2, 2, LANES), vm(2, 2, CHUNKS, SUB, 128), vm(8, 64, 128), vm(512, 128), vm(128, 128),
            vm(2, 8, LANES), vm(2, 8, LANES),
            vm(2, 2 * CHUNKS + 1, SUB, 128), vm(2, 2 * CHUNKS + 1, SUB, 128),
            vm(2, 4, 128), vm(2, 2, 4, 128),
            pltpu.VMEM((6, SUB, 128), I32),
            vm(2, CHUNKS * SUB, 128),
            vm(n_y, 9, SUB, 128), vm(n_y, 5, SUB, 128), vm(2, 2, 2, 128), vm(2, n_y, 2, 2, 128),
            vm(4, 8, SUB, 128), vm(3, 8, SUB, 128), vm(4, 4, SUB, 128), vm(3, 4, SUB, 128), vm(2, 16, 256),
            dma(8), dma(2), dma(8), dma(8), dma(5), dma(5), dma(n_y - 1), dma(n_y - 1),
            dma(n_y - 1), dma(n_y - 1), dma(2 * n_y), dma(2 * n_y), dma(6), dma(6),
        ],
        compiler_params=pltpu.CompilerParams(
            collective_id=0, has_side_effects=True, vmem_limit_bytes=32 * 1024 * 1024
        ),
    )(*[pltpu.with_memory_space_constraint(x, pltpu.HBM) for x in arrays])
    return smoothed.reshape(pressure.shape), coarse


def solution(mesh):
    group = ("depth", "inslab")
    return jax.shard_map(
        body,
        mesh=mesh,
        in_specs=(
            P(group, None, None),
            P(group, None, None),
            P(group, None, None),
            P(group),
            P(group, None),
            P(group, None),
            P(group, None, None),
            P(group),
        ),
        out_specs=(P(group, None, None), P(group, None, None)),
        check_vma=False,
    )
```

```python
import jax
import jax.numpy as jnp
from jax import lax
from jax.experimental import pallas as pl
from jax.experimental.pallas import tpu as pltpu
from jax.sharding import PartitionSpec as P

OMEGA = 0.8
MESH = pl.DeviceIdType.MESH
F32 = jnp.float32
I32 = jnp.int32
CHUNKS, SUB, LANES = 4, 8, 1024
LAST = LANES - 128


def harmonic(a, b):
    return 2.0 * a * b / (a + b)


def kernel(
    p_hbm, s_hbm, k_hbm, brink_hbm, ds_hbm, snt_hbm, eb_hbm, take_hbm,
    out_hbm, coarse_hbm,
    brink, ds, snt, eb, take,
    u0, src, perm, u1, u2, g, ga, dg, inv, wxm, wxp, wym, wyp, wzm, wzp,
    wxe, wye, res, pool, pool_face,
    xs, xr, ys, yr, edge_out, edge_in,
    tables, face_sum, bulk, late, x_out, x_in, bulk_out, bulk_in, shell_out, shell_in, coarse,
    in_sem, out_sem, hs_sem, hr_sem, ts_sem, tr_sem, bs_sem, br_sem, gs_sem, gr_sem, xs_sem, xr_sem, es_sem, er_sem,
):
    depth = lax.axis_index("depth")
    me = lax.axis_index("inslab")
    n_depth = lax.axis_size("depth")
    n_in = lax.axis_size("inslab")
    n_y = n_in // 4
    my_y = me // 4
    zh = (me // 2) % 2
    core = me % 2

    def at(d, y, z, c):
        return (d, (y * 2 + z) * 2 + c)

    deeper = [lax.rem(depth + n_depth - 1, n_depth), lax.rem(depth + 1, n_depth)]
    beside_me = [lax.rem(me + n_in - 1, n_in), lax.rem(me + 1, n_in)]
    row_peers = [
        at(depth, my_y, zh, 1 - core), at(depth, my_y, 1 - zh, core), at(depth, my_y, 1 - zh, 1 - core)
    ]
    y_peers = [at(depth, lax.rem(my_y + o, n_y), zh, core) for o in range(1, n_y)]
    x_peers = [
        [at(deeper[side], lax.rem(my_y + o, n_y), zh, core) for o in range(n_y)] for side in range(2)
    ]
    i_peers = [(depth, m) for m in beside_me]
    d_peers = [(d, me) for d in deeper]
    corners = [[(d, m) for m in beside_me] for d in deeper]

    has = [depth > 0, depth < n_depth - 1]

    barrier = pltpu.get_barrier_semaphore()

    def greet(partner):
        pl.semaphore_signal(barrier, inc=1, device_id=partner, device_id_type=MESH)

    always = i_peers + row_peers + y_peers
    for partner in always:
        greet(partner)
    for side in range(2):
        pl.when(has[side])(lambda side=side: [greet(p) for p in [d_peers[side]] + corners[side]] and None)
    greeted = len(always) + sum(jnp.where(has[side], 1 + len(corners[side]), 0) for side in range(2))

    small = [(snt_hbm, snt), (ds_hbm, ds), (eb_hbm, eb), (take_hbm, take), (brink_hbm, brink)]
    loads = [
        pltpu.make_async_copy(h, v, in_sem.at[i])
        for i, (h, v) in enumerate([(k_hbm, perm), (p_hbm, u0), (s_hbm, src)] + small)
    ]
    for load in loads:
        load.start()
    for load in loads[3:]:
        load.wait()

    lane3 = lax.broadcasted_iota(I32, (CHUNKS, SUB, 128), 2)
    lane1 = lax.broadcasted_iota(I32, (1, 128), 1)
    row = lax.broadcasted_iota(I32, (SUB, LANES), 0)
    lane = lax.broadcasted_iota(I32, (SUB, LANES), 1)
    zpos = lane % 32
    quarter3 = lane3 // 32
    quarter1 = lane1 // 32

    def remote(a, b, s, r, device):
        copy = pltpu.make_async_remote_copy(
            src_ref=a, dst_ref=b, send_sem=s, recv_sem=r, device_id=device, device_id_type=MESH
        )
        copy.start()
        return copy

    class Link:
        def __init__(self, a, b, s, r, device, side):
            self.args, self.side = (a, b, s, r, device), side
            pl.when(has[side])(lambda: self.make().start())

        def make(self):
            a, b, s, r, device = self.args
            return pltpu.make_async_remote_copy(
                src_ref=a, dst_ref=b, send_sem=s, recv_sem=r, device_id=device, device_id_type=MESH
            )

        def wait_recv(self):
            pl.when(has[1 - self.side])(lambda: self.make().wait_recv())

        def wait_send(self):
            pl.when(has[self.side])(lambda: self.make().wait_send())

    def lies_minus(low):
        found = []
        for a in range(2):
            w = snt[a, 0]
            below = w - 2 < 2 * me
            found.append((w >= 2) & (below if low else jnp.logical_not(below)))
        return found[0] | found[1]

    minus = [lies_minus(True), lies_minus(False)]

    def quarter_of(a, direction):
        w = snt[a, direction]
        column = w & 1
        q = jnp.where(w - 2 < 2 * me, column, 2 + column)
        return jnp.where(w >= 2, q, -1)

    codes = [[quarter_of(a, direction) for direction in range(2)] for a in range(2)]

    trow = lax.broadcasted_iota(I32, (SUB, 128), 0)

    def as_rows(entries):
        tile = jnp.zeros((SUB, 128), I32)
        for i, value in enumerate(entries):
            tile = jnp.where(trow == i, value, tile)
        return tile

    tables[0] = as_rows([take[0], take[1]] + [codes[a][s] for a in range(2) for s in range(2)])
    links = as_rows(
        [ds[a, s] for a in range(2) for s in range(2)]
        + [eb[0, s, c] for s in range(2) for c in range(2)]
    ).astype(F32)

    def y_faces(field):
        low = [field[a, :, :, 0:128] for a in range(2)]
        high = [pltpu.roll(field[a, :, :, LAST:LANES], 32, 2) for a in range(2)]
        return low, high

    def pair_for(faces, is_minus):
        low, high = faces
        cols = []
        for c in range(2):
            from_low = jnp.where(eb[0, 0, c] == 1, low[1], low[0])
            from_high = jnp.where(eb[0, 1, c] == 1, high[1], high[0])
            cols.append(jnp.where(is_minus, from_low, from_high))
        return jnp.where(lane3 < 32, cols[0], pltpu.roll(cols[1], 32, 2))

    def x_face(field, side, a):
        if side == 0:
            return field[a, 0, 0:1, :]
        return field[a, CHUNKS - 1, SUB - 1 : SUB, :]

    def fill(first, second, block):
        for side in range(2):
            for a in range(2):
                n = 4 * block + a
                xs[side, n : n + 1, :] = x_face(first, side, a)
                xs[side, n + 2 : n + 3, :] = x_face(second, side, a)
        one, two = y_faces(first), y_faces(second)
        for peer in range(2):
            ys[peer, CHUNKS * block : CHUNKS * block + CHUNKS] = jnp.where(
                lane3 < 64, pair_for(one, minus[peer]), pltpu.roll(pair_for(two, minus[peer]), 64, 2)
            )

    loads[0].wait()
    loads[1].wait()
    fill(u0, perm, 0)
    for peer in range(2):
        ys[peer, 2 * CHUNKS] = links
    for side in range(2):
        for f, field in enumerate((u0, perm)):
            lines = []
            for a in range(2):
                face = x_face(field, side, a)
                lines.append([face[:, 0:128], pltpu.roll(face[:, LAST:LANES], 32, 1)])
            by_column = [
                jnp.where(eb[0, s, c] == 1, lines[1][s], lines[0][s]) for s in range(2) for c in range(2)
            ]
            by_slot = [lines[a][s] for a in range(2) for s in range(2)]
            for n, listed in enumerate((by_column, by_slot)):
                packed = listed[0]
                for q in range(1, 4):
                    packed = jnp.where(quarter1 == q, pltpu.roll(listed[q], 32 * q, 1), packed)
                edge_out[side, 2 * n + f : 2 * n + f + 1, :] = packed
    def zslot(a, direction):
        return jnp.maximum(snt[a, 2 + direction], 0)

    def beside(field, a, k):
        u = field[a, k]
        before = field[a, jnp.maximum(k - 1, 0), SUB - 1 : SUB, :]
        after = field[a, jnp.minimum(k + 1, CHUNKS - 1), 0:1, :]
        um = jnp.where(row == 0, before, pltpu.roll(u, 1, 0))
        up = jnp.where(row == SUB - 1, after, pltpu.roll(u, SUB - 1, 0))
        ym = pltpu.roll(u, 32, 1)
        yp = pltpu.roll(u, LANES - 32, 1)
        nm = field[zslot(a, 0), k]
        np_ = field[zslot(a, 1), k]
        zm = jnp.where(zpos == 0, pltpu.roll(nm, LANES - 31, 1), pltpu.roll(u, 1, 1))
        zp = jnp.where(zpos == 31, pltpu.roll(np_, 31, 1), pltpu.roll(u, LANES - 1, 1))
        return u, (um, up, ym, yp, zm, zp)

    def weights(n, _):
        k = CHUNKS - 1 - n
        for a in range(2):
            kk = perm[a, k]
            before = perm[a, jnp.maximum(k - 1, 0), SUB - 1 : SUB, :]
            um = jnp.where(row == 0, before, pltpu.roll(kk, 1, 0))
            ym = pltpu.roll(kk, 32, 1)
            nm = perm[zslot(a, 0), k]
            zm = jnp.where(zpos == 0, pltpu.roll(nm, LANES - 31, 1), pltpu.roll(kk, 1, 1))
            first = (row == 0) & (k == 0)
            wxm[a, k] = jnp.where(first, 0.0, harmonic(kk, um))
            wym[a, k] = jnp.where(lane >= 32, harmonic(kk, ym), 0.0)
            wzm[a, k] = jnp.where((zpos != 0) | (snt[a, 2] >= 0), harmonic(kk, zm), 0.0)
        for a in range(2):
            after = wxm[a, jnp.minimum(k + 1, CHUNKS - 1), 0:1, :]
            after = jnp.where(k == CHUNKS - 1, 0.0, after)
            xp = jnp.where(row == SUB - 1, after, pltpu.roll(wxm[a, k], SUB - 1, 0))
            yp = pltpu.roll(wym[a, k], LANES - 32, 1)
            across_z = jnp.where(snt[a, 3] >= 0, pltpu.roll(wzm[zslot(a, 1), k], 31, 1), 0.0)
            zp = jnp.where(zpos == 31, across_z, pltpu.roll(wzm[a, k], LANES - 1, 1))
            wxp[a, k] = xp
            wyp[a, k] = yp
            wzp[a, k] = zp
            dg[a, k] = brink[a] + wxm[a, k] + xp + wym[a, k] + yp + wzm[a, k] + zp
        return 0

    lax.fori_loop(0, CHUNKS, weights, 0)
    loads[2].wait()

    def neighbour_sum(field, into, first=0, stride=1, count=CHUNKS):
        def step(n, _):
            k = first + stride * n
            for a in range(2):
                _, nbs = beside(field, a, k)
                total = src[a, k]
                for store, nb in zip((wxm, wxp, wym, wyp, wzm, wzp), nbs):
                    total = total + store[a, k] * nb
                into[a, k] = total
            return 0

        lax.fori_loop(0, count, step, 0)

    outer_tiles = ((0, 0), (LANES - 256, 128))

    def edge_sum(field, into):
        def step(n, _):
            k = 1 + n
            for a in range(2):
                for start, kept in outer_tiles:
                    part = slice(start, start + 256)
                    u = field[a, k, :, part]
                    nm = field[zslot(a, 0), k, :, part]
                    np_ = field[zslot(a, 1), k, :, part]
                    before = field[a, k - 1, SUB - 1 : SUB, part]
                    after = field[a, k + 1, 0:1, part]
                    nbs = (
                        jnp.where(row[:, 0:256] == 0, before, pltpu.roll(u, 1, 0)),
                        jnp.where(row[:, 0:256] == SUB - 1, after, pltpu.roll(u, SUB - 1, 0)),
                        pltpu.roll(u, 32, 1),
                        pltpu.roll(u, 224, 1),
                        jnp.where(zpos[:, 0:256] == 0, pltpu.roll(nm, 225, 1), pltpu.roll(u, 1, 1)),
                        jnp.where(zpos[:, 0:256] == 31, pltpu.roll(np_, 31, 1), pltpu.roll(u, 255, 1)),
                    )
                    total = src[a, k, :, part]
                    for store, nb in zip((wxm, wxp, wym, wyp, wzm, wzp), nbs):
                        total = total + store[a, k, :, part] * nb
                    into[a, k, :, start + kept : start + kept + 128] = total[:, kept : kept + 128]
            return 0

        lax.fori_loop(0, CHUNKS - 2, step, 0)

    neighbour_sum(u0, g)
    fill(g, dg, 1)

    prow = lax.broadcasted_iota(I32, (512, 128), 0)
    pcol = lax.broadcasted_iota(I32, (512, 128), 1)
    pool[...] = (0.125 * ((prow // 64) * 16 + (prow % 32) // 2 == pcol).astype(F32)).astype(jnp.bfloat16)
    frow = lax.broadcasted_iota(I32, (128, 128), 0)
    fcol = lax.broadcasted_iota(I32, (128, 128), 1)
    pool_face[...] = (0.125 * (frow // 32 * 16 + (frow % 32) // 2 == fcol).astype(F32)).astype(jnp.bfloat16)

    def exact_dot(x, matrix):
        high = x.astype(jnp.bfloat16).astype(F32)
        rest = x - high
        middle = rest.astype(jnp.bfloat16).astype(F32)
        parts = jnp.concatenate([high, middle, rest - middle, jnp.zeros_like(x)], axis=0)
        out = jnp.dot(parts.astype(jnp.bfloat16), matrix, preferred_element_type=F32)
        n = x.shape[0]
        return out[0:n] + out[n : 2 * n] + out[2 * n : 3 * n]

    def pooled_residual(field, sums):
        def step(k, _):
            for a in range(2):
                at_row = pl.multiple_of(a * 32 + k * SUB, SUB)
                r = sums[a, k] - dg[a, k] * field[a, k]
                for t in range(8):
                    res[t, pl.ds(at_row, SUB), :] = r[:, 128 * t : 128 * t + 128]
            return 0

        lax.fori_loop(0, CHUNKS, step, 0)
        paired = [
            res[t, pl.ds(0, 32, stride=2), :] + res[t, pl.ds(1, 32, stride=2), :] for t in range(8)
        ]
        stacked = [jnp.concatenate(paired[4 * h : 4 * h + 4], axis=1) for h in range(2)]
        return exact_dot(jnp.concatenate(stacked, axis=0), pool[...])

    def piece_of(pooled, a, t):
        return pooled[32 * t + 16 * a : 32 * t + 16 * a + 16, :]

    def inner_first(k, _):
        for a in range(2):
            i = OMEGA / dg[a, k]
            inv[a, k] = i
            u1[a, k] = (1.0 - OMEGA) * u0[a, k] + i * g[a, k]
        return 0

    def inner_second(k, _):
        for a in range(2):
            u2[a, k] = (1.0 - OMEGA) * u1[a, k] + inv[a, k] * ga[a, k]
        return 0

    def inner_pieces():
        lax.fori_loop(0, CHUNKS, inner_first, 0)
        neighbour_sum(u1, ga)
        lax.fori_loop(0, CHUNKS, inner_second, 0)
        neighbour_sum(u2, ga)
        pooled = pooled_residual(u2, ga)
        for a in range(2):
            for t in range(2):
                n = 4 * a + 2 * t
                bulk[my_y, n : n + 2] = piece_of(pooled, a, t).reshape(2, SUB, 128)
        sides = jnp.where(quarter1 % 2 == 0, minus[0].astype(F32), minus[1].astype(F32))
        bulk[my_y, 8] = jnp.broadcast_to(sides, (SUB, 128))

    pl.when(zh == 0)(inner_pieces)
    pl.semaphore_wait(barrier, greeted)
    sent = []
    for peer in range(2):
        sent.append(remote(ys.at[peer], yr.at[1 - peer], hs_sem.at[peer], hr_sem.at[peer], i_peers[peer]))
    for side in range(2):
        for peer in range(2):
            n = 4 + 2 * side + peer
            sent.append(
                Link(
                    edge_out.at[side], edge_in.at[1 - side, 1 - peer],
                    hs_sem.at[n], hr_sem.at[n], corners[side][peer], side,
                )
            )
    for side in range(2):
        n = 2 + side
        sent.append(
            Link(xs.at[side], xr.at[1 - side], hs_sem.at[n], hr_sem.at[n], d_peers[side], side)
        )
        sent.append(
            Link(
                tables.at[0], tables.at[2 - side], ts_sem.at[side], tr_sem.at[side], d_peers[side], side
            )
        )
    wants = [
        remote(tables.at[0], tables.at[3 + j], ts_sem.at[2 + j], tr_sem.at[2 + j], device)
        for j, device in enumerate(row_peers)
    ]
    pl.when(zh == 1)(inner_pieces)
    early = [
        remote(bulk.at[my_y], bulk.at[my_y], bs_sem.at[o], br_sem.at[o], device)
        for o, device in enumerate(y_peers)
    ]

    def pick(choice, options):
        found = jnp.zeros_like(options[0])
        for i, option in enumerate(options):
            found = jnp.where(choice == i, option, found)
        return found

    for side in range(2):

        @pl.when(jnp.logical_not(has[side]))
        def _():
            xr[side] = jnp.ones((8, LANES), F32)
            x_in[side] = jnp.zeros((n_y, 2, 2, 128), F32)
            tables[1 + side] = jnp.full((SUB, 128), -1, I32)
            for peer in range(2):
                edge_in[side, peer] = jnp.zeros((4, 128), F32)

    for copy in sent:
        copy.wait_recv()

    px, kx, gx, dx = (
        [[xr[s, n + j : n + j + 1, :] for j in range(2)] for s in range(2)] for n in (0, 2, 4, 6)
    )

    def both(block):
        low, high = [yr[peer, CHUNKS * block : CHUNKS * block + CHUNKS] for peer in range(2)]
        return (
            jnp.where(lane3 < 64, low, pltpu.roll(high, 64, 2)),
            jnp.where(lane3 < 64, pltpu.roll(low, 64, 2), high),
        )

    py, ky = both(0)
    gy, dy = both(1)

    def rotated(quarters):
        return [quarters] + [pltpu.roll(quarters, 128 - 32 * q, 2) for q in range(1, 4)]

    def own_faces(field):
        low, high = y_faces(field)
        return [[low[a], high[a]] for a in range(2)]

    def into_quarters(faces, keys):
        total = jnp.zeros((CHUNKS, SUB, 128), F32)
        for a in range(2):
            for direction in range(2):
                face = jnp.where(lane3 < 32, faces[a][direction], 0.0)
                face = face + pltpu.roll(face, 32, 2)
                face = face + pltpu.roll(face, 64, 2)
                total = total + jnp.where(quarter3 == keys[a][direction], face, 0.0)
        return total

    k_faces, u_faces = own_faces(perm), own_faces(u0)
    k_turned, u_turned = rotated(ky), rotated(py)

    def add_y(ref, a, direction, value):
        if direction == 0:
            ref[a, :, :, 0:128] += value
        else:
            ref[a, :, :, LAST:LANES] += pltpu.roll(value, 96, 2)

    def add_x(ref, a, side, value):
        if side == 0:
            ref[a, 0, 0:1, :] += value
        else:
            ref[a, CHUNKS - 1, SUB - 1 : SUB, :] += value

    for a in range(2):
        for side in range(2):
            w = harmonic(x_face(perm, side, a), pick(ds[a, side], kx[side]))
            wxe[side, a : a + 1, :] = w
            add_x(dg, a, side, w)
            add_x(g, a, side, w * pick(ds[a, side], px[side]))
        for direction in range(2):
            kg = pick(codes[a][direction], k_turned)
            w = jnp.where(lane3 < 32, harmonic(k_faces[a][direction], kg), 0.0)
            wye[a, direction] = w
            add_y(dg, a, direction, w)
            add_y(g, a, direction, w * pick(codes[a][direction], u_turned))

    def line(packed, start, target):
        return pltpu.roll(packed, (target - start) % 4 * 32, 1) if start != target else packed

    px1 = []
    for side in range(2):
        found = []
        for j in range(2):
            gsum, dsum = gx[side][j], dx[side][j]
            mine_p = jnp.zeros((1, LANES), F32)
            mine_k = jnp.zeros((1, LANES), F32)
            for a in range(2):
                linked = ds[a, side] == j
                mine_p = jnp.where(linked, x_face(u0, side, a), mine_p)
                mine_k = jnp.where(linked, x_face(perm, side, a), mine_k)
            w = harmonic(kx[side][j], mine_k)
            gsum = gsum + w * mine_p
            dsum = dsum + w
            ends = []
            for direction in range(2):
                code = tables[1 + side, 2 + 2 * j + direction : 3 + 2 * j + direction, :]
                start = 2 if direction == 0 else 0
                target = 0 if direction == 0 else 3
                values = []
                for f in range(2):
                    options = [
                        line(edge_in[side, peer, f : f + 1, :], start + c, target)
                        for peer in range(2)
                        for c in range(2)
                    ]
                    values.append(pick(code, options))
                kk = kx[side][j][:, 0:128] if direction == 0 else kx[side][j][:, LAST:LANES]
                w = jnp.where(quarter1 == target, harmonic(kk, values[1]), 0.0)
                ends.append((w, w * values[0]))
            gap = jnp.zeros((1, LANES - 256), F32)
            dsum = dsum + jnp.concatenate([ends[0][0], gap, ends[1][0]], axis=1)
            gsum = gsum + jnp.concatenate([ends[0][1], gap, ends[1][1]], axis=1)
            found.append((1.0 - OMEGA) * px[side][j] + OMEGA * gsum / dsum)
        px1.append(found)

    mine_k = into_quarters(k_faces, codes)
    w = harmonic(ky, mine_k)
    gy = gy + w * into_quarters(u_faces, codes)
    dy = dy + w
    slots = []
    for peer in range(2):
        held = yr[peer, 2 * CHUNKS]
        for c in range(2):
            slots.append(jnp.where(minus[peer], held[6 + c : 7 + c, :], held[4 + c : 5 + c, :]))
    rows3 = lax.broadcasted_iota(I32, (CHUNKS, SUB, 128), 0) * SUB + lax.broadcasted_iota(
        I32, (CHUNKS, SUB, 128), 1
    )
    for side in range(2):
        values = []
        for f in range(2):
            total = jnp.zeros((1, 128), F32)
            for q in range(4):
                peer = q // 2
                held = yr[peer, 2 * CHUNKS]
                link = jnp.where(
                    slots[q] == 1, held[2 + side : 3 + side, :], held[side : side + 1, :]
                )
                edge = edge_in[side, peer, 2 + f : 3 + f, :]
                options = [
                    jnp.where(minus[peer], line(edge, 2 * s + 1, q), line(edge, 2 * s, q))
                    for s in range(2)
                ]
                total = jnp.where(quarter1 == q, pick(link, options), total)
            values.append(total)
        r = 0 if side == 0 else CHUNKS * SUB - 1
        here = ky[0, 0:1, :] if side == 0 else ky[CHUNKS - 1, SUB - 1 : SUB, :]
        w = harmonic(here, values[1])
        dy = dy + jnp.where(rows3 == r, w.reshape(1, 1, 128), 0.0)
        gy = gy + jnp.where(rows3 == r, (w * values[0]).reshape(1, 1, 128), 0.0)
    py1 = (1.0 - OMEGA) * py + OMEGA * gy / dy

    whole = slice(0, LANES)
    parts = [(k, whole) for k in (0, CHUNKS - 1)]
    parts += [(k, part) for k in range(1, CHUNKS - 1) for part in (slice(0, 128), slice(LAST, LANES))]
    for k, part in parts:
        for a in range(2):
            i = OMEGA / dg[a, k, :, part]
            inv[a, k, :, part] = i
            u1[a, k, :, part] = (1.0 - OMEGA) * u0[a, k, :, part] + i * g[a, k, :, part]

    u_turned = rotated(py1)
    y_flow = [
        [wye[a, direction] * pick(codes[a][direction], u_turned) for direction in range(2)]
        for a in range(2)
    ]
    x_flow = [[wxe[side, a : a + 1, :] * pick(ds[a, side], px1[side]) for side in range(2)] for a in range(2)]

    def second_update(chosen):
        for k, part in chosen:
            for a in range(2):
                if part.start == 0:
                    g[a, k, :, 0:128] += y_flow[a][0][k]
                if part.stop == LANES:
                    g[a, k, :, LAST:LANES] += pltpu.roll(y_flow[a][1][k], 96, 1)
                u2[a, k, :, part] = (1.0 - OMEGA) * u1[a, k, :, part] + inv[a, k, :, part] * g[a, k, :, part]

    neighbour_sum(u1, g, 0, CHUNKS - 1, 2)
    for a in range(2):
        for side in range(2):
            add_x(g, a, side, x_flow[a][side])
    second_update(parts[0:2])
    across = []
    for side in range(2):
        flows = [wxe[side, a : a + 1, :] * x_face(u2, side, a) for a in range(2)]
        for s in range(2):
            total = jnp.zeros((1, LANES), F32)
            for a in range(2):
                total = total + jnp.where(ds[a, side] == s, flows[a], 0.0)
            across.append(total)
    across = jnp.concatenate(across, axis=0)
    crossing = exact_dot(jnp.concatenate([across[:, 0:512], across[:, 512:1024]], axis=0), pool[...])
    for side in range(2):
        for t in range(2):
            x_out[side, t] = crossing[4 * t + 2 * side : 4 * t + 2 * side + 2, :]
    spread = []
    for side in range(2):
        for o, device in enumerate(x_peers[side]):
            n = side * n_y + o
            spread.append(
                Link(x_out.at[side], x_in.at[1 - side, my_y], xs_sem.at[n], xr_sem.at[n], device, side)
            )
    edge_sum(u1, g)
    second_update(parts[2:])
    store = pltpu.make_async_copy(u2, out_hbm, out_sem.at[0])
    store.start()
    neighbour_sum(u2, g, 0, CHUNKS - 1, 2)
    edge_sum(u2, g)

    pooled = pooled_residual(u2, g)
    lane2 = lax.broadcasted_iota(I32, (16, 128), 1)
    edges = jnp.zeros((16, 128), F32)
    for a in range(2):
        for t in range(2):
            part = piece_of(pooled, a, t)
            late[my_y, a, 4 * t : 4 * t + 2, :] = part[0:2, :]
            late[my_y, a, 4 * t + 2 : 4 * t + 4, :] = part[14:16, :]
            part = part if a == t else pltpu.roll(part, 64, 1)
            edges = jnp.where(lane2 // 32 == 2 * a + t, part, edges)
    late[my_y, 2:4] = edges.reshape(2, SUB, 128)
    u_faces = own_faces(u2)
    for direction in range(2):
        total = jnp.zeros((CHUNKS, SUB, 128), F32)
        for a in range(2):
            face = wye[a, direction] * u_faces[a][direction]
            face = face + pltpu.roll(face, 32, 2)
            face = face + pltpu.roll(face, 64, 2)
            code = codes[a][direction]
            slot = pick(code, slots)
            key = jnp.where(code >= 2, 2.0, 0.0) + slot
            hit = (quarter1.astype(F32) == key) & (code >= 0)
            total = total + jnp.where(hit.reshape(1, 1, 128), face, 0.0)
        face_sum[direction] = total.reshape(CHUNKS * SUB, 128)
    halves = [
        face_sum[direction, pl.ds(first, 16, stride=2), :] for direction in range(2) for first in range(2)
    ]
    faces = exact_dot(halves[0] + halves[1] + halves[2] + halves[3], pool_face[...])
    late[my_y, 4] = jnp.where(lane2[0:8] < 64, faces[0:8], pltpu.roll(faces[8:16], 64, 1))

    spread += [
        remote(late.at[my_y], late.at[my_y], gs_sem.at[o], gr_sem.at[o], device)
        for o, device in enumerate(y_peers)
    ]
    for copy in wants + early:
        copy.wait_recv()

    def device_at(y):
        return (y * 2 + zh) * 2 + core

    def iota(shape, dim):
        return lax.broadcasted_iota(I32, shape, dim)

    bulk_shape = (n_y, 2, 4, SUB, 128)
    bulk_id = device_at(iota(bulk_shape, 0)) * 2 + iota(bulk_shape, 1)

    def want(holder, j):
        return tables[holder, j : j + 1, :]

    holders = (0, 3, 4, 5)
    for h, holder in ((2, 3), (3, 5), (1, 4), (0, 0)):
        held = bulk[:, 0:8].reshape(bulk_shape)
        for j in range(2):
            w = want(holder, j).reshape(1, 1, 1, 1, 128)
            bulk_out[h, 4 * j : 4 * j + 4] = jnp.sum(jnp.where(bulk_id == w, held, 0.0), axis=(0, 1))
        if h == 3:
            to_core = remote(
                bulk_out.at[pl.ds(2, 2)], bulk_in.at[pl.ds(0, 2)], es_sem.at[0], er_sem.at[0], row_peers[0]
            )
    to_core.wait_recv()
    bulk_out[1] += bulk_in[1]
    rows_of_bulk = [
        to_core, remote(bulk_out.at[1], bulk_in.at[2], es_sem.at[1], er_sem.at[1], row_peers[1])
    ]

    for copy in spread:
        copy.wait_recv()

    a_shape = (n_y, 2, SUB, 128)
    a_id = device_at(iota(a_shape, 0)) * 2 + iota(a_shape, 1)
    b_id = device_at(iota(a_shape, 0)) * 2 + iota(a_shape, 3) // 64
    x_shape = (n_y, 2, 128)
    x_id = device_at(iota(x_shape, 0)) * 2 + iota(x_shape, 1)
    y_shape = (n_y, SUB, 128)
    y_lane = iota(y_shape, 2)
    y_id = (device_at(iota(y_shape, 0)) + 2 * (y_lane // 32 % 2) - 1) * 2 + y_lane // 16 % 2
    row8 = iota((SUB, 128), 0)
    lane8 = iota((SUB, 128), 1)

    def shell(holder, j):
        w2 = want(holder, j)
        w3, w4 = w2.reshape(1, 1, 128), w2.reshape(1, 1, 1, 128)
        rows = jnp.sum(jnp.where(a_id == w4, late[:, 0:2], 0.0), axis=(0, 1))
        edges = jnp.sum(jnp.where(b_id == w4, late[:, 2:4], 0.0), axis=0)
        halves = [edges[n] + pltpu.roll(edges[n], 64, 1) for n in range(2)]
        for side in range(2):
            line = [
                jnp.sum(jnp.where(x_id == w3, x_in[side, :, t], 0.0), axis=(0, 1)).reshape(1, 128)
                for t in range(2)
            ]
            for t in range(2):
                rows = rows + jnp.where(row8 == 4 * t + 3 * side, line[t], 0.0)
            both_ends = jnp.where(lane8 < 32, line[0], pltpu.roll(line[1], 64, 1))
            halves[side] = halves[side] + jnp.where(row8 == 7 * side, both_ends, 0.0)
        found = jnp.where(y_id == w3, late[:, 4], 0.0)
        for f in range(2):
            part = jnp.sum(jnp.where(bulk[:, 8] == f, found, 0.0), axis=0)
            part = part + pltpu.roll(part, 112, 1)
            part = part + pltpu.roll(part, 96, 1)
            spot = lane8 // 16 == 3 * f
            for n in range(2):
                turn = (48 * f + 64 * n) % 128
                moved = pltpu.roll(part, turn, 1) if turn else part
                halves[n] = halves[n] + jnp.where(spot, moved, 0.0)
        return rows, halves

    rows_of_shells = []
    for h in (3, 2, 1, 0):
        one, two = shell(holders[h], 0), shell(holders[h], 1)
        shell_out[h, 0] = one[0]
        shell_out[h, 1] = two[0]
        for n in range(2):
            shell_out[h, 2 + n] = jnp.where(lane8 < 64, one[1][n], pltpu.roll(two[1][n], 64, 1))
        if h:
            rows_of_shells.append(
                remote(
                    shell_out.at[h], shell_in.at[h - 1], es_sem.at[2 + h], er_sem.at[2 + h],
                    row_peers[h - 1],
                )
            )
    rows_of_bulk[1].wait_recv()
    inner = bulk_out[0] + bulk_in[0] + bulk_in[2]
    for copy in rows_of_shells:
        copy.wait_recv()
    outer = shell_out[0] + shell_in[0] + shell_in[1] + shell_in[2]
    for j in range(2):
        rows = outer[j]
        turned = pltpu.roll(rows, 4, 0)
        for n in range(2):
            edges = outer[2 + n] if j == 0 else pltpu.roll(outer[2 + n], 64, 1)
            for t in range(2):
                line = rows if t == n else turned
                found = jnp.where(row8 < 2 if n == 0 else row8 >= 6, line, inner[4 * j + 2 * t + n])
                if t == 0:
                    found = jnp.where(lane8 < 32, edges, found)
                else:
                    found = jnp.where(lane8 >= 96, pltpu.roll(edges, 64, 1), found)
                coarse[j, SUB * n : SUB * n + SUB, 128 * t : 128 * t + 128] = found
    last = pltpu.make_async_copy(coarse, coarse_hbm, out_sem.at[1])
    last.start()
    for copy in sent + wants + early + spread + rows_of_bulk + rows_of_shells:
        copy.wait_send()
    store.wait()
    last.wait()


def body(pressure, source, perm, brinkman, depth_source, sideways, edge_blocks, restrict_take):
    big = (2, CHUNKS, SUB, LANES)
    n_y = lax.axis_size("inslab") // 4
    vm = lambda *shape: pltpu.VMEM(shape, F32)
    dma = lambda n: pltpu.SemaphoreType.DMA((n,))
    anywhere = pl.BlockSpec(memory_space=pltpu.HBM)
    arrays = [x.reshape(big) for x in (pressure, source, perm)]
    arrays += [brinkman, depth_source, sideways, edge_blocks, restrict_take]
    smoothed, coarse = pl.pallas_call(
        kernel,
        out_shape=(
            jax.ShapeDtypeStruct(big, F32),
            jax.ShapeDtypeStruct((2, 16, 256), F32),
        ),
        in_specs=[anywhere] * 8,
        out_specs=(anywhere, anywhere),
        scratch_shapes=[
            pltpu.SMEM((2,), F32), pltpu.SMEM((2, 2), I32), pltpu.SMEM((2, 4), I32),
            pltpu.SMEM((1, 2, 2), I32), pltpu.SMEM((2,), I32),
        ]
        + [vm(*big) for _ in range(15)]
        + [
            vm(2, 2, LANES), vm(2, 2, CHUNKS, SUB, 128), vm(8, 64, 128),
            pltpu.VMEM((512, 128), jnp.bfloat16), pltpu.VMEM((128, 128), jnp.bfloat16),
            vm(2, 8, LANES), vm(2, 8, LANES),
            vm(2, 2 * CHUNKS + 1, SUB, 128), vm(2, 2 * CHUNKS + 1, SUB, 128),
            vm(2, 4, 128), vm(2, 2, 4, 128),
            pltpu.VMEM((6, SUB, 128), I32),
            vm(2, CHUNKS * SUB, 128),
            vm(n_y, 9, SUB, 128), vm(n_y, 5, SUB, 128), vm(2, 2, 2, 128), vm(2, n_y, 2, 2, 128),
            vm(4, 8, SUB, 128), vm(3, 8, SUB, 128), vm(4, 4, SUB, 128), vm(3, 4, SUB, 128), vm(2, 16, 256),
            dma(8), dma(2), dma(8), dma(8), dma(5), dma(5), dma(n_y - 1), dma(n_y - 1),
            dma(n_y - 1), dma(n_y - 1), dma(2 * n_y), dma(2 * n_y), dma(6), dma(6),
        ],
        compiler_params=pltpu.CompilerParams(
            collective_id=0, has_side_effects=True, vmem_limit_bytes=32 * 1024 * 1024
        ),
    )(*[pltpu.with_memory_space_constraint(x, pltpu.HBM) for x in arrays])
    return smoothed.reshape(pressure.shape), coarse


def solution(mesh):
    group = ("depth", "inslab")
    return jax.shard_map(
        body,
        mesh=mesh,
        in_specs=(
            P(group, None, None),
            P(group, None, None),
            P(group, None, None),
            P(group),
            P(group, None),
            P(group, None),
            P(group, None, None),
            P(group),
        ),
        out_specs=(P(group, None, None), P(group, None, None)),
        check_vma=False,
    )
```

```python
import jax
import jax.numpy as jnp
from jax import lax
from jax.experimental import pallas as pl
from jax.experimental.pallas import tpu as pltpu
from jax.sharding import PartitionSpec as P

OMEGA = 0.8
MESH = pl.DeviceIdType.MESH
F32 = jnp.float32
I32 = jnp.int32
CHUNKS, SUB, LANES = 4, 8, 1024
LAST = LANES - 128


def harmonic(a, b):
    return 2.0 * a * b / (a + b)


def kernel(
    p_hbm, s_hbm, k_hbm, brink_hbm, ds_hbm, snt_hbm, eb_hbm, take_hbm,
    out_hbm, coarse_hbm,
    brink, ds, snt, eb, take,
    u0, src, perm, u1, u2, g, ga, dg, inv, wxm, wxp, wym, wyp, wzm, wzp,
    wxe, wye, res, pool, pool_face,
    xs, xr, ys, yr, edge_out, edge_in,
    tables, face_sum, bulk, late, x_out, x_in, bulk_out, bulk_in, shell_out, shell_in, coarse,
    in_sem, out_sem, hs_sem, hr_sem, ts_sem, tr_sem, bs_sem, br_sem, gs_sem, gr_sem, xs_sem, xr_sem, es_sem, er_sem,
):
    depth = lax.axis_index("depth")
    me = lax.axis_index("inslab")
    n_depth = lax.axis_size("depth")
    n_in = lax.axis_size("inslab")
    n_y = n_in // 4
    my_y = me // 4
    zh = (me // 2) % 2
    core = me % 2

    def at(d, y, z, c):
        return (d, (y * 2 + z) * 2 + c)

    deeper = [lax.rem(depth + n_depth - 1, n_depth), lax.rem(depth + 1, n_depth)]
    beside_me = [lax.rem(me + n_in - 1, n_in), lax.rem(me + 1, n_in)]
    row_peers = [
        at(depth, my_y, zh, 1 - core), at(depth, my_y, 1 - zh, core), at(depth, my_y, 1 - zh, 1 - core)
    ]
    offsets = sorted(range(n_y), key=lambda o: -min(o, n_y - o))
    y_peers = [at(depth, lax.rem(my_y + o, n_y), zh, core) for o in offsets if o]
    x_peers = [
        [at(deeper[side], lax.rem(my_y + o, n_y), zh, core) for o in offsets] for side in range(2)
    ]
    i_peers = [(depth, m) for m in beside_me]
    d_peers = [(d, me) for d in deeper]
    corners = [[(d, m) for m in beside_me] for d in deeper]

    has = [depth > 0, depth < n_depth - 1]

    barrier = pltpu.get_barrier_semaphore()

    def greet(partner):
        pl.semaphore_signal(barrier, inc=1, device_id=partner, device_id_type=MESH)

    always = i_peers + row_peers + y_peers
    for partner in always:
        greet(partner)
    for side in range(2):
        pl.when(has[side])(lambda side=side: [greet(p) for p in [d_peers[side]] + corners[side]] and None)
    greeted = len(always) + sum(jnp.where(has[side], 1 + len(corners[side]), 0) for side in range(2))

    small = [(snt_hbm, snt), (ds_hbm, ds), (eb_hbm, eb), (take_hbm, take), (brink_hbm, brink)]
    loads = [
        pltpu.make_async_copy(h, v, in_sem.at[i])
        for i, (h, v) in enumerate([(k_hbm, perm), (p_hbm, u0), (s_hbm, src)] + small)
    ]
    for load in loads:
        load.start()
    for load in loads[3:]:
        load.wait()

    lane3 = lax.broadcasted_iota(I32, (CHUNKS, SUB, 128), 2)
    lane1 = lax.broadcasted_iota(I32, (1, 128), 1)
    row = lax.broadcasted_iota(I32, (SUB, LANES), 0)
    lane = lax.broadcasted_iota(I32, (SUB, LANES), 1)
    zpos = lane % 32
    quarter3 = lane3 // 32
    quarter1 = lane1 // 32

    def remote(a, b, s, r, device):
        copy = pltpu.make_async_remote_copy(
            src_ref=a, dst_ref=b, send_sem=s, recv_sem=r, device_id=device, device_id_type=MESH
        )
        copy.start()
        return copy

    class Link:
        def __init__(self, a, b, s, r, device, side):
            self.args, self.side = (a, b, s, r, device), side
            pl.when(has[side])(lambda: self.make().start())

        def make(self):
            a, b, s, r, device = self.args
            return pltpu.make_async_remote_copy(
                src_ref=a, dst_ref=b, send_sem=s, recv_sem=r, device_id=device, device_id_type=MESH
            )

        def wait_recv(self):
            pl.when(has[1 - self.side])(lambda: self.make().wait_recv())

        def wait_send(self):
            pl.when(has[self.side])(lambda: self.make().wait_send())

    def lies_minus(low):
        found = []
        for a in range(2):
            w = snt[a, 0]
            below = w - 2 < 2 * me
            found.append((w >= 2) & (below if low else jnp.logical_not(below)))
        return found[0] | found[1]

    minus = [lies_minus(True), lies_minus(False)]

    def quarter_of(a, direction):
        w = snt[a, direction]
        column = w & 1
        q = jnp.where(w - 2 < 2 * me, column, 2 + column)
        return jnp.where(w >= 2, q, -1)

    codes = [[quarter_of(a, direction) for direction in range(2)] for a in range(2)]

    trow = lax.broadcasted_iota(I32, (SUB, 128), 0)

    def as_rows(entries):
        tile = jnp.zeros((SUB, 128), I32)
        for i, value in enumerate(entries):
            tile = jnp.where(trow == i, value, tile)
        return tile

    tables[0] = as_rows([take[0], take[1]] + [codes[a][s] for a in range(2) for s in range(2)])
    links = as_rows(
        [ds[a, s] for a in range(2) for s in range(2)]
        + [eb[0, s, c] for s in range(2) for c in range(2)]
    ).astype(F32)

    def y_faces(field):
        low = [field[a, :, :, 0:128] for a in range(2)]
        high = [pltpu.roll(field[a, :, :, LAST:LANES], 32, 2) for a in range(2)]
        return low, high

    def pair_for(faces, is_minus):
        low, high = faces
        cols = []
        for c in range(2):
            from_low = jnp.where(eb[0, 0, c] == 1, low[1], low[0])
            from_high = jnp.where(eb[0, 1, c] == 1, high[1], high[0])
            cols.append(jnp.where(is_minus, from_low, from_high))
        return jnp.where(lane3 < 32, cols[0], pltpu.roll(cols[1], 32, 2))

    def x_face(field, side, a):
        if side == 0:
            return field[a, 0, 0:1, :]
        return field[a, CHUNKS - 1, SUB - 1 : SUB, :]

    def fill(first, second, block):
        for side in range(2):
            for a in range(2):
                n = 4 * block + a
                xs[side, n : n + 1, :] = x_face(first, side, a)
                xs[side, n + 2 : n + 3, :] = x_face(second, side, a)
        one, two = y_faces(first), y_faces(second)
        for peer in range(2):
            ys[peer, CHUNKS * block : CHUNKS * block + CHUNKS] = jnp.where(
                lane3 < 64, pair_for(one, minus[peer]), pltpu.roll(pair_for(two, minus[peer]), 64, 2)
            )

    loads[0].wait()
    loads[1].wait()
    fill(u0, perm, 0)
    for peer in range(2):
        ys[peer, 2 * CHUNKS] = links
    for side in range(2):
        for f, field in enumerate((u0, perm)):
            lines = []
            for a in range(2):
                face = x_face(field, side, a)
                lines.append([face[:, 0:128], pltpu.roll(face[:, LAST:LANES], 32, 1)])
            by_column = [
                jnp.where(eb[0, s, c] == 1, lines[1][s], lines[0][s]) for s in range(2) for c in range(2)
            ]
            by_slot = [lines[a][s] for a in range(2) for s in range(2)]
            for n, listed in enumerate((by_column, by_slot)):
                packed = listed[0]
                for q in range(1, 4):
                    packed = jnp.where(quarter1 == q, pltpu.roll(listed[q], 32 * q, 1), packed)
                edge_out[side, 2 * n + f : 2 * n + f + 1, :] = packed
    def zslot(a, direction):
        return jnp.maximum(snt[a, 2 + direction], 0)

    def beside(field, a, k):
        u = field[a, k]
        before = field[a, jnp.maximum(k - 1, 0), SUB - 1 : SUB, :]
        after = field[a, jnp.minimum(k + 1, CHUNKS - 1), 0:1, :]
        um = jnp.where(row == 0, before, pltpu.roll(u, 1, 0))
        up = jnp.where(row == SUB - 1, after, pltpu.roll(u, SUB - 1, 0))
        ym = pltpu.roll(u, 32, 1)
        yp = pltpu.roll(u, LANES - 32, 1)
        nm = field[zslot(a, 0), k]
        np_ = field[zslot(a, 1), k]
        zm = jnp.where(zpos == 0, pltpu.roll(nm, LANES - 31, 1), pltpu.roll(u, 1, 1))
        zp = jnp.where(zpos == 31, pltpu.roll(np_, 31, 1), pltpu.roll(u, LANES - 1, 1))
        return u, (um, up, ym, yp, zm, zp)

    def weights(k, _):
        for a in range(2):
            kk, nbs = beside(perm, a, k)
            has_zm = snt[a, 2] >= 0
            has_zp = snt[a, 3] >= 0
            keep = (
                jnp.logical_not((row == 0) & (k == 0)),
                jnp.logical_not((row == SUB - 1) & (k == CHUNKS - 1)),
                lane >= 32,
                lane < LANES - 32,
                jnp.logical_or(zpos != 0, has_zm),
                jnp.logical_or(zpos != 31, has_zp),
            )
            total = jnp.full((SUB, LANES), brink[a], F32)
            for store, nb, mask in zip((wxm, wxp, wym, wyp, wzm, wzp), nbs, keep):
                w = jnp.where(mask, harmonic(kk, nb), 0.0)
                store[a, k] = w
                total = total + w
            dg[a, k] = total
        return 0

    lax.fori_loop(0, CHUNKS, weights, 0)
    loads[2].wait()

    def neighbour_sum(field, into, first=0, stride=1, count=CHUNKS):
        def step(n, _):
            k = first + stride * n
            for a in range(2):
                _, nbs = beside(field, a, k)
                total = src[a, k]
                for store, nb in zip((wxm, wxp, wym, wyp, wzm, wzp), nbs):
                    total = total + store[a, k] * nb
                into[a, k] = total
            return 0

        lax.fori_loop(0, count, step, 0)

    outer_tiles = ((0, 0), (LANES - 256, 128))

    def edge_sum(field, into):
        def step(n, _):
            k = 1 + n
            for a in range(2):
                for start, kept in outer_tiles:
                    part = slice(start, start + 256)
                    u = field[a, k, :, part]
                    nm = field[zslot(a, 0), k, :, part]
                    np_ = field[zslot(a, 1), k, :, part]
                    before = field[a, k - 1, SUB - 1 : SUB, part]
                    after = field[a, k + 1, 0:1, part]
                    nbs = (
                        jnp.where(row[:, 0:256] == 0, before, pltpu.roll(u, 1, 0)),
                        jnp.where(row[:, 0:256] == SUB - 1, after, pltpu.roll(u, SUB - 1, 0)),
                        pltpu.roll(u, 32, 1),
                        pltpu.roll(u, 224, 1),
                        jnp.where(zpos[:, 0:256] == 0, pltpu.roll(nm, 225, 1), pltpu.roll(u, 1, 1)),
                        jnp.where(zpos[:, 0:256] == 31, pltpu.roll(np_, 31, 1), pltpu.roll(u, 255, 1)),
                    )
                    total = src[a, k, :, part]
                    for store, nb in zip((wxm, wxp, wym, wyp, wzm, wzp), nbs):
                        total = total + store[a, k, :, part] * nb
                    into[a, k, :, start + kept : start + kept + 128] = total[:, kept : kept + 128]
            return 0

        lax.fori_loop(0, CHUNKS - 2, step, 0)

    neighbour_sum(u0, g)
    fill(g, dg, 1)

    prow = lax.broadcasted_iota(I32, (512, 128), 0)
    pcol = lax.broadcasted_iota(I32, (512, 128), 1)
    pool[...] = 0.125 * ((prow // 64) * 16 + (prow % 32) // 2 == pcol).astype(F32)
    frow = lax.broadcasted_iota(I32, (128, 128), 0)
    fcol = lax.broadcasted_iota(I32, (128, 128), 1)
    pool_face[...] = 0.125 * (frow // 32 * 16 + (frow % 32) // 2 == fcol).astype(F32)

    def pooled_residual(field, sums):
        def step(k, _):
            for a in range(2):
                at_row = pl.multiple_of(a * 32 + k * SUB, SUB)
                r = sums[a, k] - dg[a, k] * field[a, k]
                for t in range(8):
                    res[t, pl.ds(at_row, SUB), :] = r[:, 128 * t : 128 * t + 128]
            return 0

        lax.fori_loop(0, CHUNKS, step, 0)
        paired = [
            res[t, pl.ds(0, 32, stride=2), :] + res[t, pl.ds(1, 32, stride=2), :] for t in range(8)
        ]
        stacked = [jnp.concatenate(paired[4 * h : 4 * h + 4], axis=1) for h in range(2)]
        return jnp.dot(
            jnp.concatenate(stacked, axis=0), pool[...],
            preferred_element_type=F32, precision=lax.Precision.HIGHEST,
        )

    def piece_of(pooled, a, t):
        return pooled[32 * t + 16 * a : 32 * t + 16 * a + 16, :]

    def inner_first(k, _):
        for a in range(2):
            i = OMEGA / dg[a, k]
            inv[a, k] = i
            u1[a, k] = (1.0 - OMEGA) * u0[a, k] + i * g[a, k]
        return 0

    def inner_second(k, _):
        for a in range(2):
            u2[a, k] = (1.0 - OMEGA) * u1[a, k] + inv[a, k] * ga[a, k]
        return 0

    def inner_pieces():
        lax.fori_loop(0, CHUNKS, inner_first, 0)
        neighbour_sum(u1, ga)
        lax.fori_loop(0, CHUNKS, inner_second, 0)
        neighbour_sum(u2, ga)
        pooled = pooled_residual(u2, ga)
        for a in range(2):
            for t in range(2):
                n = 4 * a + 2 * t
                bulk[my_y, n : n + 2] = piece_of(pooled, a, t).reshape(2, SUB, 128)
        sides = jnp.where(quarter1 % 2 == 0, minus[0].astype(F32), minus[1].astype(F32))
        bulk[my_y, 8] = jnp.broadcast_to(sides, (SUB, 128))

    pl.when(zh == 0)(inner_pieces)
    pl.semaphore_wait(barrier, greeted)
    sent = []
    for peer in range(2):
        sent.append(remote(ys.at[peer], yr.at[1 - peer], hs_sem.at[peer], hr_sem.at[peer], i_peers[peer]))
    for side in range(2):
        for peer in range(2):
            n = 4 + 2 * side + peer
            sent.append(
                Link(
                    edge_out.at[side], edge_in.at[1 - side, 1 - peer],
                    hs_sem.at[n], hr_sem.at[n], corners[side][peer], side,
                )
            )
    for side in range(2):
        n = 2 + side
        sent.append(
            Link(xs.at[side], xr.at[1 - side], hs_sem.at[n], hr_sem.at[n], d_peers[side], side)
        )
        sent.append(
            Link(
                tables.at[0], tables.at[2 - side], ts_sem.at[side], tr_sem.at[side], d_peers[side], side
            )
        )
    wants = [
        remote(tables.at[0], tables.at[3 + j], ts_sem.at[2 + j], tr_sem.at[2 + j], device)
        for j, device in enumerate(row_peers)
    ]
    pl.when(zh == 1)(inner_pieces)
    early = [
        remote(bulk.at[my_y], bulk.at[my_y], bs_sem.at[o], br_sem.at[o], device)
        for o, device in enumerate(y_peers)
    ]

    def pick(choice, options):
        found = jnp.zeros_like(options[0])
        for i, option in enumerate(options):
            found = jnp.where(choice == i, option, found)
        return found

    for side in range(2):

        @pl.when(jnp.logical_not(has[side]))
        def _():
            xr[side] = jnp.ones((8, LANES), F32)
            x_in[side] = jnp.zeros((n_y, 2, 2, 128), F32)
            tables[1 + side] = jnp.full((SUB, 128), -1, I32)
            for peer in range(2):
                edge_in[side, peer] = jnp.zeros((4, 128), F32)

    for copy in sent:
        copy.wait_recv()

    px, kx, gx, dx = (
        [[xr[s, n + j : n + j + 1, :] for j in range(2)] for s in range(2)] for n in (0, 2, 4, 6)
    )

    def both(block):
        low, high = [yr[peer, CHUNKS * block : CHUNKS * block + CHUNKS] for peer in range(2)]
        return (
            jnp.where(lane3 < 64, low, pltpu.roll(high, 64, 2)),
            jnp.where(lane3 < 64, pltpu.roll(low, 64, 2), high),
        )

    py, ky = both(0)
    gy, dy = both(1)

    def rotated(quarters):
        return [quarters] + [pltpu.roll(quarters, 128 - 32 * q, 2) for q in range(1, 4)]

    def own_faces(field):
        low, high = y_faces(field)
        return [[low[a], high[a]] for a in range(2)]

    def into_quarters(faces, keys):
        total = jnp.zeros((CHUNKS, SUB, 128), F32)
        for a in range(2):
            for direction in range(2):
                face = jnp.where(lane3 < 32, faces[a][direction], 0.0)
                face = face + pltpu.roll(face, 32, 2)
                face = face + pltpu.roll(face, 64, 2)
                total = total + jnp.where(quarter3 == keys[a][direction], face, 0.0)
        return total

    k_faces, u_faces = own_faces(perm), own_faces(u0)
    k_turned, u_turned = rotated(ky), rotated(py)

    def add_y(ref, a, direction, value):
        if direction == 0:
            ref[a, :, :, 0:128] += value
        else:
            ref[a, :, :, LAST:LANES] += pltpu.roll(value, 96, 2)

    def add_x(ref, a, side, value):
        if side == 0:
            ref[a, 0, 0:1, :] += value
        else:
            ref[a, CHUNKS - 1, SUB - 1 : SUB, :] += value

    for a in range(2):
        for side in range(2):
            w = harmonic(x_face(perm, side, a), pick(ds[a, side], kx[side]))
            wxe[side, a : a + 1, :] = w
            add_x(dg, a, side, w)
            add_x(g, a, side, w * pick(ds[a, side], px[side]))
        for direction in range(2):
            kg = pick(codes[a][direction], k_turned)
            w = jnp.where(lane3 < 32, harmonic(k_faces[a][direction], kg), 0.0)
            wye[a, direction] = w
            add_y(dg, a, direction, w)
            add_y(g, a, direction, w * pick(codes[a][direction], u_turned))

    def line(packed, start, target):
        return pltpu.roll(packed, (target - start) % 4 * 32, 1) if start != target else packed

    px1 = []
    for side in range(2):
        found = []
        for j in range(2):
            gsum, dsum = gx[side][j], dx[side][j]
            mine_p = jnp.zeros((1, LANES), F32)
            mine_k = jnp.zeros((1, LANES), F32)
            for a in range(2):
                linked = ds[a, side] == j
                mine_p = jnp.where(linked, x_face(u0, side, a), mine_p)
                mine_k = jnp.where(linked, x_face(perm, side, a), mine_k)
            w = harmonic(kx[side][j], mine_k)
            gsum = gsum + w * mine_p
            dsum = dsum + w
            ends = []
            for direction in range(2):
                code = tables[1 + side, 2 + 2 * j + direction : 3 + 2 * j + direction, :]
                start = 2 if direction == 0 else 0
                target = 0 if direction == 0 else 3
                values = []
                for f in range(2):
                    options = [
                        line(edge_in[side, peer, f : f + 1, :], start + c, target)
                        for peer in range(2)
                        for c in range(2)
                    ]
                    values.append(pick(code, options))
                kk = kx[side][j][:, 0:128] if direction == 0 else kx[side][j][:, LAST:LANES]
                w = jnp.where(quarter1 == target, harmonic(kk, values[1]), 0.0)
                ends.append((w, w * values[0]))
            gap = jnp.zeros((1, LANES - 256), F32)
            dsum = dsum + jnp.concatenate([ends[0][0], gap, ends[1][0]], axis=1)
            gsum = gsum + jnp.concatenate([ends[0][1], gap, ends[1][1]], axis=1)
            found.append((1.0 - OMEGA) * px[side][j] + OMEGA * gsum / dsum)
        px1.append(found)

    mine_k = into_quarters(k_faces, codes)
    w = harmonic(ky, mine_k)
    gy = gy + w * into_quarters(u_faces, codes)
    dy = dy + w
    slots = []
    for peer in range(2):
        held = yr[peer, 2 * CHUNKS]
        for c in range(2):
            slots.append(jnp.where(minus[peer], held[6 + c : 7 + c, :], held[4 + c : 5 + c, :]))
    rows3 = lax.broadcasted_iota(I32, (CHUNKS, SUB, 128), 0) * SUB + lax.broadcasted_iota(
        I32, (CHUNKS, SUB, 128), 1
    )
    for side in range(2):
        values = []
        for f in range(2):
            total = jnp.zeros((1, 128), F32)
            for q in range(4):
                peer = q // 2
                held = yr[peer, 2 * CHUNKS]
                link = jnp.where(
                    slots[q] == 1, held[2 + side : 3 + side, :], held[side : side + 1, :]
                )
                edge = edge_in[side, peer, 2 + f : 3 + f, :]
                options = [
                    jnp.where(minus[peer], line(edge, 2 * s + 1, q), line(edge, 2 * s, q))
                    for s in range(2)
                ]
                total = jnp.where(quarter1 == q, pick(link, options), total)
            values.append(total)
        r = 0 if side == 0 else CHUNKS * SUB - 1
        here = ky[0, 0:1, :] if side == 0 else ky[CHUNKS - 1, SUB - 1 : SUB, :]
        w = harmonic(here, values[1])
        dy = dy + jnp.where(rows3 == r, w.reshape(1, 1, 128), 0.0)
        gy = gy + jnp.where(rows3 == r, (w * values[0]).reshape(1, 1, 128), 0.0)
    py1 = (1.0 - OMEGA) * py + OMEGA * gy / dy

    whole = slice(0, LANES)
    parts = [(k, whole) for k in (0, CHUNKS - 1)]
    parts += [(k, part) for k in range(1, CHUNKS - 1) for part in (slice(0, 128), slice(LAST, LANES))]
    for k, part in parts:
        for a in range(2):
            i = OMEGA / dg[a, k, :, part]
            inv[a, k, :, part] = i
            u1[a, k, :, part] = (1.0 - OMEGA) * u0[a, k, :, part] + i * g[a, k, :, part]

    u_turned = rotated(py1)
    y_flow = [
        [wye[a, direction] * pick(codes[a][direction], u_turned) for direction in range(2)]
        for a in range(2)
    ]
    x_flow = [[wxe[side, a : a + 1, :] * pick(ds[a, side], px1[side]) for side in range(2)] for a in range(2)]

    def second_update(chosen):
        for k, part in chosen:
            for a in range(2):
                if part.start == 0:
                    g[a, k, :, 0:128] += y_flow[a][0][k]
                if part.stop == LANES:
                    g[a, k, :, LAST:LANES] += pltpu.roll(y_flow[a][1][k], 96, 1)
                u2[a, k, :, part] = (1.0 - OMEGA) * u1[a, k, :, part] + inv[a, k, :, part] * g[a, k, :, part]

    neighbour_sum(u1, g, 0, CHUNKS - 1, 2)
    for a in range(2):
        for side in range(2):
            add_x(g, a, side, x_flow[a][side])
    second_update(parts[0:2])
    across = []
    for side in range(2):
        flows = [wxe[side, a : a + 1, :] * x_face(u2, side, a) for a in range(2)]
        for s in range(2):
            total = jnp.zeros((1, LANES), F32)
            for a in range(2):
                total = total + jnp.where(ds[a, side] == s, flows[a], 0.0)
            across.append(total)
    across = jnp.concatenate(across, axis=0)
    crossing = jnp.dot(
        jnp.concatenate([across[:, 0:512], across[:, 512:1024]], axis=0), pool[...],
        preferred_element_type=F32, precision=lax.Precision.HIGHEST,
    )
    for side in range(2):
        for t in range(2):
            x_out[side, t] = crossing[4 * t + 2 * side : 4 * t + 2 * side + 2, :]
    spread = []
    for side in range(2):
        for o, device in enumerate(x_peers[side]):
            n = side * n_y + o
            spread.append(
                Link(x_out.at[side], x_in.at[1 - side, my_y], xs_sem.at[n], xr_sem.at[n], device, side)
            )
    edge_sum(u1, g)
    second_update(parts[2:])
    store = pltpu.make_async_copy(u2, out_hbm, out_sem.at[0])
    store.start()
    neighbour_sum(u2, g, 0, CHUNKS - 1, 2)
    edge_sum(u2, g)

    pooled = pooled_residual(u2, g)
    lane2 = lax.broadcasted_iota(I32, (16, 128), 1)
    edges = jnp.zeros((16, 128), F32)
    for a in range(2):
        for t in range(2):
            part = piece_of(pooled, a, t)
            late[my_y, a, 4 * t : 4 * t + 2, :] = part[0:2, :]
            late[my_y, a, 4 * t + 2 : 4 * t + 4, :] = part[14:16, :]
            part = part if a == t else pltpu.roll(part, 64, 1)
            edges = jnp.where(lane2 // 32 == 2 * a + t, part, edges)
    late[my_y, 2:4] = edges.reshape(2, SUB, 128)
    u_faces = own_faces(u2)
    for direction in range(2):
        total = jnp.zeros((CHUNKS, SUB, 128), F32)
        for a in range(2):
            face = wye[a, direction] * u_faces[a][direction]
            face = face + pltpu.roll(face, 32, 2)
            face = face + pltpu.roll(face, 64, 2)
            code = codes[a][direction]
            slot = pick(code, slots)
            key = jnp.where(code >= 2, 2.0, 0.0) + slot
            hit = (quarter1.astype(F32) == key) & (code >= 0)
            total = total + jnp.where(hit.reshape(1, 1, 128), face, 0.0)
        face_sum[direction] = total.reshape(CHUNKS * SUB, 128)
    halves = [
        face_sum[direction, pl.ds(first, 16, stride=2), :] for direction in range(2) for first in range(2)
    ]
    faces = jnp.dot(
        halves[0] + halves[1] + halves[2] + halves[3], pool_face[...],
        preferred_element_type=F32, precision=lax.Precision.HIGHEST,
    )
    late[my_y, 4] = jnp.where(lane2[0:8] < 64, faces[0:8], pltpu.roll(faces[8:16], 64, 1))

    spread += [
        remote(late.at[my_y], late.at[my_y], gs_sem.at[o], gr_sem.at[o], device)
        for o, device in enumerate(y_peers)
    ]
    for copy in wants + early:
        copy.wait_recv()

    def device_at(y):
        return (y * 2 + zh) * 2 + core

    def iota(shape, dim):
        return lax.broadcasted_iota(I32, shape, dim)

    bulk_shape = (n_y, 2, 4, SUB, 128)
    bulk_id = device_at(iota(bulk_shape, 0)) * 2 + iota(bulk_shape, 1)

    def want(holder, j):
        return tables[holder, j : j + 1, :]

    holders = (0, 3, 4, 5)
    for h, holder in ((2, 3), (3, 5), (1, 4), (0, 0)):
        held = bulk[:, 0:8].reshape(bulk_shape)
        for j in range(2):
            w = want(holder, j).reshape(1, 1, 1, 1, 128)
            bulk_out[h, 4 * j : 4 * j + 4] = jnp.sum(jnp.where(bulk_id == w, held, 0.0), axis=(0, 1))
        if h == 3:
            to_core = remote(
                bulk_out.at[pl.ds(2, 2)], bulk_in.at[pl.ds(0, 2)], es_sem.at[0], er_sem.at[0], row_peers[0]
            )
    to_core.wait_recv()
    bulk_out[1] += bulk_in[1]
    rows_of_bulk = [
        to_core, remote(bulk_out.at[1], bulk_in.at[2], es_sem.at[1], er_sem.at[1], row_peers[1])
    ]

    for copy in spread:
        copy.wait_recv()

    a_shape = (n_y, 2, SUB, 128)
    a_id = device_at(iota(a_shape, 0)) * 2 + iota(a_shape, 1)
    b_id = device_at(iota(a_shape, 0)) * 2 + iota(a_shape, 3) // 64
    x_shape = (n_y, 2, 128)
    x_id = device_at(iota(x_shape, 0)) * 2 + iota(x_shape, 1)
    y_shape = (n_y, SUB, 128)
    y_lane = iota(y_shape, 2)
    y_id = (device_at(iota(y_shape, 0)) + 2 * (y_lane // 32 % 2) - 1) * 2 + y_lane // 16 % 2
    row8 = iota((SUB, 128), 0)
    lane8 = iota((SUB, 128), 1)

    def shell(holder, j):
        w2 = want(holder, j)
        w3, w4 = w2.reshape(1, 1, 128), w2.reshape(1, 1, 1, 128)
        rows = jnp.sum(jnp.where(a_id == w4, late[:, 0:2], 0.0), axis=(0, 1))
        edges = jnp.sum(jnp.where(b_id == w4, late[:, 2:4], 0.0), axis=0)
        halves = [edges[n] + pltpu.roll(edges[n], 64, 1) for n in range(2)]
        for side in range(2):
            line = [
                jnp.sum(jnp.where(x_id == w3, x_in[side, :, t], 0.0), axis=(0, 1)).reshape(1, 128)
                for t in range(2)
            ]
            for t in range(2):
                rows = rows + jnp.where(row8 == 4 * t + 3 * side, line[t], 0.0)
            both_ends = jnp.where(lane8 < 32, line[0], pltpu.roll(line[1], 64, 1))
            halves[side] = halves[side] + jnp.where(row8 == 7 * side, both_ends, 0.0)
        found = jnp.where(y_id == w3, late[:, 4], 0.0)
        for f in range(2):
            part = jnp.sum(jnp.where(bulk[:, 8] == f, found, 0.0), axis=0)
            part = part + pltpu.roll(part, 112, 1)
            part = part + pltpu.roll(part, 96, 1)
            spot = lane8 // 16 == 3 * f
            for n in range(2):
                turn = (48 * f + 64 * n) % 128
                moved = pltpu.roll(part, turn, 1) if turn else part
                halves[n] = halves[n] + jnp.where(spot, moved, 0.0)
        return rows, halves

    rows_of_shells = []
    for h in (3, 2, 1, 0):
        one, two = shell(holders[h], 0), shell(holders[h], 1)
        shell_out[h, 0] = one[0]
        shell_out[h, 1] = two[0]
        for n in range(2):
            shell_out[h, 2 + n] = jnp.where(lane8 < 64, one[1][n], pltpu.roll(two[1][n], 64, 1))
        if h:
            rows_of_shells.append(
                remote(
                    shell_out.at[h], shell_in.at[h - 1], es_sem.at[2 + h], er_sem.at[2 + h],
                    row_peers[h - 1],
                )
            )
    rows_of_bulk[1].wait_recv()
    inner = bulk_out[0] + bulk_in[0] + bulk_in[2]
    for copy in rows_of_shells:
        copy.wait_recv()
    outer = shell_out[0] + shell_in[0] + shell_in[1] + shell_in[2]
    for j in range(2):
        rows = outer[j]
        turned = pltpu.roll(rows, 4, 0)
        for n in range(2):
            edges = outer[2 + n] if j == 0 else pltpu.roll(outer[2 + n], 64, 1)
            for t in range(2):
                line = rows if t == n else turned
                found = jnp.where(row8 < 2 if n == 0 else row8 >= 6, line, inner[4 * j + 2 * t + n])
                if t == 0:
                    found = jnp.where(lane8 < 32, edges, found)
                else:
                    found = jnp.where(lane8 >= 96, pltpu.roll(edges, 64, 1), found)
                coarse[j, SUB * n : SUB * n + SUB, 128 * t : 128 * t + 128] = found
    last = pltpu.make_async_copy(coarse, coarse_hbm, out_sem.at[1])
    last.start()
    for copy in sent + wants + early + spread + rows_of_bulk + rows_of_shells:
        copy.wait_send()
    store.wait()
    last.wait()


def body(pressure, source, perm, brinkman, depth_source, sideways, edge_blocks, restrict_take):
    big = (2, CHUNKS, SUB, LANES)
    n_y = lax.axis_size("inslab") // 4
    vm = lambda *shape: pltpu.VMEM(shape, F32)
    dma = lambda n: pltpu.SemaphoreType.DMA((n,))
    anywhere = pl.BlockSpec(memory_space=pltpu.HBM)
    arrays = [x.reshape(big) for x in (pressure, source, perm)]
    arrays += [brinkman, depth_source, sideways, edge_blocks, restrict_take]
    smoothed, coarse = pl.pallas_call(
        kernel,
        out_shape=(
            jax.ShapeDtypeStruct(big, F32),
            jax.ShapeDtypeStruct((2, 16, 256), F32),
        ),
        in_specs=[anywhere] * 8,
        out_specs=(anywhere, anywhere),
        scratch_shapes=[
            pltpu.SMEM((2,), F32), pltpu.SMEM((2, 2), I32), pltpu.SMEM((2, 4), I32),
            pltpu.SMEM((1, 2, 2), I32), pltpu.SMEM((2,), I32),
        ]
        + [vm(*big) for _ in range(15)]
        + [
            vm(2, 2, LANES), vm(2, 2, CHUNKS, SUB, 128), vm(8, 64, 128), vm(512, 128), vm(128, 128),
            vm(2, 8, LANES), vm(2, 8, LANES),
            vm(2, 2 * CHUNKS + 1, SUB, 128), vm(2, 2 * CHUNKS + 1, SUB, 128),
            vm(2, 4, 128), vm(2, 2, 4, 128),
            pltpu.VMEM((6, SUB, 128), I32),
            vm(2, CHUNKS * SUB, 128),
            vm(n_y, 9, SUB, 128), vm(n_y, 5, SUB, 128), vm(2, 2, 2, 128), vm(2, n_y, 2, 2, 128),
            vm(4, 8, SUB, 128), vm(3, 8, SUB, 128), vm(4, 4, SUB, 128), vm(3, 4, SUB, 128), vm(2, 16, 256),
            dma(8), dma(2), dma(8), dma(8), dma(5), dma(5), dma(n_y - 1), dma(n_y - 1),
            dma(n_y - 1), dma(n_y - 1), dma(2 * n_y), dma(2 * n_y), dma(6), dma(6),
        ],
        compiler_params=pltpu.CompilerParams(
            collective_id=0, has_side_effects=True, vmem_limit_bytes=32 * 1024 * 1024
        ),
    )(*[pltpu.with_memory_space_constraint(x, pltpu.HBM) for x in arrays])
    return smoothed.reshape(pressure.shape), coarse


def solution(mesh):
    group = ("depth", "inslab")
    return jax.shard_map(
        body,
        mesh=mesh,
        in_specs=(
            P(group, None, None),
            P(group, None, None),
            P(group, None, None),
            P(group),
            P(group, None),
            P(group, None),
            P(group, None, None),
            P(group),
        ),
        out_specs=(P(group, None, None), P(group, None, None)),
        check_vma=False,
    )
```
